256 devices in a mesh: row: 16 (over z, core), col: 16 (over x, y).
Axes of the slice: x: 4, y: 4, z: 8, core: 2. Of those that a mesh axis runs over, the one named last changes fastest.
Arguments:
- observed: float32 [2, 4096, 4096], P(None, 'row', 'col'), may hold values from -6 to 6
- coherence_class: int32 [4096, 4096], P('row', 'col'), may hold values from 0 to 7
- class_weight: float32 [8], replicated, may hold values from 0.0002 to 0.003
- class_stiffness: float32 [8], replicated, may hold values from 0.5 to 4
Outputs:
- solution: float32 [2, 4096, 4096], P(None, 'row', 'col')
The draws below stay inside these ranges and needn't reach their ends.
All inputs are finite; a program needn't handle non-finite values.
Results may differ from the reference program's by a relative error of at most 0.0003.
Values sent between devices are 32-bit elements; how exact they have to be, the bound alone decides.
No kernel may reach another device: no remote copies, remote signals or barrier semaphores. Data moves between devices by JAX's collectives and lax.ppermute only.
A program may use at most 320 MiB of HBM per device.

```python
import math
import jax
import jax.numpy as jnp
from jax import lax

FIELDS = 2
LEVELS = 5
CG_ITERS = 12
CLASSES = 8
NR = 4096
NC = 4096


def place_ends(values, stream_key, smallest, largest):
    place = [jax.random.randint(jax.random.fold_in(stream_key, axis), (), 0, length) for axis, length in enumerate(values.shape)]
    main_axis = values.shape.index(max(values.shape))
    next_to = place[:main_axis] + [(place[main_axis] + 1) % values.shape[main_axis]] + place[main_axis + 1:]
    return values.at[tuple(place)].set(smallest).at[tuple(next_to)].set(largest)


def shard_levels(rng, extent, pieces, low, largest):
    factor_of, own = 1.0, jax.random.fold_in(rng, 6)
    for axis_at, shards_of in pieces:
        draws = jnp.exp(jax.random.uniform(jax.random.fold_in(own, axis_at), (shards_of,), jnp.float32, low / len(pieces), largest / len(pieces)))
        factor_of = factor_of * jnp.repeat(draws, extent[axis_at] // shards_of).reshape([-1 if axis == axis_at else 1 for axis in range(len(extent))])
    return factor_of


def gaussian(rng, extent, spread, most, shards=(), held_as=jnp.bfloat16):
    drawn = spread * jax.random.normal(rng, extent, jnp.float32)
    if shards:
        drawn = drawn * shard_levels(rng, extent, shards, -0.22, 0.18)
    return jnp.clip(drawn, -most, most).astype(held_as)


def setup_inputs(seed: int = 0) -> dict:
    key_of = jax.random.split(jax.random.key(seed), 5)
    observed = gaussian(key_of[0], (FIELDS, NR, NC), 1.0, 6.0, ((1, 16), (2, 16)), jnp.float32)
    coherence_class = place_ends(jax.random.randint(key_of[1], (NR, NC), 0, CLASSES), jax.random.fold_in(key_of[1], 1), 0, CLASSES - 1).astype(jnp.int32)
    class_weight = jnp.clip(jnp.exp(jax.random.uniform(key_of[2], (CLASSES,), jnp.float32, math.log(0.0002), math.log(0.003))), 0.0002, 0.003)
    class_stiffness = jnp.clip(jnp.exp(jax.random.uniform(key_of[3], (CLASSES,), jnp.float32, math.log(0.5), math.log(4.0))), 0.5, 4.0)
    return {"observed": observed, "coherence_class": coherence_class, "class_weight": class_weight, "class_stiffness": class_stiffness}


def lookup(classes, table):
    result = jnp.zeros(classes.shape, jnp.float32)
    for entry in range(table.shape[0]):
        result = jnp.where(classes == entry, table[entry], result)
    return result


def edge_terms(padded):
    centre = padded[1:-1, 1:-1]

    def single(other):
        return jnp.where(other > 0.0, 0.5 * (centre + other), 0.0)

    return (single(padded[:-2, 1:-1]), single(padded[2:, 1:-1]), single(padded[1:-1, :-2]), single(padded[1:-1, 2:]))


def pad_field(field):
    return jnp.pad(field, ((0, 0), (1, 1), (1, 1)))


def pull(padded, edges):
    north, south, west, east = edges
    total = north * padded[:, :-2, 1:-1] + south * padded[:, 2:, 1:-1]
    return total + west * padded[:, 1:-1, :-2] + east * padded[:, 1:-1, 2:]


def colour_mask(rows, cols):
    first = lax.broadcasted_iota(jnp.int32, (rows, cols), 0)
    second = lax.broadcasted_iota(jnp.int32, (rows, cols), 1)
    return (first + second) % 2 == 0


def prepare(weight, stiff):
    edges = edge_terms(jnp.pad(stiff, 1))
    diag = weight + edges[0] + edges[1] + edges[2] + edges[3]
    return edges, diag


def relax(field, rhs, edges, diag, chosen):
    fresh = (rhs + pull(pad_field(field), edges)) / diag
    return jnp.where(chosen, fresh, field)


def coarsen(field):
    shape = field.shape
    parts = field.reshape(shape[:-2] + (shape[-2] // 2, 2, shape[-1] // 2, 2))
    return jnp.sum(parts, axis=(-3, -1))


def coarse_cg(rhs, edges, diag):
    solved = jnp.zeros_like(rhs)
    resid = rhs
    direction = rhs
    norm_now = jnp.sum(resid * resid, axis=(1, 2))
    for step in range(CG_ITERS):
        image = diag * direction - pull(pad_field(direction), edges)
        alpha = norm_now / jnp.sum(direction * image, axis=(1, 2))
        solved = solved + alpha[:, None, None] * direction
        resid = resid - alpha[:, None, None] * image
        norm_next = jnp.sum(resid * resid, axis=(1, 2))
        direction = resid + (norm_next / norm_now)[:, None, None] * direction
        norm_now = norm_next
    return solved


def reference(observed, coherence_class, class_weight, class_stiffness):
    weight = lookup(coherence_class, class_weight)
    stiff = lookup(coherence_class, class_stiffness)
    rhs = observed
    saved = []
    for level in range(LEVELS):
        edges, diag = prepare(weight, stiff)
        red = colour_mask(weight.shape[0], weight.shape[1])
        field = relax(jnp.zeros_like(rhs), rhs, edges, diag, red)
        field = relax(field, rhs, edges, diag, jnp.logical_not(red))
        resid = rhs - (diag * field - pull(pad_field(field), edges))
        saved.append((field, rhs, weight, stiff))
        rhs = coarsen(resid)
        weight = coarsen(weight)
        stiff = 0.5 * coarsen(stiff)
    edges, diag = prepare(weight, stiff)
    correction = coarse_cg(rhs, edges, diag)
    for level in range(LEVELS - 1, -1, -1):
        field, rhs, weight, stiff = saved[level]
        edges, diag = prepare(weight, stiff)
        red = colour_mask(weight.shape[0], weight.shape[1])
        field = field + jnp.repeat(jnp.repeat(correction, 2, axis=1), 2, axis=2)
        field = relax(field, rhs, edges, diag, red)
        correction = relax(field, rhs, edges, diag, jnp.logical_not(red))
    return correction
```

```python
import jax
import jax.numpy as jnp
from jax import lax
from jax.experimental import pallas as pl
from jax.experimental.pallas import tpu as pltpu
from jax.sharding import PartitionSpec as P

LEVELS = 5
CG_ITERS = 12
FAR = -1.0e4


def roll(x, shift, axis):
    return pltpu.roll(x, shift % x.shape[axis], axis)


def lane_bit(shape, level):
    lane = lax.broadcasted_iota(jnp.int32, shape, len(shape) - 1)
    return (lane >> level) % 2 == 0


def ends(ref, index, count):
    ref[index + (0,)] = roll(ref[index + (count,)], 1, 0)
    ref[index + (count + 1,)] = roll(ref[index + (1,)], -1, 0)


def loop(count, body, unroll):
    if count <= unroll:
        for i in range(count):
            body(i)
        return

    def step(i, carry):
        for j in range(unroll):
            body(i * unroll + j)
        return carry

    lax.fori_loop(0, count // unroll, step, 0)


def edges_at(a, level, gr, gb, even):
    step = 1 << level
    r, b = gr[a + 1], gb[a + 1]
    same = jnp.maximum(r + b, 0.0)
    red_other = jnp.maximum(r + jnp.where(even, gb[a], gb[a + 2]), 0.0)
    red_east = jnp.maximum(r + roll(b, -step, 1), 0.0)
    red_west = jnp.maximum(r + roll(b, step, 1), 0.0)
    black_other = jnp.maximum(b + jnp.where(even, gr[a + 2], gr[a]), 0.0)
    black_east = jnp.maximum(b + roll(r, -step, 1), 0.0)
    black_west = jnp.maximum(b + roll(r, step, 1), 0.0)
    return same, red_other, red_east, red_west, black_other, black_east, black_west


def make_edges(level, count, gr, gb, wr, wb, ke, inv, width, unroll):
    even = lane_bit((8, width), level)

    def body(a):
        k = edges_at(a, level, gr, gb, even)
        for i in range(7):
            ke[i, a] = k[i]
        inv[0, a] = 1.0 / jnp.maximum(wr[a] + k[0] + k[1] + k[2] + k[3], 1e-20)
        inv[1, a] = 1.0 / jnp.maximum(wb[a] + k[0] + k[4] + k[5] + k[6], 1e-20)

    loop(count, body, unroll)


def pull_red(a, level, f, black, ke, even):
    step = 1 << level
    b = black[f, a + 1]
    total = ke[0, a] * b + ke[1, a] * jnp.where(even, black[f, a], black[f, a + 2])
    return total + ke[2, a] * roll(b, -step, 1) + ke[3, a] * roll(b, step, 1)


def pull_black(a, level, f, red, ke, even):
    step = 1 << level
    r = red[f, a + 1]
    total = ke[0, a] * r + ke[4, a] * jnp.where(even, red[f, a + 2], red[f, a])
    return total + ke[5, a] * roll(r, -step, 1) + ke[6, a] * roll(r, step, 1)


def pair_sum(x, level, even):
    step = 1 << level
    return x + jnp.where(even, roll(x, -step, 1), roll(x, step, 1))


def lookup(table, index):
    parts = []
    for c in range(index.shape[1] // 128):
        parts.append(jnp.take_along_axis(table, index[:, c * 128 : (c + 1) * 128], axis=1))
    return jnp.concatenate(parts, axis=1)


def down_kernel(own, north, south, west, east, tables, *rest):
    rhs_s, blk_s, g_s, w_s = (rest[i * LEVELS : (i + 1) * LEVELS] for i in range(4))
    message = rest[4 * LEVELS]
    full, red, ke, inv, frame, arrived = rest[4 * LEVELS + 1 :]
    width = 512
    tab_g = jnp.broadcast_to(tables[0:1, :], (8, 128))
    tab_w = jnp.broadcast_to(tables[1:2, :], (8, 128))
    tiles = 64

    copies = []
    for source, at in ((north, 0), (own, 128), (south, 384)):
        for half in range(2):
            copies.append((source.at[:, :, pl.ds(half * 128, 128)], frame.at[:, 1 + half, pl.ds(at, source.shape[1]), :]))
    copies += [(west, frame.at[:, 0]), (east, frame.at[:, 3])]
    copies = [pltpu.make_async_copy(a, b, arrived.at[i]) for i, (a, b) in enumerate(copies)]
    for copy in copies:
        copy.start()
    for copy in copies:
        copy.wait()

    def frame_tile(f, a):
        return jnp.concatenate([frame[f, c, pl.ds(a, 8, stride=tiles), :] for c in range(4)], axis=1)

    for level in range(LEVELS):
        count = tiles // 2
        even = lane_bit((8, width), level)
        rhs, blk, g, w = rhs_s[level], blk_s[level], g_s[level], w_s[level]
        gr, gb = g.at[0], g.at[1]
        unroll = 2 if level == 0 else 4

        def pack(a, level=level, even=even, rhs=rhs, g=g, w=w):
            for f in range(2):
                if level == 0:
                    x, y = frame_tile(f, 2 * a), frame_tile(f, 2 * a + 1)
                else:
                    x, y = full[f, 2 * a], full[f, 2 * a + 1]
                rhs[f, a] = jnp.where(even, x, y)
                rhs[2 + f, a] = jnp.where(even, y, x)
            if level == 0:
                i, j = (frame_tile(2, 2 * a + k).astype(jnp.int32) for k in range(2))
                gx, gy, wx, wy = lookup(tab_g, i), lookup(tab_g, j), lookup(tab_w, i), lookup(tab_w, j)
            else:
                gx, gy, wx, wy = full[2, 2 * a], full[2, 2 * a + 1], full[3, 2 * a], full[3, 2 * a + 1]
            g[0, a + 1] = jnp.where(even, gx, gy)
            g[1, a + 1] = jnp.where(even, gy, gx)
            w[0, a] = jnp.where(even, wx, wy)
            w[1, a] = jnp.where(even, wy, wx)

        loop(count, pack, unroll)
        ends(g, (0,), count)
        ends(g, (1,), count)
        make_edges(level, count, gr, gb, w.at[0], w.at[1], ke, inv, width, unroll)

        def first_red(a, rhs=rhs):
            for f in range(2):
                red[f, a + 1] = rhs[f, a] * inv[0, a]

        loop(count, first_red, unroll)
        for f in range(2):
            ends(red, (f,), count)

        def first_black(a, level=level, even=even, rhs=rhs, blk=blk):
            for f in range(2):
                blk[f, a + 1] = (rhs[2 + f, a] + pull_black(a, level, f, red, ke, even)) * inv[1, a]

        loop(count, first_black, unroll)
        for f in range(2):
            ends(blk, (f,), count)

        def restrict(a, level=level, even=even, blk=blk, g=g, w=w):
            for f in range(2):
                full[f, a] = pair_sum(pull_red(a, level, f, blk, ke, even), level, even)
            full[2, a] = 0.5 * pair_sum(g[0, a + 1] + g[1, a + 1], level, even)
            full[3, a] = pair_sum(w[0, a] + w[1, a], level, even)

        loop(count, restrict, unroll)
        tiles = count

    lane = lax.broadcasted_iota(jnp.int32, (width, 128), 0)
    out = lax.broadcasted_iota(jnp.int32, (width, 128), 1)
    pick = jnp.where(lane == (4 + out % 8) * 32, 1.0, 0.0)
    place = lax.broadcasted_iota(jnp.int32, (8, 128), 1)
    sub = lax.broadcasted_iota(jnp.int32, (8, 128), 0)
    parts = [0.0, 0.0]
    for which in range(4):
        for a in range(2):
            spread = jnp.dot(full[which, a], pick, precision=lax.Precision.HIGHEST, preferred_element_type=jnp.float32)
            mine = (place // 8) == (which % 2) * 8 + (a + 2 * sub - 4)
            mine = jnp.logical_and(mine, jnp.logical_and(a + 2 * sub >= 4, a + 2 * sub < 12))
            parts[which // 2] += jnp.sum(jnp.where(mine, spread, 0.0), axis=0, keepdims=True)
    both = jnp.concatenate(parts * 4, axis=0)

    def send(i, carry):
        message[pl.ds(i * 8, 8), :] = both
        return carry

    lax.fori_loop(0, message.shape[0] // 8, send, 0)


def cg(gathered, kc, e, r, d, q):
    lane = lax.broadcasted_iota(jnp.int32, (8, 128), 1)
    sub = lax.broadcasted_iota(jnp.int32, (8, 128), 0)
    group = lane // 8
    arrays = [[None] * 16 for _ in range(4)]
    for hi in range(2):
        for pair in range(2):
            v = [gathered[pl.ds((hi * 128 + c) * 2 + pair, 8, stride=32), :] for c in range(16)]
            for k in (1, 2, 4, 8):
                low = (group // k) % 2 == 0
                for c in range(16):
                    if not c & k:
                        x, y = v[c], v[c | k]
                        v[c] = jnp.where(low, x, roll(y, 8 * k, 1))
                        v[c | k] = jnp.where(low, roll(x, -8 * k, 1), y)
            for i in range(16):
                arrays[2 * pair + i // 8][hi * 8 + i % 8] = v[i]

    def north(tile, t):
        if t % 8:
            return tile(t - 1)
        turned = roll(tile(t + 7), 1, 0)
        return turned if t == 0 else jnp.where(sub == 0, roll(tile(7), 1, 0), turned)

    def south(tile, t):
        if t % 8 != 7:
            return tile(t + 1)
        turned = roll(tile(t - 7), -1, 0)
        return turned if t == 15 else jnp.where(sub == 7, roll(tile(8), -1, 0), turned)

    g = arrays[2]
    for t in range(16):
        up = jnp.maximum(g[t] + north(lambda i: g[i], t), 0.0)
        down = jnp.maximum(g[t] + south(lambda i: g[i], t), 0.0)
        if t == 0:
            up = jnp.where(sub == 0, 0.0, up)
        if t == 15:
            down = jnp.where(sub == 7, 0.0, down)
        left = jnp.where(lane == 0, 0.0, jnp.maximum(g[t] + roll(g[t], 1, 1), 0.0))
        right = jnp.where(lane == 127, 0.0, jnp.maximum(g[t] + roll(g[t], -1, 1), 0.0))
        kc[0, t] = up
        kc[1, t] = down
        kc[2, t] = left
        kc[3, t] = right
        kc[4, t] = arrays[3][t] + up + down + left + right

    norm = []
    for f in range(2):
        total = 0.0
        for t in range(16):
            x = arrays[f][t]
            e[f, t] = jnp.zeros_like(x)
            r[f, t] = x
            d[f, t] = x
            total += x * x
        norm.append(jnp.sum(total, axis=(0, 1), keepdims=True))

    def iterate(_, norm):
        alpha = []
        for f in range(2):
            tile = lambda i, f=f: d[f, i]
            total = 0.0
            for t in range(16):
                x = d[f, t]
                image = kc[4, t] * x - (
                    kc[0, t] * north(tile, t)
                    + kc[1, t] * south(tile, t)
                    + kc[2, t] * roll(x, 1, 1)
                    + kc[3, t] * roll(x, -1, 1)
                )
                q[f, t] = image
                total += x * image
            alpha.append(norm[f] / jnp.sum(total, axis=(0, 1), keepdims=True))
        fresh = []
        for f in range(2):
            total = 0.0
            for t in range(16):
                e[f, t] = e[f, t] + alpha[f] * d[f, t]
                x = r[f, t] - alpha[f] * q[f, t]
                r[f, t] = x
                total += x * x
            fresh.append(jnp.sum(total, axis=(0, 1), keepdims=True))
        for f in range(2):
            beta = fresh[f] / norm[f]
            for t in range(16):
                d[f, t] = r[f, t] + beta * d[f, t]
        return tuple(fresh)

    lax.fori_loop(0, CG_ITERS, iterate, tuple(norm))


def up_kernel(place, gathered, *rest):
    rhs_s, blk_s, g_s, w_s = (rest[i * LEVELS : (i + 1) * LEVELS] for i in range(4))
    out = rest[4 * LEVELS]
    full, red, blk, ke, inv, kc, e, r, d, q, result, sent = rest[4 * LEVELS + 1 :]
    width = 512
    cg(gathered, kc, e, r, d, q)
    row0 = place[0] * 8 - 4
    col0 = place[1] * 8 - 4
    o = lax.broadcasted_iota(jnp.int32, (16, 128), 0)
    n = lax.broadcasted_iota(jnp.int32, (16, 128), 1)
    row = (n // 64) * 64 + (n % 8) * 8 + (n // 8) % 8
    rows = jnp.where(row == row0 + o // 8 + 2 * (o % 8), 1.0, 0.0)
    j = lax.broadcasted_iota(jnp.int32, (128, width), 0)
    lane = lax.broadcasted_iota(jnp.int32, (128, width), 1)
    cols = jnp.where(j == col0 + lane // 32, 1.0, 0.0)
    for f in range(2):
        whole = jnp.concatenate([e[f, t] for t in range(16)], axis=0)
        part = jnp.dot(rows, whole, precision=lax.Precision.HIGHEST, preferred_element_type=jnp.float32)
        part = jnp.dot(part, cols, precision=lax.Precision.HIGHEST, preferred_element_type=jnp.float32)
        full[f, 0] = part[0:8]
        full[f, 1] = part[8:16]

    for level in range(LEVELS - 1, -1, -1):
        count = 32 >> level
        even = lane_bit((8, width), level)
        rhs, old, g, w = rhs_s[level], blk_s[level], g_s[level], w_s[level]
        unroll = 2 if level == 0 else 4
        make_edges(level, count, g.at[0], g.at[1], w.at[0], w.at[1], ke, inv, width, unroll)

        def correct(a, old=old):
            for f in range(2):
                blk[f, a + 1] = old[f, a + 1] + full[f, a]

        loop(count, correct, unroll)
        for f in range(2):
            ends(blk, (f,), count)

        def second_red(a, level=level, even=even, rhs=rhs):
            for f in range(2):
                red[f, a + 1] = (rhs[f, a] + pull_red(a, level, f, blk, ke, even)) * inv[0, a]

        loop(count, second_red, unroll)
        for f in range(2):
            ends(red, (f,), count)

        def second_black(a, level=level, even=even, rhs=rhs):
            for f in range(2):
                x = red[f, a + 1]
                y = (rhs[2 + f, a] + pull_black(a, level, f, red, ke, even)) * inv[1, a]
                first, second = jnp.where(even, x, y), jnp.where(even, y, x)
                if level:
                    full[f, 2 * a] = first
                    full[f, 2 * a + 1] = second
                else:
                    for half in range(2):
                        lanes = slice(128 + 128 * half, 256 + 128 * half)
                        result[f, half, pl.ds(2 * a, 4, stride=64), :] = first[2:6, lanes]
                        result[f, half, pl.ds(2 * a + 1, 4, stride=64), :] = second[2:6, lanes]

        loop(count, second_black, unroll)

    copies = [pltpu.make_async_copy(result.at[:, i], out.at[:, :, pl.ds(i * 128, 128)], sent.at[i]) for i in range(2)]
    for copy in copies:
        copy.start()
    for copy in copies:
        copy.wait()


def level_shapes():
    shapes = []
    for build in (
        lambda n: (4, n, 8, 512),
        lambda n: (2, n + 2, 8, 512),
        lambda n: (2, n + 2, 8, 512),
        lambda n: (2, n, 8, 512),
    ):
        shapes += [build(32 >> level) for level in range(LEVELS)]
    return shapes


def send(x, axis, step):
    count = lax.axis_size(axis)
    return lax.ppermute(x, axis, [(i, i + step) for i in range(count) if 0 <= i + step < count])


def make_tables(class_weight, class_stiffness):
    pad = lambda x, first: jnp.pad(jnp.concatenate([jnp.full((1,), first, jnp.float32), x]), (0, 119))
    return jnp.stack([pad(0.5 * class_stiffness, FAR), pad(class_weight, 0.0)])


VMEM = pl.BlockSpec(memory_space=pltpu.VMEM)
ANY = pl.BlockSpec(memory_space=pl.ANY)
PARAMS = pltpu.CompilerParams(vmem_limit_bytes=56 * 1024 * 1024)


def down(own, north, south, west, east, tables):
    return pl.pallas_call(
        down_kernel,
        out_shape=[jax.ShapeDtypeStruct(s, jnp.float32) for s in level_shapes() + [(512, 128)]],
        in_specs=[ANY] * 5 + [VMEM],
        out_specs=[VMEM] * (4 * LEVELS + 1),
        scratch_shapes=[
            pltpu.VMEM((4, 32, 8, 512), jnp.float32),
            pltpu.VMEM((2, 34, 8, 512), jnp.float32),
            pltpu.VMEM((7, 32, 8, 512), jnp.float32),
            pltpu.VMEM((2, 32, 8, 512), jnp.float32),
            pltpu.VMEM((3, 4, 512, 128), jnp.float32),
            pltpu.SemaphoreType.DMA((8,)),
        ],
        compiler_params=PARAMS,
        name="down",
    )(own, north, south, west, east, tables)


def up(place, gathered, saved):
    grid = pltpu.VMEM((2, 16, 8, 128), jnp.float32)
    return pl.pallas_call(
        up_kernel,
        out_shape=jax.ShapeDtypeStruct((2, 256, 256), jnp.float32),
        in_specs=[pl.BlockSpec(memory_space=pltpu.SMEM)] + [VMEM] * (4 * LEVELS + 1),
        out_specs=ANY,
        scratch_shapes=[
            pltpu.VMEM((2, 32, 8, 512), jnp.float32),
            pltpu.VMEM((2, 34, 8, 512), jnp.float32),
            pltpu.VMEM((2, 34, 8, 512), jnp.float32),
            pltpu.VMEM((7, 32, 8, 512), jnp.float32),
            pltpu.VMEM((2, 32, 8, 512), jnp.float32),
            pltpu.VMEM((5, 16, 8, 128), jnp.float32),
            grid,
            grid,
            grid,
            grid,
            pltpu.VMEM((2, 2, 256, 128), jnp.float32),
            pltpu.SemaphoreType.DMA((2,)),
        ],
        compiler_params=PARAMS,
        name="up",
    )(place, gathered, *saved)


def local(observed, coherence_class, class_weight, class_stiffness):
    own = jnp.concatenate([observed, (coherence_class + 1).astype(jnp.float32)[None]], axis=0)
    north = send(own[:, 128:], "row", 1)
    south = send(own[:, :128], "row", -1)
    right = jnp.concatenate([north[:, :, 128:], own[:, :, 128:], south[:, :, 128:]], axis=1)
    left = jnp.concatenate([north[:, :, :128], own[:, :, :128], south[:, :, :128]], axis=1)
    west = send(right, "col", 1)
    east = send(left, "col", -1)
    results = down(own, north, south, west, east, make_tables(class_weight, class_stiffness))
    message = results[-1].reshape(256, 2, 128)
    gathered = lax.all_to_all(message, ("row", "col"), 0, 0).reshape(512, 128)
    place = jnp.stack([lax.axis_index("row"), lax.axis_index("col")]).astype(jnp.int32)
    return up(place, gathered, results[:-1])


def solution(mesh):
    in_specs = (P(None, "row", "col"), P("row", "col"), P(), P())
    out_specs = P(None, "row", "col")
    return jax.shard_map(local, mesh=mesh, in_specs=in_specs, out_specs=out_specs, check_vma=False)
```

```python
import jax
import jax.numpy as jnp
from jax import lax
from jax.experimental import pallas as pl
from jax.experimental.pallas import tpu as pltpu
from jax.sharding import PartitionSpec as P

CG_ITERS = 12
FAR = -1.0e4
TILES = (48, 24, 12, 6, 3)
LANES = (384, 256, 128, 128, 128)
F32 = jnp.float32
BF16 = jnp.bfloat16
BLACK, EDGE, INV, STATE = 4, 6, 11, 13


def iota(shape, axis):
    return lax.broadcasted_iota(jnp.int32, shape, axis)


def roll(x, shift, axis):
    return pltpu.roll(x, shift % x.shape[axis], axis)


def dot(a, b):
    return jnp.dot(a, b, preferred_element_type=F32)


def split(x):
    high = x.astype(BF16)
    return high, (x - high.astype(F32)).astype(BF16)


def times(x, pattern):
    high, low = split(x)
    return dot(high, pattern) + dot(low, pattern)


def pick(pattern, x):
    high, low = split(x)
    return dot(pattern, high) + dot(pattern, low)


def onehot(condition):
    return jnp.where(condition, 1.0, 0.0).astype(BF16)


def even_lanes(shape):
    return iota(shape, len(shape) - 1) % 2 == 0


def signed_lane(level, lane):
    width = LANES[level]
    own = 256 >> level
    return jnp.where(lane < (own + width) // 2, lane, lane - width)


def coarse_lane(level, lane):
    c = signed_lane(level, lane) >> 1
    return jnp.where(c < 0, c + LANES[level + 1], c)


def side_lane(field, lane3):
    c = (signed_lane(3, lane3) >> 1) + 64 * field
    return jnp.where(c < 0, c + 128, c)


def ends(ref, index, count):
    ref[index, 0] = roll(ref[index, count], 1, 0)
    ref[index, count + 1] = roll(ref[index, 1], -1, 0)


def loop(count, body, unroll):
    if count <= unroll:
        for i in range(count):
            body(i)
        return

    def step(i, carry):
        for j in range(unroll):
            body(i * unroll + j)
        return carry

    lax.fori_loop(0, count // unroll, step, 0)


def pull_red(a, black, f, state, even):
    b = black[f, a + 1]
    total = state[EDGE, a + 1] * b + state[EDGE + 1, a + 1] * jnp.where(even, black[f, a], black[f, a + 2])
    return total + state[EDGE + 3, a + 1] * roll(b, -1, 1) + roll(state[EDGE + 4, a + 1] * b, 1, 1)


def pull_black(a, red, f, state, even):
    r = red[f, a + 1]
    total = state[EDGE, a + 1] * r + state[EDGE + 2, a + 1] * jnp.where(even, red[f, a + 2], red[f, a])
    return total + state[EDGE + 4, a + 1] * roll(r, -1, 1) + roll(state[EDGE + 3, a + 1] * r, 1, 1)


def lookup(table, index):
    parts = []
    for c in range(index.shape[1] // 128):
        parts.append(jnp.take_along_axis(table, index[:, c * 128 : (c + 1) * 128], axis=1))
    return jnp.concatenate(parts, axis=1)


def edges4(g, w):
    k = [jnp.maximum(g + roll(g, s, x), 0.0) for s, x in ((1, 0), (-1, 0), (1, 1), (-1, 1))]
    return k, 1.0 / jnp.maximum(w + k[0] + k[1] + k[2] + k[3], 1e-20)


def pull4(k, v):
    return k[0] * roll(v, 1, 0) + k[1] * roll(v, -1, 0) + k[2] * roll(v, 1, 1) + k[3] * roll(v, -1, 1)


def red4():
    return (iota((24, 128), 0) + iota((24, 128), 1)) % 2 == 0


def rows_kernel(observed, classes, own, top, bottom):
    x = (classes[...] + 1).astype(F32)
    own[...] = x
    top[2] = x[:64]
    bottom[2] = x[192:]
    for f in range(2):
        top[f] = observed[f, 0:64]
        bottom[f] = observed[f, 192:256]


def cols_kernel(observed, classes, north, south, left, right):
    low = iota((192, 128), 1) < 64
    for f in range(3):
        own = observed.at[f] if f < 2 else classes
        sides = []
        for c in (0, 128):
            lanes = slice(c, c + 128)
            b = jnp.concatenate([own[192:256, lanes], south[f, :, lanes], north[f, :, lanes]], axis=0)
            sides.append((own[0:192, lanes], b))
        left[f] = jnp.where(low, sides[0][0], roll(sides[0][1], 64, 1))
        right[f] = jnp.where(low, roll(sides[1][1], 64, 1), sides[1][0])


def message_row(x, pattern, mine):
    return jnp.sum(jnp.where(mine, times(x, pattern), 0.0), axis=0, keepdims=True)


def down_kernel(place, observed, classes, north, south, west, east, tables, *rest):
    saved = rest[:4]
    saved4, message = rest[4:6]
    states = rest[6:10]
    gw, red, full, sums, frame, strip, nat, arrived, sent = rest[10:]

    pieces = []
    for f in range(3):
        own = observed.at[f] if f < 2 else classes
        for half in range(2):
            lanes = pl.ds(half * 128, 128)
            pieces.append((own.at[:, lanes], frame.at[f, half, pl.ds(0, 256), :]))
            pieces.append((south.at[f, :, lanes], frame.at[f, half, pl.ds(256, 64), :]))
            pieces.append((north.at[f, :, lanes], frame.at[f, half, pl.ds(320, 64), :]))
    pieces += [(west, strip.at[0]), (east, strip.at[1])]
    copies = [pltpu.make_async_copy(a, b, arrived.at[i]) for i, (a, b) in enumerate(pieces)]
    for copy in copies:
        copy.start()
    for copy in copies:
        copy.wait()
    low = iota((192, 128), 1) < 64
    for f in range(3):
        w, e = strip[0, f], strip[1, f]
        frame[f, 2, 0:192, :] = jnp.where(low, e, w)
        frame[f, 2, 192:384, :] = roll(jnp.where(low, w, e), 64, 1)

    tab_g = jnp.broadcast_to(tables[0:1, :], (8, 128))
    tab_w = jnp.broadcast_to(tables[1:2, :], (8, 128))

    def frame_tile(f, a):
        return jnp.concatenate([frame[f, c, pl.ds(a, 8, stride=48), :] for c in range(3)], axis=1)

    outgoing = []
    for level in range(4):
        count, width = TILES[level] // 2, LANES[level]
        even = even_lanes((8, width))
        state = states[level]
        unroll = (4, 4, 6, 3)[level]
        here = pl.ds(0, width)

        def pack(a, level=level, even=even, state=state, here=here):
            for f in range(2):
                if level == 0:
                    x, y = frame_tile(f, 2 * a), frame_tile(f, 2 * a + 1)
                else:
                    x, y = full[f, 2 * a, :, here], full[f, 2 * a + 1, :, here]
                state[f, a + 1] = jnp.where(even, x, y)
                state[2 + f, a + 1] = jnp.where(even, y, x)
            if level == 0:
                i, j = (frame_tile(2, 2 * a + k).astype(jnp.int32) for k in range(2))
                pairs = ((lookup(tab_g, i), lookup(tab_g, j)), (lookup(tab_w, i), lookup(tab_w, j)))
            else:
                pairs = tuple((full[q, 2 * a, :, here], full[q, 2 * a + 1, :, here]) for q in (2, 3))
            for q, (x, y) in enumerate(pairs):
                gw[2 * q, a + 1, :, here] = jnp.where(even, x, y)
                gw[2 * q + 1, a + 1, :, here] = jnp.where(even, y, x)

        loop(count, pack, unroll)
        for q in range(2):
            gw[q, 0, :, here] = roll(gw[q, count, :, here], 1, 0)
            gw[q, count + 1, :, here] = roll(gw[q, 1, :, here], -1, 0)

        def edges(a, even=even, state=state, here=here):
            r, b = gw[0, a + 1, :, here], gw[1, a + 1, :, here]
            same = jnp.maximum(r + b, 0.0)
            r_other = jnp.maximum(r + jnp.where(even, gw[1, a, :, here], gw[1, a + 2, :, here]), 0.0)
            b_other = jnp.maximum(b + jnp.where(even, gw[0, a + 2, :, here], gw[0, a, :, here]), 0.0)
            r_east = jnp.maximum(r + roll(b, -1, 1), 0.0)
            b_east = jnp.maximum(b + roll(r, -1, 1), 0.0)
            r_inv = 1.0 / jnp.maximum(gw[2, a + 1, :, here] + same + r_other + r_east + roll(b_east, 1, 1), 1e-20)
            b_inv = 1.0 / jnp.maximum(gw[3, a + 1, :, here] + same + b_other + b_east + roll(r_east, 1, 1), 1e-20)
            for i, x in enumerate((same, r_other, b_other, r_east, b_east, r_inv, b_inv)):
                state[EDGE + i, a + 1] = x
            for f in range(2):
                red[f, a + 1, :, here] = state[f, a + 1] * r_inv
            sums[2, a, :, here] = 0.5 * (r + b)
            sums[3, a, :, here] = gw[2, a + 1, :, here] + gw[3, a + 1, :, here]

        loop(count, edges, unroll)
        for f in range(2):
            red[f, 0, :, here] = roll(red[f, count, :, here], 1, 0)
            red[f, count + 1, :, here] = roll(red[f, 1, :, here], -1, 0)

        def first_black(a, even=even, state=state, here=here):
            view = red.at[:, :, :, here]
            for f in range(2):
                state[BLACK + f, a + 1] = (state[2 + f, a + 1] + pull_black(a, view, f, state, even)) * state[INV + 1, a + 1]

        loop(count, first_black, unroll)
        for f in range(2):
            ends(state, BLACK + f, count)
        outgoing.append(pltpu.make_async_copy(state, saved[level], sent.at[level]))
        outgoing[-1].start()

        def restrict(a, even=even, state=state, here=here):
            for f in range(2):
                sums[f, a, :, here] = pull_red(a, state.at[BLACK : BLACK + 2], f, state, even)

        loop(count, restrict, unroll)
        fine = iota((width, LANES[level + 1]), 0)
        lane = iota((width, LANES[level + 1]), 1)
        if level < 3:
            pattern = onehot(coarse_lane(level, fine) == lane)
            for q in range(4):
                x = sums[q, 0:count, :, here].reshape(count * 8, width)
                full[q, 0:count, :, pl.ds(0, LANES[level + 1])] = times(x, pattern).reshape(count, 8, LANES[level + 1])
        else:
            first, second = (onehot(side_lane(f, fine) == lane) for f in range(2))
            x = [sums[q, 0:3, :, here].reshape(24, 128) for q in range(4)]
            results = [times(x[0], first) + times(x[1], second)] + [times(x[q], first + second) for q in (2, 3)]
            for q in range(3):
                for a in range(3):
                    nat[q, pl.ds(a, 8, stride=3), :] = results[q][a * 8 : a * 8 + 8]

    rhs, g, w = nat[0], nat[1], nat[2]
    is_red = red4()
    k, inv = edges4(g, w)
    v = jnp.where(is_red, rhs * inv, 0.0)
    v = jnp.where(is_red, v, (rhs + pull4(k, v)) * inv)
    merged = jnp.where(is_red, rhs, v)
    saved4[0] = merged
    saved4[1] = rhs
    saved4[2] = g
    saved4[3] = w
    nat[3] = jnp.where(is_red, pull4(k, v), 0.0)
    nat[4] = jnp.where(iota((24, 128), 1) < 64, 0.5 * g, w)

    lane = iota((128, 128), 0)
    l = iota((128, 128), 1)
    sub, at = iota((8, 128), 0), iota((8, 128), 1)
    pattern = onehot(jnp.logical_and(lane // 64 == l // 64, (lane % 64) // 2 == l % 8))
    mine = sub == (at // 8) % 8
    common = []
    for q in (3, 4):
        x = nat[q, pl.ds(0, 8, stride=2), :] + nat[q, pl.ds(1, 8, stride=2), :]
        common.append(message_row(x, pattern, mine))
    pattern = onehot(jnp.logical_and(lane // 64 == l // 64, lane % 64 == l % 16))
    top = message_row(merged[0:8], pattern, sub == (at // 16) % 4)
    bottom = message_row(merged[8:16], pattern, sub == (at // 16) % 4 + 4)
    mine = iota((16, 128), 0) == (iota((16, 128), 1) // 4) % 16
    pattern = onehot(jnp.logical_and(lane // 64 == l // 64, lane % 64 == l % 4))
    left = message_row(merged[0:16], pattern, mine)
    pattern = onehot(jnp.logical_and(lane // 64 == l // 64, lane % 64 == l % 4 + 12))
    right = message_row(merged[0:16], pattern, mine)

    block = jnp.concatenate((common + [jnp.zeros((1, 128), F32)]) * 8, axis=0)

    def send(i, carry):
        message[pl.ds(pl.multiple_of(i * 24, 8), 24), :] = block
        return carry

    lax.fori_loop(0, 32, send, 0)
    row, col = place[0], place[1]
    for dr, dc, what in NEIGHBOURS:
        x = {-1: top, 1: bottom}.get(dr, left if dc < 0 else right)
        r, c = row + dr, col + dc

        @pl.when(jnp.logical_and(jnp.logical_and(r >= 0, r < 16), jnp.logical_and(c >= 0, c < 16)))
        def _(r=r, c=c, x=x):
            message[pl.ds((r * 16 + c) * 3 + 2, 1), :] = x

    for copy in outgoing:
        copy.wait()


NEIGHBOURS = [(dr, dc, None) for dr in (-1, 0, 1) for dc in (-1, 0, 1) if dr or dc]


def cg(gathered, kc, e, r, d, q):
    lane = iota((8, 128), 1)
    sub = iota((8, 128), 0)
    group = lane // 8
    arrays = [[None] * 16 for _ in range(4)]
    for hi in range(2):
        for pair in range(2):
            v = [gathered[pl.ds((hi * 128 + c) * 3 + pair, 8, stride=48), :] for c in range(16)]
            for k in (1, 2, 4, 8):
                low = (group // k) % 2 == 0
                for c in range(16):
                    if not c & k:
                        x, y = v[c], v[c | k]
                        v[c] = jnp.where(low, x, roll(y, 8 * k, 1))
                        v[c | k] = jnp.where(low, roll(x, -8 * k, 1), y)
            for i in range(16):
                arrays[2 * pair + i // 8][hi * 8 + i % 8] = v[i]

    def north(tile, t):
        if t % 8:
            return tile(t - 1)
        turned = roll(tile(t + 7), 1, 0)
        return turned if t == 0 else jnp.where(sub == 0, roll(tile(7), 1, 0), turned)

    def south(tile, t):
        if t % 8 != 7:
            return tile(t + 1)
        turned = roll(tile(t - 7), -1, 0)
        return turned if t == 15 else jnp.where(sub == 7, roll(tile(8), -1, 0), turned)

    g = arrays[2]
    for t in range(16):
        up = jnp.maximum(g[t] + north(lambda i: g[i], t), 0.0)
        down = jnp.maximum(g[t] + south(lambda i: g[i], t), 0.0)
        if t == 0:
            up = jnp.where(sub == 0, 0.0, up)
        if t == 15:
            down = jnp.where(sub == 7, 0.0, down)
        left = jnp.where(lane == 0, 0.0, jnp.maximum(g[t] + roll(g[t], 1, 1), 0.0))
        right = jnp.where(lane == 127, 0.0, jnp.maximum(g[t] + roll(g[t], -1, 1), 0.0))
        kc[0, t] = up
        kc[1, t] = down
        kc[2, t] = left
        kc[3, t] = right
        kc[4, t] = arrays[3][t] + up + down + left + right

    norm = []
    for f in range(2):
        total = 0.0
        for t in range(16):
            x = arrays[f][t]
            e[f, t] = jnp.zeros_like(x)
            r[f, t] = x
            d[f, t] = x
            total += x * x
        norm.append(jnp.sum(total, axis=(0, 1), keepdims=True))

    def iterate(_, norm):
        alpha = []
        for f in range(2):
            tile = lambda i, f=f: d[f, i]
            total = 0.0
            for t in range(16):
                x = d[f, t]
                image = kc[4, t] * x - (
                    kc[0, t] * north(tile, t)
                    + kc[1, t] * south(tile, t)
                    + kc[2, t] * roll(x, 1, 1)
                    + kc[3, t] * roll(x, -1, 1)
                )
                q[f, t] = image
                total += x * image
            alpha.append(norm[f] / jnp.sum(total, axis=(0, 1), keepdims=True))
        fresh = []
        for f in range(2):
            total = 0.0
            for t in range(16):
                e[f, t] = e[f, t] + alpha[f] * d[f, t]
                x = r[f, t] - alpha[f] * q[f, t]
                r[f, t] = x
                total += x * x
            fresh.append(jnp.sum(total, axis=(0, 1), keepdims=True))
        for f in range(2):
            beta = fresh[f] / norm[f]
            for t in range(16):
                d[f, t] = r[f, t] + beta * d[f, t]
        return tuple(fresh)

    lax.fori_loop(0, CG_ITERS, iterate, tuple(norm))


def merged_frame(place, gathered, merged):
    row, col = place[0], place[1]
    at = iota((24, 128), 0)
    l = iota((24, 128), 1)
    total = {}
    for dr, dc, _ in NEIGHBOURS:
        r, c = row + dr, col + dc
        there = jnp.logical_and(jnp.logical_and(r >= 0, r < 16), jnp.logical_and(c >= 0, c < 16))
        index = jnp.where(there, (r * 16 + c) * 3 + 2, 0)
        x = gathered[pl.ds(index, 1), :] * jnp.where(there, 1.0, 0.0)
        if dr:
            mine = at == (20 if dr < 0 else 16) + (l // 16) % 4
        else:
            mine = at == (l // 4) % 16
        key = dc if dr else 2 * dc
        total[key] = total.get(key, 0.0) + jnp.where(mine, jnp.broadcast_to(x, (24, 128)), 0.0)
    l = iota((128, 128), 0)
    lane = iota((128, 128), 1)
    base = (l // 64) * 64
    j, c = l % 16, l % 4
    patterns = {
        0: lane == base + j,
        -1: jnp.logical_and(j >= 12, lane == (base + j - 16) % 128),
        1: jnp.logical_and(j < 4, lane == base + 16 + j),
        -2: lane == (base + c - 4) % 128,
        2: lane == base + 16 + c,
    }
    own = jnp.logical_and(at < 16, iota((24, 128), 1) % 64 < 16)
    result = jnp.where(own, merged, 0.0)
    for key, x in total.items():
        result += times(x, onehot(patterns[key]))
    return result


def up_kernel(place, gathered, saved4, *rest):
    saved, out = rest[:4], rest[4]
    states = rest[5:9]
    full, red, blk, kc, e, r, d, q, result, nat, arrived, sent = rest[9:]
    copies = [pltpu.make_async_copy(saved[level], states[level], arrived.at[level]) for level in range(4)]
    for copy in copies[::-1]:
        copy.start()
    cg(gathered, kc, e, r, d, q)

    n = iota((24, 128), 1)
    at = iota((24, 128), 0)
    grid_row = (n // 64) * 64 + (n % 8) * 8 + (n // 8) % 8
    rows = onehot(grid_row == place[0] * 8 + (jnp.where(at < 20, at, at - 24) >> 1))
    j = iota((128, 128), 0)
    lane = iota((128, 128), 1)
    correction = 0.0
    for f in range(2):
        c = (lane + 32) % 128 - 32 - 64 * f
        cols = onehot(jnp.logical_and(jnp.logical_and(c >= -32, c < 32), j == place[1] * 8 + (c >> 1)))
        whole = jnp.concatenate([e[f, t] for t in range(16)], axis=0)
        correction += times(pick(rows, whole), cols)

    is_red = red4()
    merged = merged_frame(place, gathered, saved4[0])
    k, inv = edges4(saved4[2], saved4[3])
    x = jnp.where(is_red, 0.0, merged + correction)
    x = jnp.where(is_red, (merged + pull4(k, x)) * inv, 0.0)
    nat[...] = jnp.where(is_red, x, (saved4[1] + pull4(k, x)) * inv)
    ordered = jnp.concatenate([nat[pl.ds(a, 8, stride=3), :] for a in range(3)], axis=0)

    for level in range(3, -1, -1):
        count, width = TILES[level] // 2, LANES[level]
        even = even_lanes((8, width))
        state = states[level]
        unroll = (4, 4, 6, 3)[level]
        here = pl.ds(0, width)
        if level == 3:
            lane, wide = iota((128, 128), 0), iota((128, 128), 1)
            corrections = [times(ordered, onehot(side_lane(f, wide) == lane)) for f in range(2)]
        else:
            coarse = LANES[level + 1]
            lane, wide = iota((coarse, width), 0), iota((coarse, width), 1)
            pattern = onehot(coarse_lane(level, wide) == lane)
            corrections = [
                times(full[f, 0:count, :, pl.ds(0, coarse)].reshape(count * 8, coarse), pattern) for f in range(2)
            ]
        copies[level].wait()
        for f in range(2):
            blk[f, 1 : count + 1, :, here] = state[BLACK + f, 1 : count + 1] + corrections[f].reshape(count, 8, width)
            blk[f, 0, :, here] = roll(blk[f, count, :, here], 1, 0)
            blk[f, count + 1, :, here] = roll(blk[f, 1, :, here], -1, 0)

        def second_red(a, even=even, state=state, here=here):
            view = blk.at[:, :, :, here]
            for f in range(2):
                red[f, a + 1, :, here] = (state[f, a + 1] + pull_red(a, view, f, state, even)) * state[INV, a + 1]

        loop(count, second_red, unroll)
        for f in range(2):
            red[f, 0, :, here] = roll(red[f, count, :, here], 1, 0)
            red[f, count + 1, :, here] = roll(red[f, 1, :, here], -1, 0)

        def second_black(a, level=level, even=even, state=state, here=here):
            view = red.at[:, :, :, here]
            for f in range(2):
                x = red[f, a + 1, :, here]
                y = (state[2 + f, a + 1] + pull_black(a, view, f, state, even)) * state[INV + 1, a + 1]
                first, second = jnp.where(even, x, y), jnp.where(even, y, x)
                if level:
                    full[f, 2 * a, :, here] = first
                    full[f, 2 * a + 1, :, here] = second
                else:
                    for half in range(2):
                        lanes = slice(128 * half, 128 + 128 * half)
                        result[f, half, pl.ds(2 * a, 8, stride=48), :] = first[:, lanes]
                        result[f, half, pl.ds(2 * a + 1, 8, stride=48), :] = second[:, lanes]

        loop(count, second_black, unroll)

    copies = []
    for f in range(2):
        for half in range(2):
            source = result.at[f, half, pl.ds(0, 256), :]
            copies.append(pltpu.make_async_copy(source, out.at[f, :, pl.ds(half * 128, 128)], sent.at[2 * f + half]))
    for copy in copies:
        copy.start()
    for copy in copies:
        copy.wait()


VMEM = pl.BlockSpec(memory_space=pltpu.VMEM)
ANY = pl.BlockSpec(memory_space=pl.ANY)
SMEM = pl.BlockSpec(memory_space=pltpu.SMEM)
PARAMS = pltpu.CompilerParams(vmem_limit_bytes=48 * 1024 * 1024)


def shaped(*shape):
    return jax.ShapeDtypeStruct(shape, F32)


def scratch(*shape):
    return pltpu.VMEM(shape, F32)


def state_shapes():
    return [(STATE, TILES[level] // 2 + 2, 8, LANES[level]) for level in range(4)]


def row_strips(observed, classes):
    return pl.pallas_call(
        rows_kernel,
        out_shape=[shaped(256, 256), shaped(3, 64, 256), shaped(3, 64, 256)],
        in_specs=[VMEM] * 2,
        out_specs=[VMEM] * 3,
        compiler_params=PARAMS,
        name="rows",
    )(observed, classes)


def col_strips(observed, classes, north, south):
    return pl.pallas_call(
        cols_kernel,
        out_shape=[shaped(3, 192, 128)] * 2,
        in_specs=[VMEM] * 4,
        out_specs=[VMEM] * 2,
        compiler_params=PARAMS,
        name="cols",
    )(observed, classes, north, south)


def down(place, observed, classes, north, south, west, east, tables):
    return pl.pallas_call(
        down_kernel,
        out_shape=[shaped(*s) for s in state_shapes()] + [shaped(4, 24, 128), shaped(768, 128)],
        in_specs=[SMEM] + [ANY] * 6 + [VMEM],
        out_specs=[ANY] * 4 + [VMEM] * 2,
        scratch_shapes=[scratch(*s) for s in state_shapes()]
        + [
            scratch(4, 26, 8, 384),
            scratch(2, 26, 8, 384),
            scratch(4, 24, 8, 256),
            scratch(4, 24, 8, 384),
            scratch(3, 3, 384, 128),
            scratch(2, 3, 192, 128),
            scratch(5, 24, 128),
            pltpu.SemaphoreType.DMA((20,)),
            pltpu.SemaphoreType.DMA((4,)),
        ],
        compiler_params=PARAMS,
        name="down",
    )(place, observed, classes, north, south, west, east, tables)


def up(place, gathered, saved4, saved):
    return pl.pallas_call(
        up_kernel,
        out_shape=shaped(2, 256, 256),
        in_specs=[SMEM] + [VMEM] * 2 + [ANY] * 4,
        out_specs=ANY,
        scratch_shapes=[scratch(*s) for s in state_shapes()]
        + [
            scratch(2, 24, 8, 256),
            scratch(2, 26, 8, 384),
            scratch(2, 26, 8, 384),
            scratch(5, 16, 8, 128),
            scratch(2, 16, 8, 128),
            scratch(2, 16, 8, 128),
            scratch(2, 16, 8, 128),
            scratch(2, 16, 8, 128),
            scratch(2, 2, 384, 128),
            scratch(24, 128),
            pltpu.SemaphoreType.DMA((4,)),
            pltpu.SemaphoreType.DMA((4,)),
        ],
        compiler_params=PARAMS,
        name="up",
    )(place, gathered, saved4, *saved)


def make_tables(class_weight, class_stiffness):
    pad = lambda x, first: jnp.pad(jnp.concatenate([jnp.full((1,), first, F32), x]), (0, 119))
    return jnp.stack([pad(0.5 * class_stiffness, FAR), pad(class_weight, 0.0)])


def send(x, axis, step):
    count = lax.axis_size(axis)
    return lax.ppermute(x, axis, [(i, i + step) for i in range(count) if 0 <= i + step < count])


def local(observed, coherence_class, class_weight, class_stiffness):
    place = jnp.stack([lax.axis_index("row"), lax.axis_index("col")]).astype(jnp.int32)
    classes, top, bottom = row_strips(observed, coherence_class)
    north = send(bottom, "row", 1)
    south = send(top, "row", -1)
    left, right = col_strips(observed, classes, north, south)
    west = send(right, "col", 1)
    east = send(left, "col", -1)
    tables = make_tables(class_weight, class_stiffness)
    *saved, saved4, message = down(place, observed, classes, north, south, west, east, tables)
    gathered = lax.all_to_all(message.reshape(256, 1, 384), ("row", "col"), 0, 0).reshape(768, 128)
    return up(place, gathered, saved4, saved)


def solution(mesh):
    in_specs = (P(None, "row", "col"), P("row", "col"), P(), P())
    out_specs = P(None, "row", "col")
    return jax.shard_map(local, mesh=mesh, in_specs=in_specs, out_specs=out_specs, check_vma=False)
```

```python
import jax
import jax.numpy as jnp
from jax import lax
from jax.experimental import pallas as pl
from jax.experimental.pallas import tpu as pltpu
from jax.sharding import PartitionSpec as P

CG_ITERS = 12
FAR = -1.0e4
TILES = (48, 24, 12, 6, 3)
LANES = (384, 256, 128, 128, 128)
F32 = jnp.float32
BF16 = jnp.bfloat16
BLACK, EDGE, INV, STATE = 4, 6, 11, 13


def iota(shape, axis):
    return lax.broadcasted_iota(jnp.int32, shape, axis)


def roll(x, shift, axis):
    return pltpu.roll(x, shift % x.shape[axis], axis)


def dot(a, b):
    return jnp.dot(a, b, preferred_element_type=F32)


def split(x):
    high = x.astype(BF16)
    return high, (x - high.astype(F32)).astype(BF16)


def times(x, pattern):
    high, low = split(x)
    return dot(high, pattern) + dot(low, pattern)


def pick(pattern, x):
    high, low = split(x)
    return dot(pattern, high) + dot(pattern, low)


def onehot(condition):
    return jnp.where(condition, 1.0, 0.0).astype(BF16)


def even_lanes(shape):
    return iota(shape, len(shape) - 1) % 2 == 0


def signed_lane(level, lane):
    width = LANES[level]
    own = 256 >> level
    return jnp.where(lane < (own + width) // 2, lane, lane - width)


def coarse_lane(level, lane):
    c = signed_lane(level, lane) >> 1
    return jnp.where(c < 0, c + LANES[level + 1], c)


def side_lane(field, lane3):
    c = (signed_lane(3, lane3) >> 1) + 64 * field
    return jnp.where(c < 0, c + 128, c)


def ends(ref, index, count):
    ref[index, 0] = roll(ref[index, count], 1, 0)
    ref[index, count + 1] = roll(ref[index, 1], -1, 0)


def loop(count, body, unroll):
    if count <= unroll:
        for i in range(count):
            body(i)
        return

    def step(i, carry):
        for j in range(unroll):
            body(i * unroll + j)
        return carry

    lax.fori_loop(0, count // unroll, step, 0)


def pull_red(a, black, f, state, even):
    b = black[f, a + 1]
    total = state[EDGE, a + 1] * b + state[EDGE + 1, a + 1] * jnp.where(even, black[f, a], black[f, a + 2])
    return total + state[EDGE + 3, a + 1] * roll(b, -1, 1) + roll(state[EDGE + 4, a + 1] * b, 1, 1)


def pull_black(a, red, f, state, even):
    r = red[f, a + 1]
    total = state[EDGE, a + 1] * r + state[EDGE + 2, a + 1] * jnp.where(even, red[f, a + 2], red[f, a])
    return total + state[EDGE + 4, a + 1] * roll(r, -1, 1) + roll(state[EDGE + 3, a + 1] * r, 1, 1)


def lookup(table, index):
    parts = []
    for c in range(index.shape[1] // 128):
        parts.append(jnp.take_along_axis(table, index[:, c * 128 : (c + 1) * 128], axis=1))
    return jnp.concatenate(parts, axis=1)


def edges4(g, w):
    k = [jnp.maximum(g + roll(g, s, x), 0.0) for s, x in ((1, 0), (-1, 0), (1, 1), (-1, 1))]
    return k, 1.0 / jnp.maximum(w + k[0] + k[1] + k[2] + k[3], 1e-20)


def pull4(k, v):
    return k[0] * roll(v, 1, 0) + k[1] * roll(v, -1, 0) + k[2] * roll(v, 1, 1) + k[3] * roll(v, -1, 1)


def red4():
    return (iota((24, 128), 0) + iota((24, 128), 1)) % 2 == 0


def place():
    return lax.axis_index("row"), lax.axis_index("col")


def fold(x, low, swap):
    half = x.shape[0] // 2
    first, second = x[:half], x[half:]
    if swap:
        return jnp.where(low, roll(second, 64, 1), first)
    return jnp.where(low, first, roll(second, 64, 1))


def sides_kernel(observed, classes, own, row_a, row_b, col_a, col_b):
    row, col = place()
    own[0:2] = observed[...]
    own[2] = classes[...]
    low = iota((128, 128), 1) < 64
    for f in range(3):
        x = own.at[f]
        top, bottom = x[0:64, :], x[192:256, :]
        row_a[f] = jnp.where(row % 2 == 0, bottom, top)
        row_b[f] = jnp.where(row % 2 == 0, top, bottom)
        left, right = fold(x[:, 0:128], low, False), fold(x[:, 128:256], low, True)
        col_a[f] = jnp.where(col % 2 == 0, right, left)
        col_b[f] = jnp.where(col % 2 == 0, left, right)


def corners_kernel(row_a, row_b, out_a, out_b):
    row, col = place()
    low = iota((64, 128), 1) < 64
    for f in range(3):
        a, b = row_a[f], row_b[f]
        south, north = jnp.where(row % 2 == 0, a, b), jnp.where(row % 2 == 0, b, a)
        x = jnp.concatenate([south, north], axis=0)
        left, right = fold(x[:, 0:128], low, False), fold(x[:, 128:256], low, True)
        out_a[f] = jnp.where(col % 2 == 0, right, left)
        out_b[f] = jnp.where(col % 2 == 0, left, right)


def message_row(x, pattern, mine):
    return jnp.sum(jnp.where(mine, times(x, pattern), 0.0), axis=0, keepdims=True)


def down_kernel(own, row_a, row_b, col_a, col_b, corner_a, corner_b, tables, *rest):
    saved = rest[:4]
    saved4, message = rest[4:6]
    states = rest[6:10]
    gw, red, full, sums, frame, side, corner, nat, arrived, sent = rest[10:]
    row, col = place()
    odd_row, odd_col = row % 2, col % 2

    pieces = []
    for f in range(3):
        for half in range(2):
            lanes = pl.ds(half * 128, 128)
            pieces.append((own.at[f, :, lanes], frame.at[f, half, pl.ds(0, 256), :]))
            south = pl.ds(pl.multiple_of(256 + 64 * odd_row, 64), 64)
            north = pl.ds(pl.multiple_of(320 - 64 * odd_row, 64), 64)
            pieces.append((row_a.at[f, :, lanes], frame.at[f, half, south, :]))
            pieces.append((row_b.at[f, :, lanes], frame.at[f, half, north, :]))
    pieces += [(col_a, side.at[odd_col]), (col_b, side.at[1 - odd_col])]
    pieces += [(corner_a, corner.at[odd_col]), (corner_b, corner.at[1 - odd_col])]
    copies = [pltpu.make_async_copy(a, b, arrived.at[i]) for i, (a, b) in enumerate(pieces)]
    for copy in copies:
        copy.start()
    for copy in copies:
        copy.wait()
    for ref, start, size in ((side, 0, 128), (corner, 256, 64)):
        low = iota((size, 128), 1) < 64
        for f in range(3):
            e, w = ref[0, f], ref[1, f]
            frame[f, 2, start : start + size, :] = jnp.where(low, e, w)
            frame[f, 2, start + size : start + 2 * size, :] = roll(jnp.where(low, w, e), 64, 1)

    tab_g = jnp.broadcast_to(tables[0:1, :], (8, 128))
    tab_w = jnp.broadcast_to(tables[1:2, :], (8, 128))

    def frame_tile(f, a):
        return jnp.concatenate([frame[f, c, pl.ds(a, 8, stride=48), :] for c in range(3)], axis=1)

    outgoing = []
    for level in range(4):
        count, width = TILES[level] // 2, LANES[level]
        even = even_lanes((8, width))
        state = states[level]
        unroll = (12, 12, 6, 3)[level]
        here = pl.ds(0, width)

        def pack(a, level=level, even=even, state=state, here=here):
            for f in range(2):
                if level == 0:
                    x, y = frame_tile(f, 2 * a), frame_tile(f, 2 * a + 1)
                else:
                    x, y = full[f, 2 * a, :, here], full[f, 2 * a + 1, :, here]
                state[f, a + 1] = jnp.where(even, x, y)
                state[2 + f, a + 1] = jnp.where(even, y, x)
            if level == 0:
                i, j = (frame_tile(2, 2 * a + k).astype(jnp.int32) for k in range(2))
                pairs = ((lookup(tab_g, i), lookup(tab_g, j)), (lookup(tab_w, i), lookup(tab_w, j)))
            else:
                pairs = tuple((full[q, 2 * a, :, here], full[q, 2 * a + 1, :, here]) for q in (2, 3))
            for q, (x, y) in enumerate(pairs):
                gw[2 * q, a + 1, :, here] = jnp.where(even, x, y)
                gw[2 * q + 1, a + 1, :, here] = jnp.where(even, y, x)

        loop(count, pack, unroll)
        for q in range(2):
            gw[q, 0, :, here] = roll(gw[q, count, :, here], 1, 0)
            gw[q, count + 1, :, here] = roll(gw[q, 1, :, here], -1, 0)

        def edges(a, even=even, state=state, here=here):
            r, b = gw[0, a + 1, :, here], gw[1, a + 1, :, here]
            same = jnp.maximum(r + b, 0.0)
            r_other = jnp.maximum(r + jnp.where(even, gw[1, a, :, here], gw[1, a + 2, :, here]), 0.0)
            b_other = jnp.maximum(b + jnp.where(even, gw[0, a + 2, :, here], gw[0, a, :, here]), 0.0)
            r_east = jnp.maximum(r + roll(b, -1, 1), 0.0)
            b_east = jnp.maximum(b + roll(r, -1, 1), 0.0)
            r_inv = 1.0 / jnp.maximum(gw[2, a + 1, :, here] + same + r_other + r_east + roll(b_east, 1, 1), 1e-20)
            b_inv = 1.0 / jnp.maximum(gw[3, a + 1, :, here] + same + b_other + b_east + roll(r_east, 1, 1), 1e-20)
            for i, x in enumerate((same, r_other, b_other, r_east, b_east, r_inv, b_inv)):
                state[EDGE + i, a + 1] = x
            for f in range(2):
                red[f, a + 1, :, here] = state[f, a + 1] * r_inv
            sums[2, a, :, here] = 0.5 * (r + b)
            sums[3, a, :, here] = gw[2, a + 1, :, here] + gw[3, a + 1, :, here]

        loop(count, edges, unroll)
        for f in range(2):
            red[f, 0, :, here] = roll(red[f, count, :, here], 1, 0)
            red[f, count + 1, :, here] = roll(red[f, 1, :, here], -1, 0)

        def first_black(a, even=even, state=state, here=here):
            view = red.at[:, :, :, here]
            for f in range(2):
                state[BLACK + f, a + 1] = (state[2 + f, a + 1] + pull_black(a, view, f, state, even)) * state[INV + 1, a + 1]

        loop(count, first_black, unroll)
        for f in range(2):
            ends(state, BLACK + f, count)
        outgoing.append(pltpu.make_async_copy(state, saved[level], sent.at[level]))
        outgoing[-1].start()

        def restrict(a, even=even, state=state, here=here):
            for f in range(2):
                sums[f, a, :, here] = pull_red(a, state.at[BLACK : BLACK + 2], f, state, even)

        loop(count, restrict, unroll)
        fine = iota((width, LANES[level + 1]), 0)
        lane = iota((width, LANES[level + 1]), 1)
        if level < 3:
            pattern = onehot(coarse_lane(level, fine) == lane)
            for q in range(4):
                x = sums[q, 0:count, :, here].reshape(count * 8, width)
                full[q, 0:count, :, pl.ds(0, LANES[level + 1])] = times(x, pattern).reshape(count, 8, LANES[level + 1])
        else:
            first, second = (onehot(side_lane(f, fine) == lane) for f in range(2))
            x = [sums[q, 0:3, :, here].reshape(24, 128) for q in range(4)]
            results = [times(x[0], first) + times(x[1], second)] + [times(x[q], first + second) for q in (2, 3)]
            for q in range(3):
                for a in range(3):
                    nat[q, pl.ds(a, 8, stride=3), :] = results[q][a * 8 : a * 8 + 8]

    rhs, g, w = nat[0], nat[1], nat[2]
    is_red = red4()
    k, inv = edges4(g, w)
    v = jnp.where(is_red, rhs * inv, 0.0)
    v = jnp.where(is_red, v, (rhs + pull4(k, v)) * inv)
    merged = jnp.where(is_red, rhs, v)
    saved4[0] = merged
    saved4[1] = rhs
    saved4[2] = g
    saved4[3] = w
    nat[3] = jnp.where(is_red, pull4(k, v), 0.0)
    nat[4] = jnp.where(iota((24, 128), 1) < 64, 0.5 * g, w)

    lane = iota((128, 128), 0)
    l = iota((128, 128), 1)
    sub, at = iota((8, 128), 0), iota((8, 128), 1)
    pattern = onehot(jnp.logical_and(lane // 64 == l // 64, (lane % 64) // 2 == l % 8))
    mine = sub == (at // 8) % 8
    common = []
    for q in (3, 4):
        x = nat[q, pl.ds(0, 8, stride=2), :] + nat[q, pl.ds(1, 8, stride=2), :]
        common.append(message_row(x, pattern, mine))
    pattern = onehot(jnp.logical_and(lane // 64 == l // 64, lane % 64 == l % 16))
    top = message_row(merged[0:8], pattern, sub == (at // 16) % 4)
    bottom = message_row(merged[8:16], pattern, sub == (at // 16) % 4 + 4)
    mine = iota((16, 128), 0) == (iota((16, 128), 1) // 4) % 16
    pattern = onehot(jnp.logical_and(lane // 64 == l // 64, lane % 64 == l % 4))
    left = message_row(merged[0:16], pattern, mine)
    pattern = onehot(jnp.logical_and(lane // 64 == l // 64, lane % 64 == l % 4 + 12))
    right = message_row(merged[0:16], pattern, mine)

    block = jnp.concatenate((common + [jnp.zeros((1, 128), F32)]) * 8, axis=0)

    def send(i, carry):
        message[pl.ds(pl.multiple_of(i * 24, 8), 24), :] = block
        return carry

    lax.fori_loop(0, 32, send, 0)
    for dr, dc, what in NEIGHBOURS:
        x = {-1: top, 1: bottom}.get(dr, left if dc < 0 else right)
        r, c = row + dr, col + dc

        @pl.when(jnp.logical_and(jnp.logical_and(r >= 0, r < 16), jnp.logical_and(c >= 0, c < 16)))
        def _(r=r, c=c, x=x):
            message[pl.ds((r * 16 + c) * 3 + 2, 1), :] = x

    for copy in outgoing:
        copy.wait()


NEIGHBOURS = [(dr, dc, None) for dr in (-1, 0, 1) for dc in (-1, 0, 1) if dr or dc]


def cg(gathered, kc, e, r, d, q):
    lane = iota((8, 128), 1)
    sub = iota((8, 128), 0)
    group = lane // 8
    arrays = [[None] * 16 for _ in range(4)]
    for hi in range(2):
        for pair in range(2):
            v = [gathered[pl.ds((hi * 128 + c) * 3 + pair, 8, stride=48), :] for c in range(16)]
            for k in (1, 2, 4, 8):
                low = (group // k) % 2 == 0
                for c in range(16):
                    if not c & k:
                        x, y = v[c], v[c | k]
                        v[c] = jnp.where(low, x, roll(y, 8 * k, 1))
                        v[c | k] = jnp.where(low, roll(x, -8 * k, 1), y)
            for i in range(16):
                arrays[2 * pair + i // 8][hi * 8 + i % 8] = v[i]

    def north(tile, t):
        if t % 8:
            return tile(t - 1)
        turned = roll(tile(t + 7), 1, 0)
        return turned if t == 0 else jnp.where(sub == 0, roll(tile(7), 1, 0), turned)

    def south(tile, t):
        if t % 8 != 7:
            return tile(t + 1)
        turned = roll(tile(t - 7), -1, 0)
        return turned if t == 15 else jnp.where(sub == 7, roll(tile(8), -1, 0), turned)

    g = arrays[2]
    for t in range(16):
        up = jnp.maximum(g[t] + north(lambda i: g[i], t), 0.0)
        down = jnp.maximum(g[t] + south(lambda i: g[i], t), 0.0)
        if t == 0:
            up = jnp.where(sub == 0, 0.0, up)
        if t == 15:
            down = jnp.where(sub == 7, 0.0, down)
        left = jnp.where(lane == 0, 0.0, jnp.maximum(g[t] + roll(g[t], 1, 1), 0.0))
        right = jnp.where(lane == 127, 0.0, jnp.maximum(g[t] + roll(g[t], -1, 1), 0.0))
        kc[0, t] = up
        kc[1, t] = down
        kc[2, t] = left
        kc[3, t] = right
        kc[4, t] = arrays[3][t] + up + down + left + right

    norm = []
    for f in range(2):
        total = 0.0
        for t in range(16):
            x = arrays[f][t]
            e[f, t] = jnp.zeros_like(x)
            r[f, t] = x
            d[f, t] = x
            total += x * x
        norm.append(jnp.sum(total, axis=(0, 1), keepdims=True))

    def iterate(_, norm):
        alpha = []
        for f in range(2):
            tile = lambda i, f=f: d[f, i]
            total = 0.0
            for t in range(16):
                x = d[f, t]
                image = kc[4, t] * x - (
                    kc[0, t] * north(tile, t)
                    + kc[1, t] * south(tile, t)
                    + kc[2, t] * roll(x, 1, 1)
                    + kc[3, t] * roll(x, -1, 1)
                )
                q[f, t] = image
                total += x * image
            alpha.append(norm[f] / jnp.sum(total, axis=(0, 1), keepdims=True))
        fresh = []
        for f in range(2):
            total = 0.0
            for t in range(16):
                e[f, t] = e[f, t] + alpha[f] * d[f, t]
                x = r[f, t] - alpha[f] * q[f, t]
                r[f, t] = x
                total += x * x
            fresh.append(jnp.sum(total, axis=(0, 1), keepdims=True))
        for f in range(2):
            beta = fresh[f] / norm[f]
            for t in range(16):
                d[f, t] = r[f, t] + beta * d[f, t]
        return tuple(fresh)

    lax.fori_loop(0, CG_ITERS, iterate, tuple(norm))


def merged_frame(gathered, merged):
    row, col = place()
    at = iota((24, 128), 0)
    l = iota((24, 128), 1)
    total = {}
    for dr, dc, _ in NEIGHBOURS:
        r, c = row + dr, col + dc
        there = jnp.logical_and(jnp.logical_and(r >= 0, r < 16), jnp.logical_and(c >= 0, c < 16))
        index = jnp.where(there, (r * 16 + c) * 3 + 2, 0)
        x = gathered[pl.ds(index, 1), :] * jnp.where(there, 1.0, 0.0)
        if dr:
            mine = at == (20 if dr < 0 else 16) + (l // 16) % 4
        else:
            mine = at == (l // 4) % 16
        key = dc if dr else 2 * dc
        total[key] = total.get(key, 0.0) + jnp.where(mine, jnp.broadcast_to(x, (24, 128)), 0.0)
    l = iota((128, 128), 0)
    lane = iota((128, 128), 1)
    base = (l // 64) * 64
    j, c = l % 16, l % 4
    patterns = {
        0: lane == base + j,
        -1: jnp.logical_and(j >= 12, lane == (base + j - 16) % 128),
        1: jnp.logical_and(j < 4, lane == base + 16 + j),
        -2: lane == (base + c - 4) % 128,
        2: lane == base + 16 + c,
    }
    own = jnp.logical_and(at < 16, iota((24, 128), 1) % 64 < 16)
    result = jnp.where(own, merged, 0.0)
    for key, x in total.items():
        result += times(x, onehot(patterns[key]))
    return result


def up_kernel(gathered, saved4, *rest):
    saved, out = rest[:4], rest[4]
    states = rest[5:9]
    full, red, blk, kc, e, r, d, q, result, nat, arrived, sent = rest[9:]
    copies = [pltpu.make_async_copy(saved[level], states[level], arrived.at[level]) for level in range(4)]
    for copy in copies[::-1]:
        copy.start()
    cg(gathered, kc, e, r, d, q)

    row, col = place()
    n = iota((24, 128), 1)
    at = iota((24, 128), 0)
    grid_row = (n // 64) * 64 + (n % 8) * 8 + (n // 8) % 8
    rows = onehot(grid_row == row * 8 + (jnp.where(at < 20, at, at - 24) >> 1))
    j = iota((128, 128), 0)
    lane = iota((128, 128), 1)
    correction = 0.0
    for f in range(2):
        c = (lane + 32) % 128 - 32 - 64 * f
        cols = onehot(jnp.logical_and(jnp.logical_and(c >= -32, c < 32), j == col * 8 + (c >> 1)))
        whole = jnp.concatenate([e[f, t] for t in range(16)], axis=0)
        correction += times(pick(rows, whole), cols)

    is_red = red4()
    merged = merged_frame(gathered, saved4[0])
    k, inv = edges4(saved4[2], saved4[3])
    x = jnp.where(is_red, 0.0, merged + correction)
    x = jnp.where(is_red, (merged + pull4(k, x)) * inv, 0.0)
    nat[...] = jnp.where(is_red, x, (saved4[1] + pull4(k, x)) * inv)
    ordered = jnp.concatenate([nat[pl.ds(a, 8, stride=3), :] for a in range(3)], axis=0)

    for level in range(3, -1, -1):
        count, width = TILES[level] // 2, LANES[level]
        even = even_lanes((8, width))
        state = states[level]
        unroll = (12, 12, 6, 3)[level]
        here = pl.ds(0, width)
        if level == 3:
            lane, wide = iota((128, 128), 0), iota((128, 128), 1)
            corrections = [times(ordered, onehot(side_lane(f, wide) == lane)) for f in range(2)]
        else:
            coarse = LANES[level + 1]
            lane, wide = iota((coarse, width), 0), iota((coarse, width), 1)
            pattern = onehot(coarse_lane(level, wide) == lane)
            corrections = [
                times(full[f, 0:count, :, pl.ds(0, coarse)].reshape(count * 8, coarse), pattern) for f in range(2)
            ]
        copies[level].wait()
        for f in range(2):
            blk[f, 1 : count + 1, :, here] = state[BLACK + f, 1 : count + 1] + corrections[f].reshape(count, 8, width)
            blk[f, 0, :, here] = roll(blk[f, count, :, here], 1, 0)
            blk[f, count + 1, :, here] = roll(blk[f, 1, :, here], -1, 0)

        def second_red(a, even=even, state=state, here=here):
            view = blk.at[:, :, :, here]
            for f in range(2):
                red[f, a + 1, :, here] = (state[f, a + 1] + pull_red(a, view, f, state, even)) * state[INV, a + 1]

        loop(count, second_red, unroll)
        for f in range(2):
            red[f, 0, :, here] = roll(red[f, count, :, here], 1, 0)
            red[f, count + 1, :, here] = roll(red[f, 1, :, here], -1, 0)

        def second_black(a, level=level, even=even, state=state, here=here):
            view = red.at[:, :, :, here]
            for f in range(2):
                x = red[f, a + 1, :, here]
                y = (state[2 + f, a + 1] + pull_black(a, view, f, state, even)) * state[INV + 1, a + 1]
                first, second = jnp.where(even, x, y), jnp.where(even, y, x)
                if level:
                    full[f, 2 * a, :, here] = first
                    full[f, 2 * a + 1, :, here] = second
                else:
                    for half in range(2):
                        lanes = slice(128 * half, 128 + 128 * half)
                        result[f, half, pl.ds(2 * a, 8, stride=48), :] = first[:, lanes]
                        result[f, half, pl.ds(2 * a + 1, 8, stride=48), :] = second[:, lanes]

        loop(count, second_black, unroll)

    copies = []
    for f in range(2):
        for half in range(2):
            source = result.at[f, half, pl.ds(0, 256), :]
            copies.append(pltpu.make_async_copy(source, out.at[f, :, pl.ds(half * 128, 128)], sent.at[2 * f + half]))
    for copy in copies:
        copy.start()
    for copy in copies:
        copy.wait()


VMEM = pl.BlockSpec(memory_space=pltpu.VMEM)
ANY = pl.BlockSpec(memory_space=pl.ANY)
PARAMS = pltpu.CompilerParams(vmem_limit_bytes=48 * 1024 * 1024)


def shaped(*shape):
    return jax.ShapeDtypeStruct(shape, F32)


def scratch(*shape):
    return pltpu.VMEM(shape, F32)


def state_shapes():
    return [(STATE, TILES[level] // 2 + 2, 8, LANES[level]) for level in range(4)]


def side_strips(observed, classes):
    return pl.pallas_call(
        sides_kernel,
        out_shape=[shaped(3, 256, 256), shaped(3, 64, 256), shaped(3, 64, 256), shaped(3, 128, 128), shaped(3, 128, 128)],
        in_specs=[VMEM] * 2,
        out_specs=[VMEM] * 5,
        compiler_params=PARAMS,
        name="sides",
    )(observed, classes)


def corner_strips(row_a, row_b):
    return pl.pallas_call(
        corners_kernel,
        out_shape=[shaped(3, 64, 128)] * 2,
        in_specs=[VMEM] * 2,
        out_specs=[VMEM] * 2,
        compiler_params=PARAMS,
        name="corners",
    )(row_a, row_b)


def down(*args):
    return pl.pallas_call(
        down_kernel,
        out_shape=[shaped(*s) for s in state_shapes()] + [shaped(4, 24, 128), shaped(768, 128)],
        in_specs=[ANY] * 7 + [VMEM],
        out_specs=[ANY] * 4 + [VMEM] * 2,
        scratch_shapes=[scratch(*s) for s in state_shapes()]
        + [
            scratch(4, 26, 8, 384),
            scratch(2, 26, 8, 384),
            scratch(4, 24, 8, 256),
            scratch(4, 24, 8, 384),
            scratch(3, 3, 384, 128),
            scratch(2, 3, 128, 128),
            scratch(2, 3, 64, 128),
            scratch(5, 24, 128),
            pltpu.SemaphoreType.DMA((22,)),
            pltpu.SemaphoreType.DMA((4,)),
        ],
        compiler_params=PARAMS,
        name="down",
    )(*args)


def up(gathered, saved4, saved):
    return pl.pallas_call(
        up_kernel,
        out_shape=shaped(2, 256, 256),
        in_specs=[VMEM] * 2 + [ANY] * 4,
        out_specs=ANY,
        scratch_shapes=[scratch(*s) for s in state_shapes()]
        + [
            scratch(2, 24, 8, 256),
            scratch(2, 26, 8, 384),
            scratch(2, 26, 8, 384),
            scratch(5, 16, 8, 128),
            scratch(2, 16, 8, 128),
            scratch(2, 16, 8, 128),
            scratch(2, 16, 8, 128),
            scratch(2, 16, 8, 128),
            scratch(2, 2, 384, 128),
            scratch(24, 128),
            pltpu.SemaphoreType.DMA((4,)),
            pltpu.SemaphoreType.DMA((4,)),
        ],
        compiler_params=PARAMS,
        name="up",
    )(gathered, saved4, *saved)


def make_tables(class_weight, class_stiffness):
    pad = lambda x, first: jnp.pad(jnp.concatenate([jnp.full((1,), first, F32), x]), (0, 119))
    return jnp.stack([pad(0.5 * class_stiffness, FAR), pad(class_weight, 0.0)])


def swap(x, axis, first):
    pairs = [(i, i + 1) for i in range(first, lax.axis_size(axis) - 1, 2)]
    return lax.ppermute(x, axis, pairs + [(j, i) for i, j in pairs])


def local(observed, coherence_class, class_weight, class_stiffness):
    own, row_a, row_b, col_a, col_b = side_strips(observed, (coherence_class + 1).astype(F32))
    row_a, row_b = swap(row_a, "row", 0), swap(row_b, "row", 1)
    col_a, col_b = swap(col_a, "col", 0), swap(col_b, "col", 1)
    corner_a, corner_b = corner_strips(row_a, row_b)
    corner_a, corner_b = swap(corner_a, "col", 0), swap(corner_b, "col", 1)
    tables = make_tables(class_weight, class_stiffness)
    *saved, saved4, message = down(own, row_a, row_b, col_a, col_b, corner_a, corner_b, tables)
    gathered = lax.all_to_all(message.reshape(256, 1, 384), ("row", "col"), 0, 0).reshape(768, 128)
    return up(gathered, saved4, saved)


def solution(mesh):
    in_specs = (P(None, "row", "col"), P("row", "col"), P(), P())
    out_specs = P(None, "row", "col")
    return jax.shard_map(local, mesh=mesh, in_specs=in_specs, out_specs=out_specs, check_vma=False)
```

```python
import jax
import jax.numpy as jnp
from jax import lax
from jax.experimental import pallas as pl
from jax.experimental.pallas import tpu as pltpu
from jax.sharding import PartitionSpec as P

CG_ITERS = 12
FAR = -1.0e4
TILES = (48, 24, 12, 6, 3)
LANES = (384, 256, 128, 128, 128)
F32 = jnp.float32
BF16 = jnp.bfloat16
BLACK, EDGE, INV, STATE = 4, 6, 11, 13


def iota(shape, axis):
    return lax.broadcasted_iota(jnp.int32, shape, axis)


def roll(x, shift, axis):
    return pltpu.roll(x, shift % x.shape[axis], axis)


def dot(a, b):
    return jnp.dot(a, b, preferred_element_type=F32)


def split(x):
    high = x.astype(BF16)
    return high, (x - high.astype(F32)).astype(BF16)


def times(x, pattern):
    high, low = split(x)
    return dot(high, pattern) + dot(low, pattern)


def pick(pattern, x):
    high, low = split(x)
    return dot(pattern, high) + dot(pattern, low)


def onehot(condition):
    return jnp.where(condition, 1.0, 0.0).astype(BF16)


def even_lanes(shape):
    return iota(shape, len(shape) - 1) % 2 == 0


def signed_lane(level, lane):
    width = LANES[level]
    own = 256 >> level
    return jnp.where(lane < (own + width) // 2, lane, lane - width)


def coarse_lane(level, lane):
    c = signed_lane(level, lane) >> 1
    return jnp.where(c < 0, c + LANES[level + 1], c)


def side_lane(field, lane3):
    c = (signed_lane(3, lane3) >> 1) + 64 * field
    return jnp.where(c < 0, c + 128, c)


def ends(ref, index, count):
    ref[index, 0] = roll(ref[index, count], 1, 0)
    ref[index, count + 1] = roll(ref[index, 1], -1, 0)


def loop(count, body, unroll):
    if count <= unroll:
        for i in range(count):
            body(i)
        return

    def step(i, carry):
        for j in range(unroll):
            body(i * unroll + j)
        return carry

    lax.fori_loop(0, count // unroll, step, 0)


def pull_red(a, black, f, state, even):
    b = black[f, a + 1]
    total = state[EDGE, a + 1] * b + state[EDGE + 1, a + 1] * jnp.where(even, black[f, a], black[f, a + 2])
    return total + state[EDGE + 3, a + 1] * roll(b, -1, 1) + roll(state[EDGE + 4, a + 1] * b, 1, 1)


def pull_black(a, red, f, state, even):
    r = red[f, a + 1]
    total = state[EDGE, a + 1] * r + state[EDGE + 2, a + 1] * jnp.where(even, red[f, a + 2], red[f, a])
    return total + state[EDGE + 4, a + 1] * roll(r, -1, 1) + roll(state[EDGE + 3, a + 1] * r, 1, 1)


def lookup(table, index):
    parts = []
    for c in range(index.shape[1] // 128):
        parts.append(jnp.take_along_axis(table, index[:, c * 128 : (c + 1) * 128], axis=1))
    return jnp.concatenate(parts, axis=1)


def edges4(g, w):
    k = [jnp.maximum(g + roll(g, s, x), 0.0) for s, x in ((1, 0), (-1, 0), (1, 1), (-1, 1))]
    return k, 1.0 / jnp.maximum(w + k[0] + k[1] + k[2] + k[3], 1e-20)


def pull4(k, v):
    return k[0] * roll(v, 1, 0) + k[1] * roll(v, -1, 0) + k[2] * roll(v, 1, 1) + k[3] * roll(v, -1, 1)


def red4():
    return (iota((24, 128), 0) + iota((24, 128), 1)) % 2 == 0


def place():
    return lax.axis_index("row"), lax.axis_index("col")


def fold(x, low, swap):
    half = x.shape[0] // 2
    first, second = x[:half], x[half:]
    if swap:
        return jnp.where(low, roll(second, 64, 1), first)
    return jnp.where(low, first, roll(second, 64, 1))


def sides_kernel(observed, classes, own, row_a, row_b, col_a, col_b):
    row, col = place()
    own[0:2] = observed[...]
    own[2] = classes[...]
    low = iota((128, 128), 1) < 64
    for f in range(3):
        x = own.at[f]
        top, bottom = x[0:64, :], x[192:256, :]
        row_a[f] = jnp.where(row % 2 == 0, bottom, top)
        row_b[f] = jnp.where(row % 2 == 0, top, bottom)
        left, right = fold(x[:, 0:128], low, False), fold(x[:, 128:256], low, True)
        col_a[f] = jnp.where(col % 2 == 0, right, left)
        col_b[f] = jnp.where(col % 2 == 0, left, right)


def corners_kernel(row_a, row_b, out_a, out_b):
    row, col = place()
    low = iota((64, 128), 1) < 64
    for f in range(3):
        a, b = row_a[f], row_b[f]
        south, north = jnp.where(row % 2 == 0, a, b), jnp.where(row % 2 == 0, b, a)
        x = jnp.concatenate([south, north], axis=0)
        left, right = fold(x[:, 0:128], low, False), fold(x[:, 128:256], low, True)
        out_a[f] = jnp.where(col % 2 == 0, right, left)
        out_b[f] = jnp.where(col % 2 == 0, left, right)


def message_row(x, pattern, mine):
    return jnp.sum(jnp.where(mine, times(x, pattern), 0.0), axis=0, keepdims=True)


def class_tables(table):
    lane = iota((8, 128), 1)
    g, w = jnp.full((8, 128), FAR, F32), jnp.zeros((8, 128), F32)
    for i in range(8):
        g = jnp.where(lane == i + 1, 0.5 * table[8 + i], g)
        w = jnp.where(lane == i + 1, table[i], w)
    return g, w


def interleave(x, y, even):
    return jnp.where(even, x, y), jnp.where(even, y, x)


def middle_kernel(own, row_a, row_b, table, rhs, gw, frame):
    row, _ = place()
    for f in range(3):
        for half in range(2):
            lanes = slice(half * 128, half * 128 + 128)
            x, y = row_a[f, :, lanes], row_b[f, :, lanes]
            frame[f, half, 0:256, :] = own[f, :, lanes]
            frame[f, half, 256:320, :] = jnp.where(row % 2 == 0, x, y)
            frame[f, half, 320:384, :] = jnp.where(row % 2 == 0, y, x)
    tables = class_tables(table)
    even = even_lanes((8, 256))

    def tile(f, a):
        return jnp.concatenate([frame[f, c, pl.ds(a, 8, stride=48), :] for c in range(2)], axis=1)

    def pack(a):
        for f in range(2):
            rhs[f, a], rhs[2 + f, a] = interleave(tile(f, 2 * a), tile(f, 2 * a + 1), even)
        i, j = (tile(2, 2 * a + k).astype(jnp.int32) for k in range(2))
        for q in range(2):
            gw[2 * q, a], gw[2 * q + 1, a] = interleave(lookup(tables[q], i), lookup(tables[q], j), even)

    loop(24, pack, 12)


def down_kernel(rhs0, gw0, col_a, col_b, corner_a, corner_b, table, *rest):
    states = rest[:4]
    saved4, message = rest[4:6]
    gw, red, full, sums, frame, nat = rest[6:]
    row, col = place()
    even_col = col % 2 == 0

    for a, b, start, size in ((col_a, col_b, 0, 128), (corner_a, corner_b, 256, 64)):
        low = iota((size, 128), 1) < 64
        for f in range(3):
            x, y = a[f], b[f]
            e, w = jnp.where(even_col, x, y), jnp.where(even_col, y, x)
            frame[f, start : start + size, :] = jnp.where(low, e, w)
            frame[f, start + size : start + 2 * size, :] = roll(jnp.where(low, w, e), 64, 1)
    tables = class_tables(table)
    narrow = even_lanes((8, 128))

    def side_tile(f, a):
        return frame[f, pl.ds(a, 8, stride=48), :]

    for level in range(4):
        count, width = TILES[level] // 2, LANES[level]
        even = even_lanes((8, width))
        state = states[level]
        unroll = (24, 12, 6, 3)[level]
        here = pl.ds(0, width)

        def pack(a, level=level, even=even, state=state, here=here):
            if level == 0:
                for f in range(2):
                    x = interleave(side_tile(f, 2 * a), side_tile(f, 2 * a + 1), narrow)
                    for k in range(2):
                        state[2 * k + f, a + 1] = jnp.concatenate([rhs0[2 * k + f, a], x[k]], axis=1)
                i, j = (side_tile(2, 2 * a + k).astype(jnp.int32) for k in range(2))
                for q in range(2):
                    x = interleave(lookup(tables[q], i), lookup(tables[q], j), narrow)
                    for k in range(2):
                        gw[2 * q + k, a + 1] = jnp.concatenate([gw0[2 * q + k, a], x[k]], axis=1)
            else:
                for f in range(2):
                    x = interleave(full[f, 2 * a, :, here], full[f, 2 * a + 1, :, here], even)
                    state[f, a + 1], state[2 + f, a + 1] = x
                for q in range(2):
                    x = interleave(full[2 + q, 2 * a, :, here], full[2 + q, 2 * a + 1, :, here], even)
                    gw[2 * q, a + 1, :, here], gw[2 * q + 1, a + 1, :, here] = x

        loop(count, pack, unroll)
        for q in range(2):
            gw[q, 0, :, here] = roll(gw[q, count, :, here], 1, 0)
            gw[q, count + 1, :, here] = roll(gw[q, 1, :, here], -1, 0)

        def edges(a, even=even, state=state, here=here):
            r, b = gw[0, a + 1, :, here], gw[1, a + 1, :, here]
            same = jnp.maximum(r + b, 0.0)
            r_other = jnp.maximum(r + jnp.where(even, gw[1, a, :, here], gw[1, a + 2, :, here]), 0.0)
            b_other = jnp.maximum(b + jnp.where(even, gw[0, a + 2, :, here], gw[0, a, :, here]), 0.0)
            r_east = jnp.maximum(r + roll(b, -1, 1), 0.0)
            b_east = jnp.maximum(b + roll(r, -1, 1), 0.0)
            r_inv = 1.0 / jnp.maximum(gw[2, a + 1, :, here] + same + r_other + r_east + roll(b_east, 1, 1), 1e-20)
            b_inv = 1.0 / jnp.maximum(gw[3, a + 1, :, here] + same + b_other + b_east + roll(r_east, 1, 1), 1e-20)
            for i, x in enumerate((same, r_other, b_other, r_east, b_east, r_inv, b_inv)):
                state[EDGE + i, a + 1] = x
            for f in range(2):
                red[f, a + 1, :, here] = state[f, a + 1] * r_inv
            sums[2, a, :, here] = 0.5 * (r + b)
            sums[3, a, :, here] = gw[2, a + 1, :, here] + gw[3, a + 1, :, here]

        loop(count, edges, unroll)
        for f in range(2):
            red[f, 0, :, here] = roll(red[f, count, :, here], 1, 0)
            red[f, count + 1, :, here] = roll(red[f, 1, :, here], -1, 0)

        def first_black(a, even=even, state=state, here=here):
            view = red.at[:, :, :, here]
            for f in range(2):
                state[BLACK + f, a + 1] = (state[2 + f, a + 1] + pull_black(a, view, f, state, even)) * state[INV + 1, a + 1]

        loop(count, first_black, unroll)
        for f in range(2):
            ends(state, BLACK + f, count)

        def restrict(a, even=even, state=state, here=here):
            for f in range(2):
                sums[f, a, :, here] = pull_red(a, state.at[BLACK : BLACK + 2], f, state, even)

        loop(count, restrict, unroll)
        fine = iota((width, LANES[level + 1]), 0)
        lane = iota((width, LANES[level + 1]), 1)
        if level < 3:
            pattern = onehot(coarse_lane(level, fine) == lane)
            for q in range(4):
                x = sums[q, 0:count, :, here].reshape(count * 8, width)
                full[q, 0:count, :, pl.ds(0, LANES[level + 1])] = times(x, pattern).reshape(count, 8, LANES[level + 1])
        else:
            first, second = (onehot(side_lane(f, fine) == lane) for f in range(2))
            x = [sums[q, 0:3, :, here].reshape(24, 128) for q in range(4)]
            results = [times(x[0], first) + times(x[1], second)] + [times(x[q], first + second) for q in (2, 3)]
            for q in range(3):
                for a in range(3):
                    nat[q, pl.ds(a, 8, stride=3), :] = results[q][a * 8 : a * 8 + 8]

    rhs, g, w = nat[0], nat[1], nat[2]
    is_red = red4()
    k, inv = edges4(g, w)
    v = jnp.where(is_red, rhs * inv, 0.0)
    v = jnp.where(is_red, v, (rhs + pull4(k, v)) * inv)
    merged = jnp.where(is_red, rhs, v)
    saved4[0] = merged
    saved4[1] = rhs
    saved4[2] = g
    saved4[3] = w
    nat[3] = jnp.where(is_red, pull4(k, v), 0.0)
    nat[4] = jnp.where(iota((24, 128), 1) < 64, 0.5 * g, w)

    lane = iota((128, 128), 0)
    l = iota((128, 128), 1)
    sub, at = iota((8, 128), 0), iota((8, 128), 1)
    pattern = onehot(jnp.logical_and(lane // 64 == l // 64, (lane % 64) // 2 == l % 8))
    mine = sub == (at // 8) % 8
    common = []
    for q in (3, 4):
        x = nat[q, pl.ds(0, 8, stride=2), :] + nat[q, pl.ds(1, 8, stride=2), :]
        common.append(message_row(x, pattern, mine))
    pattern = onehot(jnp.logical_and(lane // 64 == l // 64, lane % 64 == l % 16))
    top = message_row(merged[0:8], pattern, sub == (at // 16) % 4)
    bottom = message_row(merged[8:16], pattern, sub == (at // 16) % 4 + 4)
    mine = iota((16, 128), 0) == (iota((16, 128), 1) // 4) % 16
    pattern = onehot(jnp.logical_and(lane // 64 == l // 64, lane % 64 == l % 4))
    left = message_row(merged[0:16], pattern, mine)
    pattern = onehot(jnp.logical_and(lane // 64 == l // 64, lane % 64 == l % 4 + 12))
    right = message_row(merged[0:16], pattern, mine)

    block = jnp.concatenate((common + [jnp.zeros((1, 128), F32)]) * 8, axis=0)

    def send(i, carry):
        message[pl.ds(pl.multiple_of(i * 24, 8), 24), :] = block
        return carry

    lax.fori_loop(0, 32, send, 0)
    for dr, dc, what in NEIGHBOURS:
        x = {-1: top, 1: bottom}.get(dr, left if dc < 0 else right)
        r, c = row + dr, col + dc

        @pl.when(jnp.logical_and(jnp.logical_and(r >= 0, r < 16), jnp.logical_and(c >= 0, c < 16)))
        def _(r=r, c=c, x=x):
            message[pl.ds((r * 16 + c) * 3 + 2, 1), :] = x


NEIGHBOURS = [(dr, dc, None) for dr in (-1, 0, 1) for dc in (-1, 0, 1) if dr or dc]


def cg(gathered, kc, e, d, s, w, r):
    lane = iota((8, 128), 1)
    sub = iota((8, 128), 0)
    group = lane // 8
    arrays = [[None] * 16 for _ in range(4)]
    for hi in range(2):
        for pair in range(2):
            v = [gathered[pl.ds((hi * 128 + c) * 3 + pair, 8, stride=48), :] for c in range(16)]
            for k in (1, 2, 4, 8):
                low = (group // k) % 2 == 0
                for c in range(16):
                    if not c & k:
                        x, y = v[c], v[c | k]
                        v[c] = jnp.where(low, x, roll(y, 8 * k, 1))
                        v[c | k] = jnp.where(low, roll(x, -8 * k, 1), y)
            for i in range(16):
                arrays[2 * pair + i // 8][hi * 8 + i % 8] = v[i]

    def north(tile, t):
        if t % 8:
            return tile(t - 1)
        turned = roll(tile(t + 7), 1, 0)
        return turned if t == 0 else jnp.where(sub == 0, roll(tile(7), 1, 0), turned)

    def south(tile, t):
        if t % 8 != 7:
            return tile(t + 1)
        turned = roll(tile(t - 7), -1, 0)
        return turned if t == 15 else jnp.where(sub == 7, roll(tile(8), -1, 0), turned)

    g = arrays[2]
    for t in range(16):
        up = jnp.maximum(g[t] + north(lambda i: g[i], t), 0.0)
        down = jnp.maximum(g[t] + south(lambda i: g[i], t), 0.0)
        if t == 0:
            up = jnp.where(sub == 0, 0.0, up)
        if t == 15:
            down = jnp.where(sub == 7, 0.0, down)
        left = jnp.where(lane == 0, 0.0, jnp.maximum(g[t] + roll(g[t], 1, 1), 0.0))
        right = jnp.where(lane == 127, 0.0, jnp.maximum(g[t] + roll(g[t], -1, 1), 0.0))
        kc[0, t] = up
        kc[1, t] = down
        kc[2, t] = left
        kc[3, t] = right
        kc[4, t] = arrays[3][t] + up + down + left + right

    def sums(f):
        x = [r[f, t] for t in range(16)]
        tile = lambda i: x[i]
        total, norm = 0.0, 0.0
        for t in range(16):
            image = kc[4, t] * x[t] - (
                kc[0, t] * north(tile, t)
                + kc[1, t] * south(tile, t)
                + kc[2, t] * roll(x[t], 1, 1)
                + kc[3, t] * roll(x[t], -1, 1)
            )
            w[f, t] = image
            norm += x[t] * x[t]
            total += x[t] * image
        return tuple(jnp.sum(y, axis=(0, 1), keepdims=True) for y in (norm, total))

    state = []
    for f in range(2):
        for t in range(16):
            x = arrays[f][t]
            e[f, t] = jnp.zeros_like(x)
            d[f, t] = jnp.zeros_like(x)
            s[f, t] = jnp.zeros_like(x)
            r[f, t] = x
    for f in range(2):
        norm, total = sums(f)
        state.append((norm, norm / total, jnp.zeros_like(norm)))

    def iterate(_, state):
        for f in range(2):
            norm, alpha, beta = state[f]
            for t in range(16):
                x = r[f, t] + beta * d[f, t]
                y = w[f, t] + beta * s[f, t]
                d[f, t] = x
                s[f, t] = y
                e[f, t] = e[f, t] + alpha * x
                r[f, t] = r[f, t] - alpha * y
        result = []
        fresh = [sums(f) for f in range(2)]
        for f in range(2):
            norm, alpha, _ = state[f]
            beta = fresh[f][0] / norm
            result.append((fresh[f][0], fresh[f][0] / (fresh[f][1] - beta * fresh[f][0] / alpha), beta))
        return tuple(result)

    state = lax.fori_loop(0, CG_ITERS - 1, iterate, tuple(state))
    for f in range(2):
        _, alpha, beta = state[f]
        for t in range(16):
            e[f, t] = e[f, t] + alpha * (r[f, t] + beta * d[f, t])


def merged_frame(gathered, merged):
    row, col = place()
    at = iota((24, 128), 0)
    l = iota((24, 128), 1)
    total = {}
    for dr, dc, _ in NEIGHBOURS:
        r, c = row + dr, col + dc
        there = jnp.logical_and(jnp.logical_and(r >= 0, r < 16), jnp.logical_and(c >= 0, c < 16))
        index = jnp.where(there, (r * 16 + c) * 3 + 2, 0)
        x = gathered[pl.ds(index, 1), :] * jnp.where(there, 1.0, 0.0)
        if dr:
            mine = at == (20 if dr < 0 else 16) + (l // 16) % 4
        else:
            mine = at == (l // 4) % 16
        key = dc if dr else 2 * dc
        total[key] = total.get(key, 0.0) + jnp.where(mine, jnp.broadcast_to(x, (24, 128)), 0.0)
    l = iota((128, 128), 0)
    lane = iota((128, 128), 1)
    base = (l // 64) * 64
    j, c = l % 16, l % 4
    patterns = {
        0: lane == base + j,
        -1: jnp.logical_and(j >= 12, lane == (base + j - 16) % 128),
        1: jnp.logical_and(j < 4, lane == base + 16 + j),
        -2: lane == (base + c - 4) % 128,
        2: lane == base + 16 + c,
    }
    own = jnp.logical_and(at < 16, iota((24, 128), 1) % 64 < 16)
    result = jnp.where(own, merged, 0.0)
    for key, x in total.items():
        result += times(x, onehot(patterns[key]))
    return result


def up_kernel(gathered, saved4, *rest):
    states, out = rest[:4], rest[4]
    full, red, blk, kc, e, d, s, w, r, result, nat, sent = rest[5:]
    cg(gathered, kc, e, d, s, w, r)

    row, col = place()
    n = iota((24, 128), 1)
    at = iota((24, 128), 0)
    grid_row = (n // 64) * 64 + (n % 8) * 8 + (n // 8) % 8
    rows = onehot(grid_row == row * 8 + (jnp.where(at < 20, at, at - 24) >> 1))
    j = iota((128, 128), 0)
    lane = iota((128, 128), 1)
    correction = 0.0
    for f in range(2):
        c = (lane + 32) % 128 - 32 - 64 * f
        cols = onehot(jnp.logical_and(jnp.logical_and(c >= -32, c < 32), j == col * 8 + (c >> 1)))
        whole = jnp.concatenate([e[f, t] for t in range(16)], axis=0)
        correction += times(pick(rows, whole), cols)

    is_red = red4()
    merged = merged_frame(gathered, saved4[0])
    k, inv = edges4(saved4[2], saved4[3])
    x = jnp.where(is_red, 0.0, merged + correction)
    x = jnp.where(is_red, (merged + pull4(k, x)) * inv, 0.0)
    nat[...] = jnp.where(is_red, x, (saved4[1] + pull4(k, x)) * inv)
    ordered = jnp.concatenate([nat[pl.ds(a, 8, stride=3), :] for a in range(3)], axis=0)

    for level in range(3, -1, -1):
        count, width = TILES[level] // 2, LANES[level]
        even = even_lanes((8, width))
        state = states[level]
        unroll = (24, 12, 6, 3)[level]
        here = pl.ds(0, width)
        if level == 3:
            lane, wide = iota((128, 128), 0), iota((128, 128), 1)
            corrections = [times(ordered, onehot(side_lane(f, wide) == lane)) for f in range(2)]
        else:
            coarse = LANES[level + 1]
            lane, wide = iota((coarse, width), 0), iota((coarse, width), 1)
            pattern = onehot(coarse_lane(level, wide) == lane)
            corrections = [
                times(full[f, 0:count, :, pl.ds(0, coarse)].reshape(count * 8, coarse), pattern) for f in range(2)
            ]
        for f in range(2):
            blk[f, 1 : count + 1, :, here] = state[BLACK + f, 1 : count + 1] + corrections[f].reshape(count, 8, width)
            blk[f, 0, :, here] = roll(blk[f, count, :, here], 1, 0)
            blk[f, count + 1, :, here] = roll(blk[f, 1, :, here], -1, 0)

        def second_red(a, even=even, state=state, here=here):
            view = blk.at[:, :, :, here]
            for f in range(2):
                red[f, a + 1, :, here] = (state[f, a + 1] + pull_red(a, view, f, state, even)) * state[INV, a + 1]

        loop(count, second_red, unroll)
        for f in range(2):
            red[f, 0, :, here] = roll(red[f, count, :, here], 1, 0)
            red[f, count + 1, :, here] = roll(red[f, 1, :, here], -1, 0)

        def second_black(a, fields=(0, 1), level=level, even=even, state=state, here=here):
            view = red.at[:, :, :, here]
            for f in fields:
                x = red[f, a + 1, :, here]
                y = (state[2 + f, a + 1] + pull_black(a, view, f, state, even)) * state[INV + 1, a + 1]
                first, second = jnp.where(even, x, y), jnp.where(even, y, x)
                if level:
                    full[f, 2 * a, :, here] = first
                    full[f, 2 * a + 1, :, here] = second
                else:
                    for half in range(2):
                        lanes = slice(128 * half, 128 + 128 * half)
                        result[f, half, pl.ds(2 * a, 8, stride=48), :] = first[:, lanes]
                        result[f, half, pl.ds(2 * a + 1, 8, stride=48), :] = second[:, lanes]

        if level:
            loop(count, second_black, unroll)

    copies = []
    for f in range(2):
        loop(24, lambda a, f=f: second_black(a, (f,)), 24)
        for half in range(2):
            source = result.at[f, half, pl.ds(0, 256), :]
            copies.append(pltpu.make_async_copy(source, out.at[f, :, pl.ds(half * 128, 128)], sent.at[2 * f + half]))
            copies[-1].start()
    for copy in copies:
        copy.wait()


VMEM = pl.BlockSpec(memory_space=pltpu.VMEM)
ANY = pl.BlockSpec(memory_space=pl.ANY)
SMEM = pl.BlockSpec(memory_space=pltpu.SMEM)
PARAMS = pltpu.CompilerParams(vmem_limit_bytes=24 * 1024 * 1024)


def shaped(*shape):
    return jax.ShapeDtypeStruct(shape, F32)


def scratch(*shape):
    return pltpu.VMEM(shape, F32)


def state_shapes():
    return [(STATE, TILES[level] // 2 + 2, 8, LANES[level]) for level in range(4)]


def side_strips(observed, classes):
    return pl.pallas_call(
        sides_kernel,
        out_shape=[shaped(3, 256, 256), shaped(3, 64, 256), shaped(3, 64, 256), shaped(3, 128, 128), shaped(3, 128, 128)],
        in_specs=[VMEM] * 2,
        out_specs=[VMEM] * 5,
        compiler_params=PARAMS,
        name="sides",
    )(observed, classes)


def corner_strips(row_a, row_b):
    return pl.pallas_call(
        corners_kernel,
        out_shape=[shaped(3, 64, 128)] * 2,
        in_specs=[VMEM] * 2,
        out_specs=[VMEM] * 2,
        compiler_params=PARAMS,
        name="corners",
    )(row_a, row_b)


def middle(own, row_a, row_b, table):
    return pl.pallas_call(
        middle_kernel,
        out_shape=[shaped(4, 24, 8, 256)] * 2,
        in_specs=[VMEM] * 3 + [SMEM],
        out_specs=[VMEM] * 2,
        scratch_shapes=[scratch(3, 2, 384, 128)],
        compiler_params=PARAMS,
        name="middle",
    )(own, row_a, row_b, table)


def down(*args):
    return pl.pallas_call(
        down_kernel,
        out_shape=[shaped(*s) for s in state_shapes()] + [shaped(4, 24, 128), shaped(768, 128)],
        in_specs=[VMEM] * 6 + [SMEM],
        out_specs=[VMEM] * 6,
        scratch_shapes=[
            scratch(4, 26, 8, 384),
            scratch(2, 26, 8, 384),
            scratch(4, 24, 8, 256),
            scratch(4, 24, 8, 384),
            scratch(3, 384, 128),
            scratch(5, 24, 128),
        ],
        compiler_params=PARAMS,
        name="down",
    )(*args)


def up(gathered, saved4, saved):
    return pl.pallas_call(
        up_kernel,
        out_shape=shaped(2, 256, 256),
        in_specs=[VMEM] * 6,
        out_specs=ANY,
        scratch_shapes=[
            scratch(2, 24, 8, 256),
            scratch(2, 26, 8, 384),
            scratch(2, 26, 8, 384),
            scratch(5, 16, 8, 128),
            scratch(2, 16, 8, 128),
            scratch(2, 16, 8, 128),
            scratch(2, 16, 8, 128),
            scratch(2, 16, 8, 128),
            scratch(2, 16, 8, 128),
            scratch(2, 2, 384, 128),
            scratch(24, 128),
            pltpu.SemaphoreType.DMA((4,)),
        ],
        compiler_params=PARAMS,
        name="up",
    )(gathered, saved4, *saved)


def swap(x, axis, first):
    pairs = [(i, i + 1) for i in range(first, lax.axis_size(axis) - 1, 2)]
    return lax.ppermute(x, axis, pairs + [(j, i) for i, j in pairs])


def local(observed, coherence_class, class_weight, class_stiffness):
    own, row_a, row_b, col_a, col_b = side_strips(observed, (coherence_class + 1).astype(F32))
    row_a, row_b = swap(row_a, "row", 0), swap(row_b, "row", 1)
    col_a, col_b = swap(col_a, "col", 0), swap(col_b, "col", 1)
    corner_a, corner_b = corner_strips(row_a, row_b)
    held = lax.optimization_barrier((corner_a, corner_b, own, row_a, row_b, class_weight, class_stiffness))
    corner_a, corner_b, own, row_a, row_b, class_weight, class_stiffness = held
    corner_a, corner_b = swap(corner_a, "col", 0), swap(corner_b, "col", 1)
    table = jnp.concatenate([class_weight, class_stiffness])
    rhs, gw = middle(own, row_a, row_b, table)
    results = down(rhs, gw, col_a, col_b, corner_a, corner_b, table)
    *saved, saved4, message = results
    gathered = lax.all_to_all(message.reshape(256, 1, 384), ("row", "col"), 0, 0).reshape(768, 128)
    return up(gathered, saved4, saved)


def solution(mesh):
    in_specs = (P(None, "row", "col"), P("row", "col"), P(), P())
    out_specs = P(None, "row", "col")
    return jax.shard_map(local, mesh=mesh, in_specs=in_specs, out_specs=out_specs, check_vma=False)
```

```python
import jax
import jax.numpy as jnp
from jax import lax
from jax.experimental import pallas as pl
from jax.experimental.pallas import tpu as pltpu
from jax.sharding import Mesh
from jax.sharding import PartitionSpec as P

CG_ITERS = 12
FAR = -1.0e4
TILES = (48, 24, 12, 6, 3)
LANES = (384, 256, 128, 128, 128)
F32 = jnp.float32
ROW = ("z", "core")
BF16 = jnp.bfloat16
BLACK, EDGE, INV, STATE = 4, 6, 11, 13


def iota(shape, axis):
    return lax.broadcasted_iota(jnp.int32, shape, axis)


def roll(x, shift, axis):
    return pltpu.roll(x, shift % x.shape[axis], axis)


def dot(a, b):
    return jnp.dot(a, b, preferred_element_type=F32)


def split(x):
    high = x.astype(BF16)
    return high, (x - high.astype(F32)).astype(BF16)


def times(x, pattern):
    high, low = split(x)
    return dot(high, pattern) + dot(low, pattern)


def pick(pattern, x):
    high, low = split(x)
    return dot(pattern, high) + dot(pattern, low)


def onehot(condition):
    return jnp.where(condition, 1.0, 0.0).astype(BF16)


def even_lanes(shape):
    return iota(shape, len(shape) - 1) % 2 == 0


def signed_lane(level, lane):
    width = LANES[level]
    own = 256 >> level
    return jnp.where(lane < (own + width) // 2, lane, lane - width)


def coarse_lane(level, lane):
    c = signed_lane(level, lane) >> 1
    return jnp.where(c < 0, c + LANES[level + 1], c)


def side_lane(field, lane3):
    c = (signed_lane(3, lane3) >> 1) + 64 * field
    return jnp.where(c < 0, c + 128, c)


def ends(ref, index, count):
    ref[index, 0] = roll(ref[index, count], 1, 0)
    ref[index, count + 1] = roll(ref[index, 1], -1, 0)


def loop(count, body, unroll):
    if count <= unroll:
        for i in range(count):
            body(i)
        return

    def step(i, carry):
        for j in range(unroll):
            body(i * unroll + j)
        return carry

    lax.fori_loop(0, count // unroll, step, 0)


def pull_red(a, black, f, state, even):
    b = black[f, a + 1]
    total = state[EDGE, a + 1] * b + state[EDGE + 1, a + 1] * jnp.where(even, black[f, a], black[f, a + 2])
    return total + state[EDGE + 3, a + 1] * roll(b, -1, 1) + roll(state[EDGE + 4, a + 1] * b, 1, 1)


def pull_black(a, red, f, state, even):
    r = red[f, a + 1]
    total = state[EDGE, a + 1] * r + state[EDGE + 2, a + 1] * jnp.where(even, red[f, a + 2], red[f, a])
    return total + state[EDGE + 4, a + 1] * roll(r, -1, 1) + roll(state[EDGE + 3, a + 1] * r, 1, 1)


def lookup(table, index):
    parts = []
    for c in range(index.shape[1] // 128):
        parts.append(jnp.take_along_axis(table, index[:, c * 128 : (c + 1) * 128], axis=1))
    return jnp.concatenate(parts, axis=1)


def edges4(g, w):
    k = [jnp.maximum(g + roll(g, s, x), 0.0) for s, x in ((1, 0), (-1, 0), (1, 1), (-1, 1))]
    return k, 1.0 / jnp.maximum(w + k[0] + k[1] + k[2] + k[3], 1e-20)


def pull4(k, v):
    return k[0] * roll(v, 1, 0) + k[1] * roll(v, -1, 0) + k[2] * roll(v, 1, 1) + k[3] * roll(v, -1, 1)


def red4():
    return (iota((24, 128), 0) + iota((24, 128), 1)) % 2 == 0


def place():
    return 2 * lax.axis_index("z") + lax.axis_index("core"), lax.axis_index("col")


def fold(x, low, swap):
    half = x.shape[0] // 2
    first, second = x[:half], x[half:]
    if swap:
        return jnp.where(low, roll(second, 64, 1), first)
    return jnp.where(low, first, roll(second, 64, 1))


def sides_kernel(observed, classes, own, row_a, row_b, col_a, col_b):
    row, col = place()
    own[0:2] = observed[...]
    own[2] = classes[...]
    low = iota((128, 128), 1) < 64
    for f in range(3):
        x = own.at[f]
        top, bottom = x[0:64, :], x[192:256, :]
        row_a[f] = jnp.where(row % 2 == 0, bottom, top)
        row_b[f] = jnp.where(row % 2 == 0, top, bottom)
        left, right = fold(x[:, 0:128], low, False), fold(x[:, 128:256], low, True)
        col_a[f] = jnp.where(col % 2 == 0, right, left)
        col_b[f] = jnp.where(col % 2 == 0, left, right)


def corners_kernel(row_a, row_b, out_a, out_b):
    row, col = place()
    low = iota((64, 128), 1) < 64
    for f in range(3):
        a, b = row_a[f], row_b[f]
        south, north = jnp.where(row % 2 == 0, a, b), jnp.where(row % 2 == 0, b, a)
        x = jnp.concatenate([south, north], axis=0)
        left, right = fold(x[:, 0:128], low, False), fold(x[:, 128:256], low, True)
        out_a[f] = jnp.where(col % 2 == 0, right, left)
        out_b[f] = jnp.where(col % 2 == 0, left, right)


def message_row(x, pattern, mine):
    return jnp.sum(jnp.where(mine, times(x, pattern), 0.0), axis=0, keepdims=True)


def class_tables(table):
    lane = iota((8, 128), 1)
    g, w = jnp.full((8, 128), FAR, F32), jnp.zeros((8, 128), F32)
    for i in range(8):
        g = jnp.where(lane == i + 1, 0.5 * table[8 + i], g)
        w = jnp.where(lane == i + 1, table[i], w)
    return g, w


def interleave(x, y, even):
    return jnp.where(even, x, y), jnp.where(even, y, x)


def middle_kernel(own, row_a, row_b, table, rhs, gw, frame):
    row, _ = place()
    for f in range(3):
        for half in range(2):
            lanes = slice(half * 128, half * 128 + 128)
            x, y = row_a[f, :, lanes], row_b[f, :, lanes]
            frame[f, half, 0:256, :] = own[f, :, lanes]
            frame[f, half, 256:320, :] = jnp.where(row % 2 == 0, x, y)
            frame[f, half, 320:384, :] = jnp.where(row % 2 == 0, y, x)
    tables = class_tables(table)
    even = even_lanes((8, 256))

    def tile(f, a):
        return jnp.concatenate([frame[f, c, pl.ds(a, 8, stride=48), :] for c in range(2)], axis=1)

    def pack(a):
        for f in range(2):
            rhs[f, a], rhs[2 + f, a] = interleave(tile(f, 2 * a), tile(f, 2 * a + 1), even)
        i, j = (tile(2, 2 * a + k).astype(jnp.int32) for k in range(2))
        for q in range(2):
            gw[2 * q, a], gw[2 * q + 1, a] = interleave(lookup(tables[q], i), lookup(tables[q], j), even)

    loop(24, pack, 12)


def down_kernel(rhs0, gw0, col_a, col_b, corner_a, corner_b, table, *rest):
    states = rest[:4]
    saved4, message = rest[4:6]
    gw, red, full, sums, frame, nat = rest[6:]
    row, col = place()
    even_col = col % 2 == 0

    for a, b, start, size in ((col_a, col_b, 0, 128), (corner_a, corner_b, 256, 64)):
        low = iota((size, 128), 1) < 64
        for f in range(3):
            x, y = a[f], b[f]
            e, w = jnp.where(even_col, x, y), jnp.where(even_col, y, x)
            frame[f, start : start + size, :] = jnp.where(low, e, w)
            frame[f, start + size : start + 2 * size, :] = roll(jnp.where(low, w, e), 64, 1)
    tables = class_tables(table)
    narrow = even_lanes((8, 128))

    def side_tile(f, a):
        return frame[f, pl.ds(a, 8, stride=48), :]

    for level in range(4):
        count, width = TILES[level] // 2, LANES[level]
        even = even_lanes((8, width))
        state = states[level]
        unroll = (24, 12, 6, 3)[level]
        here = pl.ds(0, width)

        def pack(a, level=level, even=even, state=state, here=here):
            if level == 0:
                for f in range(2):
                    x = interleave(side_tile(f, 2 * a), side_tile(f, 2 * a + 1), narrow)
                    for k in range(2):
                        state[2 * k + f, a + 1] = jnp.concatenate([rhs0[2 * k + f, a], x[k]], axis=1)
                i, j = (side_tile(2, 2 * a + k).astype(jnp.int32) for k in range(2))
                for q in range(2):
                    x = interleave(lookup(tables[q], i), lookup(tables[q], j), narrow)
                    for k in range(2):
                        gw[2 * q + k, a + 1] = jnp.concatenate([gw0[2 * q + k, a], x[k]], axis=1)
            else:
                for f in range(2):
                    x = interleave(full[f, 2 * a, :, here], full[f, 2 * a + 1, :, here], even)
                    state[f, a + 1], state[2 + f, a + 1] = x
                for q in range(2):
                    x = interleave(full[2 + q, 2 * a, :, here], full[2 + q, 2 * a + 1, :, here], even)
                    gw[2 * q, a + 1, :, here], gw[2 * q + 1, a + 1, :, here] = x

        loop(count, pack, unroll)
        for q in range(2):
            gw[q, 0, :, here] = roll(gw[q, count, :, here], 1, 0)
            gw[q, count + 1, :, here] = roll(gw[q, 1, :, here], -1, 0)

        def edges(a, even=even, state=state, here=here):
            r, b = gw[0, a + 1, :, here], gw[1, a + 1, :, here]
            same = jnp.maximum(r + b, 0.0)
            r_other = jnp.maximum(r + jnp.where(even, gw[1, a, :, here], gw[1, a + 2, :, here]), 0.0)
            b_other = jnp.maximum(b + jnp.where(even, gw[0, a + 2, :, here], gw[0, a, :, here]), 0.0)
            r_east = jnp.maximum(r + roll(b, -1, 1), 0.0)
            b_east = jnp.maximum(b + roll(r, -1, 1), 0.0)
            r_inv = 1.0 / jnp.maximum(gw[2, a + 1, :, here] + same + r_other + r_east + roll(b_east, 1, 1), 1e-20)
            b_inv = 1.0 / jnp.maximum(gw[3, a + 1, :, here] + same + b_other + b_east + roll(r_east, 1, 1), 1e-20)
            for i, x in enumerate((same, r_other, b_other, r_east, b_east, r_inv, b_inv)):
                state[EDGE + i, a + 1] = x
            for f in range(2):
                red[f, a + 1, :, here] = state[f, a + 1] * r_inv
            sums[2, a, :, here] = 0.5 * (r + b)
            sums[3, a, :, here] = gw[2, a + 1, :, here] + gw[3, a + 1, :, here]

        loop(count, edges, unroll)
        for f in range(2):
            red[f, 0, :, here] = roll(red[f, count, :, here], 1, 0)
            red[f, count + 1, :, here] = roll(red[f, 1, :, here], -1, 0)

        def first_black(a, even=even, state=state, here=here):
            view = red.at[:, :, :, here]
            for f in range(2):
                state[BLACK + f, a + 1] = (state[2 + f, a + 1] + pull_black(a, view, f, state, even)) * state[INV + 1, a + 1]

        loop(count, first_black, unroll)
        for f in range(2):
            ends(state, BLACK + f, count)

        def restrict(a, even=even, state=state, here=here):
            for f in range(2):
                sums[f, a, :, here] = pull_red(a, state.at[BLACK : BLACK + 2], f, state, even)

        loop(count, restrict, unroll)
        fine = iota((width, LANES[level + 1]), 0)
        lane = iota((width, LANES[level + 1]), 1)
        if level < 3:
            pattern = onehot(coarse_lane(level, fine) == lane)
            for q in range(4):
                x = sums[q, 0:count, :, here].reshape(count * 8, width)
                full[q, 0:count, :, pl.ds(0, LANES[level + 1])] = times(x, pattern).reshape(count, 8, LANES[level + 1])
        else:
            first, second = (onehot(side_lane(f, fine) == lane) for f in range(2))
            x = [sums[q, 0:3, :, here].reshape(24, 128) for q in range(4)]
            results = [times(x[0], first) + times(x[1], second)] + [times(x[q], first + second) for q in (2, 3)]
            for q in range(3):
                for a in range(3):
                    nat[q, pl.ds(a, 8, stride=3), :] = results[q][a * 8 : a * 8 + 8]

    rhs, g, w = nat[0], nat[1], nat[2]
    is_red = red4()
    k, inv = edges4(g, w)
    v = jnp.where(is_red, rhs * inv, 0.0)
    v = jnp.where(is_red, v, (rhs + pull4(k, v)) * inv)
    merged = jnp.where(is_red, rhs, v)
    saved4[0] = merged
    saved4[1] = rhs
    saved4[2] = g
    saved4[3] = w
    nat[3] = jnp.where(is_red, pull4(k, v), 0.0)
    nat[4] = jnp.where(iota((24, 128), 1) < 64, 0.5 * g, w)

    lane = iota((128, 128), 0)
    l = iota((128, 128), 1)
    sub, at = iota((8, 128), 0), iota((8, 128), 1)
    pattern = onehot(jnp.logical_and(lane // 64 == l // 64, (lane % 64) // 2 == l % 8))
    mine = sub == (at // 8) % 8
    common = []
    for q in (3, 4):
        x = nat[q, pl.ds(0, 8, stride=2), :] + nat[q, pl.ds(1, 8, stride=2), :]
        common.append(message_row(x, pattern, mine))
    pattern = onehot(jnp.logical_and(lane // 64 == l // 64, lane % 64 == l % 16))
    top = message_row(merged[0:8], pattern, sub == (at // 16) % 4)
    bottom = message_row(merged[8:16], pattern, sub == (at // 16) % 4 + 4)
    mine = iota((16, 128), 0) == (iota((16, 128), 1) // 4) % 16
    pattern = onehot(jnp.logical_and(lane // 64 == l // 64, lane % 64 == l % 4))
    left = message_row(merged[0:16], pattern, mine)
    pattern = onehot(jnp.logical_and(lane // 64 == l // 64, lane % 64 == l % 4 + 12))
    right = message_row(merged[0:16], pattern, mine)

    block = jnp.concatenate((common + [jnp.zeros((2, 128), F32)]) * 8, axis=0)

    def send(i, carry):
        message[pl.ds(pl.multiple_of(i * 32, 32), 32), :] = block
        return carry

    lax.fori_loop(0, 16, send, 0)
    for dr, dc, what in NEIGHBOURS:
        x = {-1: top, 1: bottom}.get(dr, left if dc < 0 else right)
        r, c = row + dr, col + dc

        @pl.when(jnp.logical_and(jnp.logical_and(r >= 0, r < 16), jnp.logical_and(c >= 0, c < 16)))
        def _(r=r, c=c, x=x, dr=dr):
            message[pl.ds(((r >> 1) * 16 + c) * 4 + (3 if dr else 2), 1), :] = x


NEIGHBOURS = [(dr, dc, None) for dr in (-1, 0, 1) for dc in (-1, 0, 1) if dr or dc]


def cg(mine, theirs, mix, kc, e, d, s, w, r):
    lane = iota((8, 128), 1)
    sub = iota((8, 128), 0)
    group = lane // 8
    first_core = place()[0] % 2 == 0
    arrays = [[None] * 16 for _ in range(4)]
    for hi in range(2):
        for pair in range(2):
            v = []
            for c in range(16):
                rows = pl.ds((hi * 64 + c) * 4 + pair, 4, stride=64)
                x, y = mine[rows, :], theirs[rows, :]
                start = ((hi * 2 + pair) * 16 + c) * 8
                mix[pl.ds(start, 4, stride=2), :] = jnp.where(first_core, x, y)
                mix[pl.ds(start + 1, 4, stride=2), :] = jnp.where(first_core, y, x)
            for c in range(16):
                v.append(mix[pl.ds(((hi * 2 + pair) * 16 + c) * 8, 8), :])
            for k in (1, 2, 4, 8):
                low = (group // k) % 2 == 0
                for c in range(16):
                    if not c & k:
                        x, y = v[c], v[c | k]
                        v[c] = jnp.where(low, x, roll(y, 8 * k, 1))
                        v[c | k] = jnp.where(low, roll(x, -8 * k, 1), y)
            for i in range(16):
                arrays[2 * pair + i // 8][hi * 8 + i % 8] = v[i]

    def north(tile, t):
        if t % 8:
            return tile(t - 1)
        turned = roll(tile(t + 7), 1, 0)
        return turned if t == 0 else jnp.where(sub == 0, roll(tile(7), 1, 0), turned)

    def south(tile, t):
        if t % 8 != 7:
            return tile(t + 1)
        turned = roll(tile(t - 7), -1, 0)
        return turned if t == 15 else jnp.where(sub == 7, roll(tile(8), -1, 0), turned)

    g = arrays[2]
    for t in range(16):
        up = jnp.maximum(g[t] + north(lambda i: g[i], t), 0.0)
        down = jnp.maximum(g[t] + south(lambda i: g[i], t), 0.0)
        if t == 0:
            up = jnp.where(sub == 0, 0.0, up)
        if t == 15:
            down = jnp.where(sub == 7, 0.0, down)
        left = jnp.where(lane == 0, 0.0, jnp.maximum(g[t] + roll(g[t], 1, 1), 0.0))
        right = jnp.where(lane == 127, 0.0, jnp.maximum(g[t] + roll(g[t], -1, 1), 0.0))
        kc[0, t] = up
        kc[1, t] = down
        kc[2, t] = left
        kc[3, t] = right
        kc[4, t] = arrays[3][t] + up + down + left + right

    def sums(f):
        x = [r[f, t] for t in range(16)]
        tile = lambda i: x[i]
        total, norm = 0.0, 0.0
        for t in range(16):
            image = kc[4, t] * x[t] - (
                kc[0, t] * north(tile, t)
                + kc[1, t] * south(tile, t)
                + kc[2, t] * roll(x[t], 1, 1)
                + kc[3, t] * roll(x[t], -1, 1)
            )
            w[f, t] = image
            norm += x[t] * x[t]
            total += x[t] * image
        return tuple(jnp.sum(y, axis=(0, 1), keepdims=True) for y in (norm, total))

    state = []
    for f in range(2):
        for t in range(16):
            x = arrays[f][t]
            e[f, t] = jnp.zeros_like(x)
            d[f, t] = jnp.zeros_like(x)
            s[f, t] = jnp.zeros_like(x)
            r[f, t] = x
    for f in range(2):
        norm, total = sums(f)
        state.append((norm, norm / total, jnp.zeros_like(norm)))

    def iterate(_, state):
        for f in range(2):
            norm, alpha, beta = state[f]
            for t in range(16):
                x = r[f, t] + beta * d[f, t]
                y = w[f, t] + beta * s[f, t]
                d[f, t] = x
                s[f, t] = y
                e[f, t] = e[f, t] + alpha * x
                r[f, t] = r[f, t] - alpha * y
        result = []
        fresh = [sums(f) for f in range(2)]
        for f in range(2):
            norm, alpha, _ = state[f]
            beta = fresh[f][0] / norm
            result.append((fresh[f][0], fresh[f][0] / (fresh[f][1] - beta * fresh[f][0] / alpha), beta))
        return tuple(result)

    state = lax.fori_loop(0, CG_ITERS - 1, iterate, tuple(state))
    for f in range(2):
        _, alpha, beta = state[f]
        for t in range(16):
            e[f, t] = e[f, t] + alpha * (r[f, t] + beta * d[f, t])


def merged_frame(mine, theirs, merged):
    row, col = place()
    at = iota((24, 128), 0)
    l = iota((24, 128), 1)
    total = {}
    for dr, dc, _ in NEIGHBOURS:
        r, c = row + dr, col + dc
        there = jnp.logical_and(jnp.logical_and(r >= 0, r < 16), jnp.logical_and(c >= 0, c < 16))
        index = jnp.where(there, ((r >> 1) * 16 + c) * 4 + (3 if dr else 2), 0)
        x = (theirs if dr else mine)[pl.ds(index, 1), :] * jnp.where(there, 1.0, 0.0)
        if dr:
            ours = at == (20 if dr < 0 else 16) + (l // 16) % 4
        else:
            ours = at == (l // 4) % 16
        key = dc if dr else 2 * dc
        total[key] = total.get(key, 0.0) + jnp.where(ours, jnp.broadcast_to(x, (24, 128)), 0.0)
    l = iota((128, 128), 0)
    lane = iota((128, 128), 1)
    base = (l // 64) * 64
    j, c = l % 16, l % 4
    patterns = {
        0: lane == base + j,
        -1: jnp.logical_and(j >= 12, lane == (base + j - 16) % 128),
        1: jnp.logical_and(j < 4, lane == base + 16 + j),
        -2: lane == (base + c - 4) % 128,
        2: lane == base + 16 + c,
    }
    own = jnp.logical_and(at < 16, iota((24, 128), 1) % 64 < 16)
    result = jnp.where(own, merged, 0.0)
    for key, x in total.items():
        result += times(x, onehot(patterns[key]))
    return result


def up_kernel(mine, theirs, saved4, *rest):
    states, out = rest[:4], rest[4]
    full, red, blk, mix, kc, e, d, s, w, r, result, nat, sent = rest[5:]
    cg(mine, theirs, mix, kc, e, d, s, w, r)

    row, col = place()
    n = iota((24, 128), 1)
    at = iota((24, 128), 0)
    grid_row = (n // 64) * 64 + (n % 8) * 8 + (n // 8) % 8
    rows = onehot(grid_row == row * 8 + (jnp.where(at < 20, at, at - 24) >> 1))
    j = iota((128, 128), 0)
    lane = iota((128, 128), 1)
    correction = 0.0
    for f in range(2):
        c = (lane + 32) % 128 - 32 - 64 * f
        cols = onehot(jnp.logical_and(jnp.logical_and(c >= -32, c < 32), j == col * 8 + (c >> 1)))
        whole = jnp.concatenate([e[f, t] for t in range(16)], axis=0)
        correction += times(pick(rows, whole), cols)

    is_red = red4()
    merged = merged_frame(mine, theirs, saved4[0])
    k, inv = edges4(saved4[2], saved4[3])
    x = jnp.where(is_red, 0.0, merged + correction)
    x = jnp.where(is_red, (merged + pull4(k, x)) * inv, 0.0)
    nat[...] = jnp.where(is_red, x, (saved4[1] + pull4(k, x)) * inv)
    ordered = jnp.concatenate([nat[pl.ds(a, 8, stride=3), :] for a in range(3)], axis=0)

    for level in range(3, -1, -1):
        count, width = TILES[level] // 2, LANES[level]
        even = even_lanes((8, width))
        state = states[level]
        unroll = (24, 12, 6, 3)[level]
        here = pl.ds(0, width)
        if level == 3:
            lane, wide = iota((128, 128), 0), iota((128, 128), 1)
            corrections = [times(ordered, onehot(side_lane(f, wide) == lane)) for f in range(2)]
        else:
            coarse = LANES[level + 1]
            lane, wide = iota((coarse, width), 0), iota((coarse, width), 1)
            pattern = onehot(coarse_lane(level, wide) == lane)
            corrections = [
                times(full[f, 0:count, :, pl.ds(0, coarse)].reshape(count * 8, coarse), pattern) for f in range(2)
            ]
        for f in range(2):
            blk[f, 1 : count + 1, :, here] = state[BLACK + f, 1 : count + 1] + corrections[f].reshape(count, 8, width)
            blk[f, 0, :, here] = roll(blk[f, count, :, here], 1, 0)
            blk[f, count + 1, :, here] = roll(blk[f, 1, :, here], -1, 0)

        def second_red(a, even=even, state=state, here=here):
            view = blk.at[:, :, :, here]
            for f in range(2):
                red[f, a + 1, :, here] = (state[f, a + 1] + pull_red(a, view, f, state, even)) * state[INV, a + 1]

        loop(count, second_red, unroll)
        for f in range(2):
            red[f, 0, :, here] = roll(red[f, count, :, here], 1, 0)
            red[f, count + 1, :, here] = roll(red[f, 1, :, here], -1, 0)

        def second_black(a, fields=(0, 1), level=level, even=even, state=state, here=here):
            view = red.at[:, :, :, here]
            for f in fields:
                x = red[f, a + 1, :, here]
                y = (state[2 + f, a + 1] + pull_black(a, view, f, state, even)) * state[INV + 1, a + 1]
                first, second = jnp.where(even, x, y), jnp.where(even, y, x)
                if level:
                    full[f, 2 * a, :, here] = first
                    full[f, 2 * a + 1, :, here] = second
                else:
                    for half in range(2):
                        lanes = slice(128 * half, 128 + 128 * half)
                        result[f, half, pl.ds(2 * a, 8, stride=48), :] = first[:, lanes]
                        result[f, half, pl.ds(2 * a + 1, 8, stride=48), :] = second[:, lanes]

        if level:
            loop(count, second_black, unroll)

    copies = []
    for f in range(2):
        loop(24, lambda a, f=f: second_black(a, (f,)), 24)
        for half in range(2):
            source = result.at[f, half, pl.ds(0, 256), :]
            copies.append(pltpu.make_async_copy(source, out.at[f, :, pl.ds(half * 128, 128)], sent.at[2 * f + half]))
            copies[-1].start()
    for copy in copies:
        copy.wait()


VMEM = pl.BlockSpec(memory_space=pltpu.VMEM)
ANY = pl.BlockSpec(memory_space=pl.ANY)
SMEM = pl.BlockSpec(memory_space=pltpu.SMEM)
PARAMS = pltpu.CompilerParams(vmem_limit_bytes=24 * 1024 * 1024)


def shaped(*shape):
    return jax.ShapeDtypeStruct(shape, F32)


def scratch(*shape):
    return pltpu.VMEM(shape, F32)


def state_shapes():
    return [(STATE, TILES[level] // 2 + 2, 8, LANES[level]) for level in range(4)]


def side_strips(observed, classes):
    return pl.pallas_call(
        sides_kernel,
        out_shape=[shaped(3, 256, 256), shaped(3, 64, 256), shaped(3, 64, 256), shaped(3, 128, 128), shaped(3, 128, 128)],
        in_specs=[VMEM] * 2,
        out_specs=[VMEM] * 5,
        compiler_params=PARAMS,
        name="sides",
    )(observed, classes)


def corner_strips(row_a, row_b):
    return pl.pallas_call(
        corners_kernel,
        out_shape=[shaped(3, 64, 128)] * 2,
        in_specs=[VMEM] * 2,
        out_specs=[VMEM] * 2,
        compiler_params=PARAMS,
        name="corners",
    )(row_a, row_b)


def middle(own, row_a, row_b, table):
    return pl.pallas_call(
        middle_kernel,
        out_shape=[shaped(4, 24, 8, 256)] * 2,
        in_specs=[VMEM] * 3 + [SMEM],
        out_specs=[VMEM] * 2,
        scratch_shapes=[scratch(3, 2, 384, 128)],
        compiler_params=PARAMS,
        name="middle",
    )(own, row_a, row_b, table)


def down(*args):
    return pl.pallas_call(
        down_kernel,
        out_shape=[shaped(*s) for s in state_shapes()] + [shaped(4, 24, 128), shaped(512, 128)],
        in_specs=[VMEM] * 6 + [SMEM],
        out_specs=[VMEM] * 6,
        scratch_shapes=[
            scratch(4, 26, 8, 384),
            scratch(2, 26, 8, 384),
            scratch(4, 24, 8, 256),
            scratch(4, 24, 8, 384),
            scratch(3, 384, 128),
            scratch(5, 24, 128),
        ],
        compiler_params=PARAMS,
        name="down",
    )(*args)


def up(mine, theirs, saved4, saved):
    return pl.pallas_call(
        up_kernel,
        out_shape=shaped(2, 256, 256),
        in_specs=[VMEM] * 7,
        out_specs=ANY,
        scratch_shapes=[
            scratch(2, 24, 8, 256),
            scratch(2, 26, 8, 384),
            scratch(2, 26, 8, 384),
            scratch(512, 128),
            scratch(5, 16, 8, 128),
            scratch(2, 16, 8, 128),
            scratch(2, 16, 8, 128),
            scratch(2, 16, 8, 128),
            scratch(2, 16, 8, 128),
            scratch(2, 16, 8, 128),
            scratch(2, 2, 384, 128),
            scratch(24, 128),
            pltpu.SemaphoreType.DMA((4,)),
        ],
        compiler_params=PARAMS,
        name="up",
    )(mine, theirs, saved4, *saved)


def swap(x, axis, first):
    pairs = [(i, i + 1) for i in range(first, 15, 2)]
    return lax.ppermute(x, axis, pairs + [(j, i) for i, j in pairs])


def local(observed, coherence_class, class_weight, class_stiffness):
    own, row_a, row_b, col_a, col_b = side_strips(observed, (coherence_class + 1).astype(F32))
    row_a, row_b = swap(row_a, ROW, 0), swap(row_b, ROW, 1)
    col_a, col_b = swap(col_a, "col", 0), swap(col_b, "col", 1)
    corner_a, corner_b = corner_strips(row_a, row_b)
    held = lax.optimization_barrier((corner_a, corner_b, own, row_a, row_b, class_weight, class_stiffness))
    corner_a, corner_b, own, row_a, row_b, class_weight, class_stiffness = held
    corner_a, corner_b = swap(corner_a, "col", 0), swap(corner_b, "col", 1)
    table = jnp.concatenate([class_weight, class_stiffness])
    rhs, gw = middle(own, row_a, row_b, table)
    results = down(rhs, gw, col_a, col_b, corner_a, corner_b, table)
    *saved, saved4, message = results
    mine = lax.all_to_all(message.reshape(128, 4, 128), ("z", "col"), 0, 0)
    theirs = lax.ppermute(mine, "core", [(0, 1), (1, 0)])
    return up(mine.reshape(512, 128), theirs.reshape(512, 128), saved4, saved)


def solution(mesh):
    chips = Mesh(mesh.devices.reshape(8, 2, 16), ("z", "core", "col"))
    in_specs = (P(None, ROW, "col"), P(ROW, "col"), P(), P())
    out_specs = P(None, ROW, "col")
    return jax.shard_map(local, mesh=chips, in_specs=in_specs, out_specs=out_specs, check_vma=False)
```

```python
import jax
import jax.numpy as jnp
from jax import lax
from jax.experimental import pallas as pl
from jax.experimental.pallas import tpu as pltpu
from jax.sharding import Mesh
from jax.sharding import PartitionSpec as P

CG_ITERS = 12
FAR = -1.0e4
TILES = (48, 24, 12, 6, 3)
LANES = (384, 256, 128, 128, 128)
F32 = jnp.float32
ROW = ("z", "core")
BF16 = jnp.bfloat16
BLACK, EDGE, INV, STATE = 4, 6, 11, 13


def iota(shape, axis):
    return lax.broadcasted_iota(jnp.int32, shape, axis)


def roll(x, shift, axis):
    return pltpu.roll(x, shift % x.shape[axis], axis)


def dot(a, b):
    return jnp.dot(a, b, preferred_element_type=F32)


def split(x):
    high = x.astype(BF16)
    return high, (x - high.astype(F32)).astype(BF16)


def times(x, pattern):
    high, low = split(x)
    return dot(high, pattern) + dot(low, pattern)


def pick(pattern, x):
    high, low = split(x)
    return dot(pattern, high) + dot(pattern, low)


def onehot(condition):
    return jnp.where(condition, 1.0, 0.0).astype(BF16)


def even_lanes(shape):
    return iota(shape, len(shape) - 1) % 2 == 0


def signed_lane(level, lane):
    width = LANES[level]
    own = 256 >> level
    return jnp.where(lane < (own + width) // 2, lane, lane - width)


def coarse_lane(level, lane):
    c = signed_lane(level, lane) >> 1
    return jnp.where(c < 0, c + LANES[level + 1], c)


def side_lane(field, lane3):
    c = (signed_lane(3, lane3) >> 1) + 64 * field
    return jnp.where(c < 0, c + 128, c)


def ends(ref, index, count):
    ref[index, 0] = roll(ref[index, count], 1, 0)
    ref[index, count + 1] = roll(ref[index, 1], -1, 0)


def loop(count, body, unroll):
    if count <= unroll:
        for i in range(count):
            body(i)
        return

    def step(i, carry):
        for j in range(unroll):
            body(i * unroll + j)
        return carry

    lax.fori_loop(0, count // unroll, step, 0)


def pull_red(a, black, f, state, even):
    b = black[f, a + 1]
    total = state[EDGE, a + 1] * b + state[EDGE + 1, a + 1] * jnp.where(even, black[f, a], black[f, a + 2])
    return total + state[EDGE + 3, a + 1] * roll(b, -1, 1) + roll(state[EDGE + 4, a + 1] * b, 1, 1)


def pull_black(a, red, f, state, even):
    r = red[f, a + 1]
    total = state[EDGE, a + 1] * r + state[EDGE + 2, a + 1] * jnp.where(even, red[f, a + 2], red[f, a])
    return total + state[EDGE + 4, a + 1] * roll(r, -1, 1) + roll(state[EDGE + 3, a + 1] * r, 1, 1)


def lookup(table, index):
    parts = []
    for c in range(index.shape[1] // 128):
        parts.append(jnp.take_along_axis(table, index[:, c * 128 : (c + 1) * 128], axis=1))
    return jnp.concatenate(parts, axis=1)


def edges4(g, w):
    k = [jnp.maximum(g + roll(g, s, x), 0.0) for s, x in ((1, 0), (-1, 0), (1, 1), (-1, 1))]
    return k, 1.0 / jnp.maximum(w + k[0] + k[1] + k[2] + k[3], 1e-20)


def pull4(k, v):
    return k[0] * roll(v, 1, 0) + k[1] * roll(v, -1, 0) + k[2] * roll(v, 1, 1) + k[3] * roll(v, -1, 1)


def red4():
    return (iota((24, 128), 0) + iota((24, 128), 1)) % 2 == 0


def place():
    return 2 * lax.axis_index("z") + lax.axis_index("core"), lax.axis_index("col")


def fold(x, low, swap):
    half = x.shape[0] // 2
    first, second = x[:half], x[half:]
    if swap:
        return jnp.where(low, roll(second, 64, 1), first)
    return jnp.where(low, first, roll(second, 64, 1))


def sides_kernel(observed, classes, own, row_a, row_b, col_a, col_b):
    row, col = place()
    own[0:2] = observed[...]
    own[2] = classes[...]
    low = iota((128, 128), 1) < 64
    for f in range(3):
        x = own.at[f]
        top, bottom = x[0:64, :], x[192:256, :]
        row_a[f] = jnp.where(row % 2 == 0, bottom, top)
        row_b[f] = jnp.where(row % 2 == 0, top, bottom)
        left, right = fold(x[:, 0:128], low, False), fold(x[:, 128:256], low, True)
        col_a[f] = jnp.where(col % 2 == 0, right, left)
        col_b[f] = jnp.where(col % 2 == 0, left, right)


def unfold(east, west, low):
    return jnp.where(low, east, west), roll(jnp.where(low, west, east), 64, 1)


def corners_kernel(col_a, col_b, out_a, out_b):
    row, col = place()
    low = iota((128, 128), 1) < 64
    for f in range(3):
        a, b = col_a[f], col_b[f]
        first, second = unfold(jnp.where(col % 2 == 0, a, b), jnp.where(col % 2 == 0, b, a), low)
        top, bottom = first[0:64], second[64:128]
        out_a[f] = jnp.where(row % 2 == 0, bottom, top)
        out_b[f] = jnp.where(row % 2 == 0, top, bottom)


def message_row(x, pattern, mine):
    return jnp.sum(jnp.where(mine, times(x, pattern), 0.0), axis=0, keepdims=True)


def class_tables(table):
    lane = iota((8, 128), 1)
    g, w = jnp.full((8, 128), FAR, F32), jnp.zeros((8, 128), F32)
    for i in range(8):
        g = jnp.where(lane == i + 1, 0.5 * table[8 + i], g)
        w = jnp.where(lane == i + 1, table[i], w)
    return g, w


def interleave(x, y, even):
    return jnp.where(even, x, y), jnp.where(even, y, x)


def middle_kernel(own, row_a, row_b, table, rhs, gw, frame):
    row, _ = place()
    for f in range(3):
        for half in range(2):
            lanes = slice(half * 128, half * 128 + 128)
            x, y = row_a[f, :, lanes], row_b[f, :, lanes]
            frame[f, half, 0:256, :] = own[f, :, lanes]
            frame[f, half, 256:320, :] = jnp.where(row % 2 == 0, x, y)
            frame[f, half, 320:384, :] = jnp.where(row % 2 == 0, y, x)
    tables = class_tables(table)
    even = even_lanes((8, 256))

    def tile(f, a):
        return jnp.concatenate([frame[f, c, pl.ds(a, 8, stride=48), :] for c in range(2)], axis=1)

    def pack(a):
        for f in range(2):
            rhs[f, a], rhs[2 + f, a] = interleave(tile(f, 2 * a), tile(f, 2 * a + 1), even)
        i, j = (tile(2, 2 * a + k).astype(jnp.int32) for k in range(2))
        for q in range(2):
            gw[2 * q, a], gw[2 * q + 1, a] = interleave(lookup(tables[q], i), lookup(tables[q], j), even)

    loop(24, pack, 12)


def down_kernel(rhs0, gw0, col_a, col_b, corner_a, corner_b, table, *rest):
    states = rest[:4]
    saved4, message = rest[4:6]
    gw, red, full, sums, frame, nat = rest[6:]
    row, col = place()
    even_row, even_col = row % 2 == 0, col % 2 == 0

    low = iota((128, 128), 1) < 64
    for f in range(3):
        a, b = col_a[f], col_b[f]
        first, second = unfold(jnp.where(even_col, a, b), jnp.where(even_col, b, a), low)
        frame[f, 0:128, :] = first
        frame[f, 128:256, :] = second
        a, b = corner_a[f], corner_b[f]
        frame[f, 256:320, :] = jnp.where(even_row, a, b)
        frame[f, 320:384, :] = jnp.where(even_row, b, a)
    tables = class_tables(table)
    narrow = even_lanes((8, 128))

    def side_tile(f, a):
        return frame[f, pl.ds(a, 8, stride=48), :]

    for level in range(4):
        count, width = TILES[level] // 2, LANES[level]
        even = even_lanes((8, width))
        state = states[level]
        unroll = (24, 12, 6, 3)[level]
        here = pl.ds(0, width)

        def pack(a, level=level, even=even, state=state, here=here):
            if level == 0:
                for f in range(2):
                    x = interleave(side_tile(f, 2 * a), side_tile(f, 2 * a + 1), narrow)
                    for k in range(2):
                        state[2 * k + f, a + 1] = jnp.concatenate([rhs0[2 * k + f, a], x[k]], axis=1)
                i, j = (side_tile(2, 2 * a + k).astype(jnp.int32) for k in range(2))
                for q in range(2):
                    x = interleave(lookup(tables[q], i), lookup(tables[q], j), narrow)
                    for k in range(2):
                        gw[2 * q + k, a + 1] = jnp.concatenate([gw0[2 * q + k, a], x[k]], axis=1)
            else:
                for f in range(2):
                    x = interleave(full[f, 2 * a, :, here], full[f, 2 * a + 1, :, here], even)
                    state[f, a + 1], state[2 + f, a + 1] = x
                for q in range(2):
                    x = interleave(full[2 + q, 2 * a, :, here], full[2 + q, 2 * a + 1, :, here], even)
                    gw[2 * q, a + 1, :, here], gw[2 * q + 1, a + 1, :, here] = x

        loop(count, pack, unroll)
        for q in range(2):
            gw[q, 0, :, here] = roll(gw[q, count, :, here], 1, 0)
            gw[q, count + 1, :, here] = roll(gw[q, 1, :, here], -1, 0)

        def edges(a, even=even, state=state, here=here):
            r, b = gw[0, a + 1, :, here], gw[1, a + 1, :, here]
            same = jnp.maximum(r + b, 0.0)
            r_other = jnp.maximum(r + jnp.where(even, gw[1, a, :, here], gw[1, a + 2, :, here]), 0.0)
            b_other = jnp.maximum(b + jnp.where(even, gw[0, a + 2, :, here], gw[0, a, :, here]), 0.0)
            r_east = jnp.maximum(r + roll(b, -1, 1), 0.0)
            b_east = jnp.maximum(b + roll(r, -1, 1), 0.0)
            r_inv = 1.0 / jnp.maximum(gw[2, a + 1, :, here] + same + r_other + r_east + roll(b_east, 1, 1), 1e-20)
            b_inv = 1.0 / jnp.maximum(gw[3, a + 1, :, here] + same + b_other + b_east + roll(r_east, 1, 1), 1e-20)
            for i, x in enumerate((same, r_other, b_other, r_east, b_east, r_inv, b_inv)):
                state[EDGE + i, a + 1] = x
            for f in range(2):
                red[f, a + 1, :, here] = state[f, a + 1] * r_inv
            sums[2, a, :, here] = 0.5 * (r + b)
            sums[3, a, :, here] = gw[2, a + 1, :, here] + gw[3, a + 1, :, here]

        loop(count, edges, unroll)
        for f in range(2):
            red[f, 0, :, here] = roll(red[f, count, :, here], 1, 0)
            red[f, count + 1, :, here] = roll(red[f, 1, :, here], -1, 0)

        def first_black(a, even=even, state=state, here=here):
            view = red.at[:, :, :, here]
            for f in range(2):
                state[BLACK + f, a + 1] = (state[2 + f, a + 1] + pull_black(a, view, f, state, even)) * state[INV + 1, a + 1]

        loop(count, first_black, unroll)
        for f in range(2):
            ends(state, BLACK + f, count)

        def restrict(a, even=even, state=state, here=here):
            for f in range(2):
                sums[f, a, :, here] = pull_red(a, state.at[BLACK : BLACK + 2], f, state, even)

        loop(count, restrict, unroll)
        fine = iota((width, LANES[level + 1]), 0)
        lane = iota((width, LANES[level + 1]), 1)
        if level < 3:
            pattern = onehot(coarse_lane(level, fine) == lane)
            for q in range(4):
                x = sums[q, 0:count, :, here].reshape(count * 8, width)
                full[q, 0:count, :, pl.ds(0, LANES[level + 1])] = times(x, pattern).reshape(count, 8, LANES[level + 1])
        else:
            first, second = (onehot(side_lane(f, fine) == lane) for f in range(2))
            x = [sums[q, 0:3, :, here].reshape(24, 128) for q in range(4)]
            results = [times(x[0], first) + times(x[1], second)] + [times(x[q], first + second) for q in (2, 3)]
            for q in range(3):
                for a in range(3):
                    nat[q, pl.ds(a, 8, stride=3), :] = results[q][a * 8 : a * 8 + 8]

    rhs, g, w = nat[0], nat[1], nat[2]
    is_red = red4()
    k, inv = edges4(g, w)
    v = jnp.where(is_red, rhs * inv, 0.0)
    v = jnp.where(is_red, v, (rhs + pull4(k, v)) * inv)
    merged = jnp.where(is_red, rhs, v)
    saved4[0] = merged
    saved4[1] = rhs
    saved4[2] = g
    saved4[3] = w
    nat[3] = jnp.where(is_red, pull4(k, v), 0.0)
    nat[4] = jnp.where(iota((24, 128), 1) < 64, 0.5 * g, w)

    lane = iota((128, 128), 0)
    l = iota((128, 128), 1)
    sub, at = iota((8, 128), 0), iota((8, 128), 1)
    pattern = onehot(jnp.logical_and(lane // 64 == l // 64, (lane % 64) // 2 == l % 8))
    mine = sub == (at // 8) % 8
    common = []
    for q in (3, 4):
        x = nat[q, pl.ds(0, 8, stride=2), :] + nat[q, pl.ds(1, 8, stride=2), :]
        common.append(message_row(x, pattern, mine))
    pattern = onehot(jnp.logical_and(lane // 64 == l // 64, lane % 64 == l % 16))
    top = message_row(merged[0:8], pattern, sub == (at // 16) % 4)
    bottom = message_row(merged[8:16], pattern, sub == (at // 16) % 4 + 4)
    mine = iota((16, 128), 0) == (iota((16, 128), 1) // 4) % 16
    pattern = onehot(jnp.logical_and(lane // 64 == l // 64, lane % 64 == l % 4))
    left = message_row(merged[0:16], pattern, mine)
    pattern = onehot(jnp.logical_and(lane // 64 == l // 64, lane % 64 == l % 4 + 12))
    right = message_row(merged[0:16], pattern, mine)

    block = jnp.concatenate((common + [jnp.zeros((2, 128), F32)]) * 8, axis=0)

    def send(i, carry):
        message[pl.ds(pl.multiple_of(i * 32, 32), 32), :] = block
        return carry

    lax.fori_loop(0, 16, send, 0)
    for dr, dc, what in NEIGHBOURS:
        x = {-1: top, 1: bottom}.get(dr, left if dc < 0 else right)
        r, c = row + dr, col + dc

        @pl.when(jnp.logical_and(jnp.logical_and(r >= 0, r < 16), jnp.logical_and(c >= 0, c < 16)))
        def _(r=r, c=c, x=x, dr=dr):
            message[pl.ds(((r >> 1) * 16 + c) * 4 + (3 if dr else 2), 1), :] = x


NEIGHBOURS = [(dr, dc, None) for dr in (-1, 0, 1) for dc in (-1, 0, 1) if dr or dc]


def cg(mine, theirs, mix, kc, e, d, s, w, r):
    lane = iota((8, 128), 1)
    sub = iota((8, 128), 0)
    group = lane // 8
    first_core = place()[0] % 2 == 0
    arrays = [[None] * 16 for _ in range(4)]
    for hi in range(2):
        for pair in range(2):
            v = []
            for c in range(16):
                rows = pl.ds((hi * 64 + c) * 4 + pair, 4, stride=64)
                x, y = mine[rows, :], theirs[rows, :]
                start = ((hi * 2 + pair) * 16 + c) * 8
                mix[pl.ds(start, 4, stride=2), :] = jnp.where(first_core, x, y)
                mix[pl.ds(start + 1, 4, stride=2), :] = jnp.where(first_core, y, x)
            for c in range(16):
                v.append(mix[pl.ds(((hi * 2 + pair) * 16 + c) * 8, 8), :])
            for k in (1, 2, 4, 8):
                low = (group // k) % 2 == 0
                for c in range(16):
                    if not c & k:
                        x, y = v[c], v[c | k]
                        v[c] = jnp.where(low, x, roll(y, 8 * k, 1))
                        v[c | k] = jnp.where(low, roll(x, -8 * k, 1), y)
            for i in range(16):
                arrays[2 * pair + i // 8][hi * 8 + i % 8] = v[i]

    def north(tile, t):
        if t % 8:
            return tile(t - 1)
        turned = roll(tile(t + 7), 1, 0)
        return turned if t == 0 else jnp.where(sub == 0, roll(tile(7), 1, 0), turned)

    def south(tile, t):
        if t % 8 != 7:
            return tile(t + 1)
        turned = roll(tile(t - 7), -1, 0)
        return turned if t == 15 else jnp.where(sub == 7, roll(tile(8), -1, 0), turned)

    g = arrays[2]
    for t in range(16):
        up = jnp.maximum(g[t] + north(lambda i: g[i], t), 0.0)
        down = jnp.maximum(g[t] + south(lambda i: g[i], t), 0.0)
        if t == 0:
            up = jnp.where(sub == 0, 0.0, up)
        if t == 15:
            down = jnp.where(sub == 7, 0.0, down)
        left = jnp.where(lane == 0, 0.0, jnp.maximum(g[t] + roll(g[t], 1, 1), 0.0))
        right = jnp.where(lane == 127, 0.0, jnp.maximum(g[t] + roll(g[t], -1, 1), 0.0))
        kc[0, t] = up
        kc[1, t] = down
        kc[2, t] = left
        kc[3, t] = right
        kc[4, t] = arrays[3][t] + up + down + left + right

    def sums(f):
        x = [r[f, t] for t in range(16)]
        tile = lambda i: x[i]
        total, norm = 0.0, 0.0
        for t in range(16):
            image = kc[4, t] * x[t] - (
                kc[0, t] * north(tile, t)
                + kc[1, t] * south(tile, t)
                + kc[2, t] * roll(x[t], 1, 1)
                + kc[3, t] * roll(x[t], -1, 1)
            )
            w[f, t] = image
            norm += x[t] * x[t]
            total += x[t] * image
        return tuple(jnp.sum(y, axis=(0, 1), keepdims=True) for y in (norm, total))

    state = []
    for f in range(2):
        for t in range(16):
            x = arrays[f][t]
            e[f, t] = jnp.zeros_like(x)
            d[f, t] = jnp.zeros_like(x)
            s[f, t] = jnp.zeros_like(x)
            r[f, t] = x
    for f in range(2):
        norm, total = sums(f)
        state.append((norm, norm / total, jnp.zeros_like(norm)))

    def iterate(_, state):
        for f in range(2):
            norm, alpha, beta = state[f]
            for t in range(16):
                x = r[f, t] + beta * d[f, t]
                y = w[f, t] + beta * s[f, t]
                d[f, t] = x
                s[f, t] = y
                e[f, t] = e[f, t] + alpha * x
                r[f, t] = r[f, t] - alpha * y
        result = []
        fresh = [sums(f) for f in range(2)]
        for f in range(2):
            norm, alpha, _ = state[f]
            beta = fresh[f][0] / norm
            result.append((fresh[f][0], fresh[f][0] / (fresh[f][1] - beta * fresh[f][0] / alpha), beta))
        return tuple(result)

    state = lax.fori_loop(0, CG_ITERS - 1, iterate, tuple(state))
    for f in range(2):
        _, alpha, beta = state[f]
        for t in range(16):
            e[f, t] = e[f, t] + alpha * (r[f, t] + beta * d[f, t])


def merged_frame(mine, theirs, merged):
    row, col = place()
    at = iota((24, 128), 0)
    l = iota((24, 128), 1)
    total = {}
    for dr, dc, _ in NEIGHBOURS:
        r, c = row + dr, col + dc
        there = jnp.logical_and(jnp.logical_and(r >= 0, r < 16), jnp.logical_and(c >= 0, c < 16))
        index = jnp.where(there, ((r >> 1) * 16 + c) * 4 + (3 if dr else 2), 0)
        x = (theirs if dr else mine)[pl.ds(index, 1), :] * jnp.where(there, 1.0, 0.0)
        if dr:
            ours = at == (20 if dr < 0 else 16) + (l // 16) % 4
        else:
            ours = at == (l // 4) % 16
        key = dc if dr else 2 * dc
        total[key] = total.get(key, 0.0) + jnp.where(ours, jnp.broadcast_to(x, (24, 128)), 0.0)
    l = iota((128, 128), 0)
    lane = iota((128, 128), 1)
    base = (l // 64) * 64
    j, c = l % 16, l % 4
    patterns = {
        0: lane == base + j,
        -1: jnp.logical_and(j >= 12, lane == (base + j - 16) % 128),
        1: jnp.logical_and(j < 4, lane == base + 16 + j),
        -2: lane == (base + c - 4) % 128,
        2: lane == base + 16 + c,
    }
    own = jnp.logical_and(at < 16, iota((24, 128), 1) % 64 < 16)
    result = jnp.where(own, merged, 0.0)
    for key, x in total.items():
        result += times(x, onehot(patterns[key]))
    return result


def up_kernel(mine, theirs, saved4, *rest):
    states, out = rest[:4], rest[4]
    full, red, blk, mix, kc, e, d, s, w, r, result, nat, sent = rest[5:]
    cg(mine, theirs, mix, kc, e, d, s, w, r)

    row, col = place()
    n = iota((24, 128), 1)
    at = iota((24, 128), 0)
    grid_row = (n // 64) * 64 + (n % 8) * 8 + (n // 8) % 8
    rows = onehot(grid_row == row * 8 + (jnp.where(at < 20, at, at - 24) >> 1))
    j = iota((128, 128), 0)
    lane = iota((128, 128), 1)
    correction = 0.0
    for f in range(2):
        c = (lane + 32) % 128 - 32 - 64 * f
        cols = onehot(jnp.logical_and(jnp.logical_and(c >= -32, c < 32), j == col * 8 + (c >> 1)))
        whole = jnp.concatenate([e[f, t] for t in range(16)], axis=0)
        correction += times(pick(rows, whole), cols)

    is_red = red4()
    merged = merged_frame(mine, theirs, saved4[0])
    k, inv = edges4(saved4[2], saved4[3])
    x = jnp.where(is_red, 0.0, merged + correction)
    x = jnp.where(is_red, (merged + pull4(k, x)) * inv, 0.0)
    nat[...] = jnp.where(is_red, x, (saved4[1] + pull4(k, x)) * inv)
    ordered = jnp.concatenate([nat[pl.ds(a, 8, stride=3), :] for a in range(3)], axis=0)

    for level in range(3, -1, -1):
        count, width = TILES[level] // 2, LANES[level]
        even = even_lanes((8, width))
        state = states[level]
        unroll = (24, 12, 6, 3)[level]
        here = pl.ds(0, width)
        if level == 3:
            lane, wide = iota((128, 128), 0), iota((128, 128), 1)
            corrections = [times(ordered, onehot(side_lane(f, wide) == lane)) for f in range(2)]
        else:
            coarse = LANES[level + 1]
            lane, wide = iota((coarse, width), 0), iota((coarse, width), 1)
            pattern = onehot(coarse_lane(level, wide) == lane)
            corrections = [
                times(full[f, 0:count, :, pl.ds(0, coarse)].reshape(count * 8, coarse), pattern) for f in range(2)
            ]
        for f in range(2):
            blk[f, 1 : count + 1, :, here] = state[BLACK + f, 1 : count + 1] + corrections[f].reshape(count, 8, width)
            blk[f, 0, :, here] = roll(blk[f, count, :, here], 1, 0)
            blk[f, count + 1, :, here] = roll(blk[f, 1, :, here], -1, 0)

        def second_red(a, even=even, state=state, here=here):
            view = blk.at[:, :, :, here]
            for f in range(2):
                red[f, a + 1, :, here] = (state[f, a + 1] + pull_red(a, view, f, state, even)) * state[INV, a + 1]

        loop(count, second_red, unroll)
        for f in range(2):
            red[f, 0, :, here] = roll(red[f, count, :, here], 1, 0)
            red[f, count + 1, :, here] = roll(red[f, 1, :, here], -1, 0)

        def second_black(a, fields=(0, 1), level=level, even=even, state=state, here=here):
            view = red.at[:, :, :, here]
            for f in fields:
                x = red[f, a + 1, :, here]
                y = (state[2 + f, a + 1] + pull_black(a, view, f, state, even)) * state[INV + 1, a + 1]
                first, second = jnp.where(even, x, y), jnp.where(even, y, x)
                if level:
                    full[f, 2 * a, :, here] = first
                    full[f, 2 * a + 1, :, here] = second
                else:
                    for half in range(2):
                        lanes = slice(128 * half, 128 + 128 * half)
                        result[f, half, pl.ds(2 * a, 8, stride=48), :] = first[:, lanes]
                        result[f, half, pl.ds(2 * a + 1, 8, stride=48), :] = second[:, lanes]

        if level:
            loop(count, second_black, unroll)

    copies = []
    for f in range(2):
        loop(24, lambda a, f=f: second_black(a, (f,)), 24)
        for half in range(2):
            source = result.at[f, half, pl.ds(0, 256), :]
            copies.append(pltpu.make_async_copy(source, out.at[f, :, pl.ds(half * 128, 128)], sent.at[2 * f + half]))
            copies[-1].start()
    for copy in copies:
        copy.wait()


VMEM = pl.BlockSpec(memory_space=pltpu.VMEM)
ANY = pl.BlockSpec(memory_space=pl.ANY)
SMEM = pl.BlockSpec(memory_space=pltpu.SMEM)
PARAMS = pltpu.CompilerParams(vmem_limit_bytes=24 * 1024 * 1024)


def shaped(*shape):
    return jax.ShapeDtypeStruct(shape, F32)


def scratch(*shape):
    return pltpu.VMEM(shape, F32)


def state_shapes():
    return [(STATE, TILES[level] // 2 + 2, 8, LANES[level]) for level in range(4)]


def side_strips(observed, classes):
    return pl.pallas_call(
        sides_kernel,
        out_shape=[shaped(3, 256, 256), shaped(3, 64, 256), shaped(3, 64, 256), shaped(3, 128, 128), shaped(3, 128, 128)],
        in_specs=[VMEM] * 2,
        out_specs=[VMEM] * 5,
        compiler_params=PARAMS,
        name="sides",
    )(observed, classes)


def corner_strips(col_a, col_b):
    return pl.pallas_call(
        corners_kernel,
        out_shape=[shaped(3, 64, 128)] * 2,
        in_specs=[VMEM] * 2,
        out_specs=[VMEM] * 2,
        compiler_params=PARAMS,
        name="corners",
    )(col_a, col_b)


def middle(own, row_a, row_b, table):
    return pl.pallas_call(
        middle_kernel,
        out_shape=[shaped(4, 24, 8, 256)] * 2,
        in_specs=[VMEM] * 3 + [SMEM],
        out_specs=[VMEM] * 2,
        scratch_shapes=[scratch(3, 2, 384, 128)],
        compiler_params=PARAMS,
        name="middle",
    )(own, row_a, row_b, table)


def down(*args):
    return pl.pallas_call(
        down_kernel,
        out_shape=[shaped(*s) for s in state_shapes()] + [shaped(4, 24, 128), shaped(512, 128)],
        in_specs=[VMEM] * 6 + [SMEM],
        out_specs=[VMEM] * 6,
        scratch_shapes=[
            scratch(4, 26, 8, 384),
            scratch(2, 26, 8, 384),
            scratch(4, 24, 8, 256),
            scratch(4, 24, 8, 384),
            scratch(3, 384, 128),
            scratch(5, 24, 128),
        ],
        compiler_params=PARAMS,
        name="down",
    )(*args)


def up(mine, theirs, saved4, saved):
    return pl.pallas_call(
        up_kernel,
        out_shape=shaped(2, 256, 256),
        in_specs=[VMEM] * 7,
        out_specs=ANY,
        scratch_shapes=[
            scratch(2, 24, 8, 256),
            scratch(2, 26, 8, 384),
            scratch(2, 26, 8, 384),
            scratch(512, 128),
            scratch(5, 16, 8, 128),
            scratch(2, 16, 8, 128),
            scratch(2, 16, 8, 128),
            scratch(2, 16, 8, 128),
            scratch(2, 16, 8, 128),
            scratch(2, 16, 8, 128),
            scratch(2, 2, 384, 128),
            scratch(24, 128),
            pltpu.SemaphoreType.DMA((4,)),
        ],
        compiler_params=PARAMS,
        name="up",
    )(mine, theirs, saved4, *saved)


def swap(x, axis, first):
    pairs = [(i, i + 1) for i in range(first, 15, 2)]
    return lax.ppermute(x, axis, pairs + [(j, i) for i, j in pairs])


def local(observed, coherence_class, class_weight, class_stiffness):
    own, row_a, row_b, col_a, col_b = side_strips(observed, (coherence_class + 1).astype(F32))
    col_a, col_b = swap(col_a, "col", 0), swap(col_b, "col", 1)
    row_a, row_b = swap(row_a, ROW, 0), swap(row_b, ROW, 1)
    corner_a, corner_b = corner_strips(col_a, col_b)
    held = lax.optimization_barrier((corner_a, corner_b, own, class_weight, class_stiffness))
    corner_a, corner_b, own, class_weight, class_stiffness = held
    corner_a, corner_b = swap(corner_a, ROW, 0), swap(corner_b, ROW, 1)
    table = jnp.concatenate([class_weight, class_stiffness])
    rhs, gw = middle(own, row_a, row_b, table)
    results = down(rhs, gw, col_a, col_b, corner_a, corner_b, table)
    *saved, saved4, message = results
    mine = lax.all_to_all(message.reshape(128, 4, 128), ("z", "col"), 0, 0)
    theirs = lax.ppermute(mine, "core", [(0, 1), (1, 0)])
    return up(mine.reshape(512, 128), theirs.reshape(512, 128), saved4, saved)


def solution(mesh):
    chips = Mesh(mesh.devices.reshape(8, 2, 16), ("z", "core", "col"))
    in_specs = (P(None, ROW, "col"), P(ROW, "col"), P(), P())
    out_specs = P(None, ROW, "col")
    return jax.shard_map(local, mesh=chips, in_specs=in_specs, out_specs=out_specs, check_vma=False)
```

```python
import jax
import jax.numpy as jnp
from jax import lax
from jax.experimental import pallas as pl
from jax.experimental.pallas import tpu as pltpu
from jax.sharding import Mesh
from jax.sharding import PartitionSpec as P

CG_ITERS = 12
FAR = -1.0e4
TILES = (48, 24, 12, 6, 3)
LANES = (384, 256, 128, 128, 128)
F32 = jnp.float32
ROW = ("z", "core")
BF16 = jnp.bfloat16
BLACK, EDGE, INV, STATE = 4, 6, 11, 13


def iota(shape, axis):
    return lax.broadcasted_iota(jnp.int32, shape, axis)


def roll(x, shift, axis):
    return pltpu.roll(x, shift % x.shape[axis], axis)


def dot(a, b):
    return jnp.dot(a, b, preferred_element_type=F32)


def split(x):
    high = x.astype(BF16)
    return high, (x - high.astype(F32)).astype(BF16)


def times(x, pattern):
    high, low = split(x)
    return dot(high, pattern) + dot(low, pattern)


def pick(pattern, x):
    high, low = split(x)
    return dot(pattern, high) + dot(pattern, low)


def onehot(condition):
    return jnp.where(condition, 1.0, 0.0).astype(BF16)


def even_lanes(shape):
    return iota(shape, len(shape) - 1) % 2 == 0


def signed_lane(level, lane):
    width = LANES[level]
    own = 256 >> level
    return jnp.where(lane < (own + width) // 2, lane, lane - width)


def coarse_lane(level, lane):
    c = signed_lane(level, lane) >> 1
    return jnp.where(c < 0, c + LANES[level + 1], c)


def side_lane(field, lane3):
    c = (signed_lane(3, lane3) >> 1) + 64 * field
    return jnp.where(c < 0, c + 128, c)


def ends(ref, index, count):
    ref[index, 0] = roll(ref[index, count], 1, 0)
    ref[index, count + 1] = roll(ref[index, 1], -1, 0)


def loop(count, body, unroll):
    if count <= unroll:
        for i in range(count):
            body(i)
        return

    def step(i, carry):
        for j in range(unroll):
            body(i * unroll + j)
        return carry

    lax.fori_loop(0, count // unroll, step, 0)


def pull_red(a, black, f, state, even):
    b = black[f, a + 1]
    total = state[EDGE, a + 1] * b + state[EDGE + 1, a + 1] * jnp.where(even, black[f, a], black[f, a + 2])
    return total + state[EDGE + 3, a + 1] * roll(b, -1, 1) + roll(state[EDGE + 4, a + 1] * b, 1, 1)


def pull_black(a, red, f, state, even):
    r = red[f, a + 1]
    total = state[EDGE, a + 1] * r + state[EDGE + 2, a + 1] * jnp.where(even, red[f, a + 2], red[f, a])
    return total + state[EDGE + 4, a + 1] * roll(r, -1, 1) + roll(state[EDGE + 3, a + 1] * r, 1, 1)


def lookup(table, index):
    parts = []
    for c in range(index.shape[1] // 128):
        parts.append(jnp.take_along_axis(table, index[:, c * 128 : (c + 1) * 128], axis=1))
    return jnp.concatenate(parts, axis=1)


def edges4(g, w):
    k = [jnp.maximum(g + roll(g, s, x), 0.0) for s, x in ((1, 0), (-1, 0), (1, 1), (-1, 1))]
    return k, 1.0 / jnp.maximum(w + k[0] + k[1] + k[2] + k[3], 1e-20)


def pull4(k, v):
    return k[0] * roll(v, 1, 0) + k[1] * roll(v, -1, 0) + k[2] * roll(v, 1, 1) + k[3] * roll(v, -1, 1)


def red4():
    return (iota((24, 128), 0) + iota((24, 128), 1)) % 2 == 0


def place():
    return 2 * lax.axis_index("z") + lax.axis_index("core"), lax.axis_index("col")


def fold(x, low, swap):
    half = x.shape[0] // 2
    first, second = x[:half], x[half:]
    if swap:
        return jnp.where(low, roll(second, 64, 1), first)
    return jnp.where(low, first, roll(second, 64, 1))


def sides_kernel(observed, classes, own, row_a, row_b, col_a, col_b):
    row, col = place()
    own[0:2] = observed[...]
    own[2] = classes[...]
    low = iota((128, 128), 1) < 64
    for f in range(3):
        x = own.at[f]
        top, bottom = x[0:64, :], x[192:256, :]
        row_a[f] = jnp.where(row % 2 == 0, bottom, top)
        row_b[f] = jnp.where(row % 2 == 0, top, bottom)
        left, right = fold(x[:, 0:128], low, False), fold(x[:, 128:256], low, True)
        col_a[f] = jnp.where(col % 2 == 0, right, left)
        col_b[f] = jnp.where(col % 2 == 0, left, right)


def corners_kernel(row_a, row_b, out_a, out_b):
    row, col = place()
    low = iota((64, 128), 1) < 64
    for f in range(3):
        a, b = row_a[f], row_b[f]
        south, north = jnp.where(row % 2 == 0, a, b), jnp.where(row % 2 == 0, b, a)
        x = jnp.concatenate([south, north], axis=0)
        left, right = fold(x[:, 0:128], low, False), fold(x[:, 128:256], low, True)
        out_a[f] = jnp.where(col % 2 == 0, right, left)
        out_b[f] = jnp.where(col % 2 == 0, left, right)


def message_row(x, pattern, mine):
    return jnp.sum(jnp.where(mine, times(x, pattern), 0.0), axis=0, keepdims=True)


def class_tables(table):
    lane = iota((8, 128), 1)
    g, w = jnp.full((8, 128), FAR, F32), jnp.zeros((8, 128), F32)
    for i in range(8):
        g = jnp.where(lane == i + 1, 0.5 * table[8 + i], g)
        w = jnp.where(lane == i + 1, table[i], w)
    return g, w


def interleave(x, y, even):
    return jnp.where(even, x, y), jnp.where(even, y, x)


def small_patterns(col):
    x, y = iota((128, 128), 0), iota((128, 128), 1)
    same = x // 64 == y // 64
    result = [coarse_lane(2, x) == y, side_lane(0, x) == y, side_lane(1, x) == y]
    result.append(jnp.logical_and(same, (x % 64) // 2 == y % 8))
    result.append(jnp.logical_and(same, x % 64 == y % 16))
    result.append(jnp.logical_and(same, x % 64 == y % 4))
    result.append(jnp.logical_and(same, x % 64 == y % 4 + 12))
    result += [side_lane(0, y) == x, side_lane(1, y) == x, coarse_lane(2, y) == x]
    for f in range(2):
        c = (y + 32) % 128 - 32 - 64 * f
        result.append(jnp.logical_and(jnp.logical_and(c >= -32, c < 32), x == col * 8 + (c >> 1)))
    base = (x // 64) * 64
    j, c = x % 16, x % 4
    result.append(y == base + j)
    result.append(jnp.logical_and(j >= 12, y == (base + j - 16) % 128))
    result.append(jnp.logical_and(j < 4, y == base + 16 + j))
    result.append(y == (base + c - 4) % 128)
    result.append(y == base + 16 + c)
    return result


(TO_4, TO_5, COMMON, ROWS, LEFT, RIGHT, FROM_4, FROM_3, COLS, AROUND) = (0, 1, 3, 4, 5, 6, 7, 9, 10, 12)
BIG = ((384, 256), (256, 128), (128, 256), (256, 384))


def middle_kernel(own, row_a, row_b, table, rhs, gw, small, down0, down1, up1, up0, frame):
    row, col = place()
    for i, pattern in enumerate(small_patterns(col)):
        small[i] = onehot(pattern)
    for level, fine, ref in ((0, 0, down0), (1, 0, down1), (1, 1, up1), (0, 1, up0)):
        ref[...] = onehot(coarse_lane(level, iota(ref.shape, fine)) == iota(ref.shape, 1 - fine))
    for f in range(3):
        for half in range(2):
            lanes = slice(half * 128, half * 128 + 128)
            x, y = row_a[f, :, lanes], row_b[f, :, lanes]
            frame[f, half, 0:256, :] = own[f, :, lanes]
            frame[f, half, 256:320, :] = jnp.where(row % 2 == 0, x, y)
            frame[f, half, 320:384, :] = jnp.where(row % 2 == 0, y, x)
    tables = class_tables(table)
    even = even_lanes((8, 256))

    def tile(f, a):
        return jnp.concatenate([frame[f, c, pl.ds(a, 8, stride=48), :] for c in range(2)], axis=1)

    def pack(a):
        for f in range(2):
            rhs[f, a], rhs[2 + f, a] = interleave(tile(f, 2 * a), tile(f, 2 * a + 1), even)
        i, j = (tile(2, 2 * a + k).astype(jnp.int32) for k in range(2))
        for q in range(2):
            gw[2 * q, a], gw[2 * q + 1, a] = interleave(lookup(tables[q], i), lookup(tables[q], j), even)

    loop(24, pack, 12)


def down_kernel(rhs0, gw0, small, down0, down1, col_a, col_b, corner_a, corner_b, table, *rest):
    states = rest[:4]
    saved4, message = rest[4:6]
    gw, red, full, sums, frame, nat = rest[6:]
    row, col = place()
    even_col = col % 2 == 0

    for a, b, start, size in ((col_a, col_b, 0, 128), (corner_a, corner_b, 256, 64)):
        low = iota((size, 128), 1) < 64
        for f in range(3):
            x, y = a[f], b[f]
            e, w = jnp.where(even_col, x, y), jnp.where(even_col, y, x)
            frame[f, start : start + size, :] = jnp.where(low, e, w)
            frame[f, start + size : start + 2 * size, :] = roll(jnp.where(low, w, e), 64, 1)
    tables = class_tables(table)
    narrow = even_lanes((8, 128))

    def side_tile(f, a):
        return frame[f, pl.ds(a, 8, stride=48), :]

    for level in range(4):
        count, width = TILES[level] // 2, LANES[level]
        even = even_lanes((8, width))
        state = states[level]
        unroll = (24, 12, 6, 3)[level]
        here = pl.ds(0, width)

        def pack(a, level=level, even=even, state=state, here=here):
            if level == 0:
                for f in range(2):
                    x = interleave(side_tile(f, 2 * a), side_tile(f, 2 * a + 1), narrow)
                    for k in range(2):
                        state[2 * k + f, a + 1] = jnp.concatenate([rhs0[2 * k + f, a], x[k]], axis=1)
                i, j = (side_tile(2, 2 * a + k).astype(jnp.int32) for k in range(2))
                for q in range(2):
                    x = interleave(lookup(tables[q], i), lookup(tables[q], j), narrow)
                    for k in range(2):
                        gw[2 * q + k, a + 1] = jnp.concatenate([gw0[2 * q + k, a], x[k]], axis=1)
            else:
                for f in range(2):
                    x = interleave(full[f, 2 * a, :, here], full[f, 2 * a + 1, :, here], even)
                    state[f, a + 1], state[2 + f, a + 1] = x
                for q in range(2):
                    x = interleave(full[2 + q, 2 * a, :, here], full[2 + q, 2 * a + 1, :, here], even)
                    gw[2 * q, a + 1, :, here], gw[2 * q + 1, a + 1, :, here] = x

        loop(count, pack, unroll)
        for q in range(2):
            gw[q, 0, :, here] = roll(gw[q, count, :, here], 1, 0)
            gw[q, count + 1, :, here] = roll(gw[q, 1, :, here], -1, 0)

        def edges(a, even=even, state=state, here=here):
            r, b = gw[0, a + 1, :, here], gw[1, a + 1, :, here]
            same = jnp.maximum(r + b, 0.0)
            r_other = jnp.maximum(r + jnp.where(even, gw[1, a, :, here], gw[1, a + 2, :, here]), 0.0)
            b_other = jnp.maximum(b + jnp.where(even, gw[0, a + 2, :, here], gw[0, a, :, here]), 0.0)
            r_east = jnp.maximum(r + roll(b, -1, 1), 0.0)
            b_east = jnp.maximum(b + roll(r, -1, 1), 0.0)
            r_inv = 1.0 / jnp.maximum(gw[2, a + 1, :, here] + same + r_other + r_east + roll(b_east, 1, 1), 1e-20)
            b_inv = 1.0 / jnp.maximum(gw[3, a + 1, :, here] + same + b_other + b_east + roll(r_east, 1, 1), 1e-20)
            for i, x in enumerate((same, r_other, b_other, r_east, b_east, r_inv, b_inv)):
                state[EDGE + i, a + 1] = x
            for f in range(2):
                red[f, a + 1, :, here] = state[f, a + 1] * r_inv
            sums[2, a, :, here] = 0.5 * (r + b)
            sums[3, a, :, here] = gw[2, a + 1, :, here] + gw[3, a + 1, :, here]

        loop(count, edges, unroll)
        for f in range(2):
            red[f, 0, :, here] = roll(red[f, count, :, here], 1, 0)
            red[f, count + 1, :, here] = roll(red[f, 1, :, here], -1, 0)

        def first_black(a, even=even, state=state, here=here):
            view = red.at[:, :, :, here]
            for f in range(2):
                state[BLACK + f, a + 1] = (state[2 + f, a + 1] + pull_black(a, view, f, state, even)) * state[INV + 1, a + 1]

        loop(count, first_black, unroll)
        for f in range(2):
            ends(state, BLACK + f, count)

        def restrict(a, even=even, state=state, here=here):
            for f in range(2):
                sums[f, a, :, here] = pull_red(a, state.at[BLACK : BLACK + 2], f, state, even)

        loop(count, restrict, unroll)
        if level < 3:
            pattern = (down0[...], down1[...], small[TO_4])[level]
            for q in range(4):
                x = sums[q, 0:count, :, here].reshape(count * 8, width)
                full[q, 0:count, :, pl.ds(0, LANES[level + 1])] = times(x, pattern).reshape(count, 8, LANES[level + 1])
        else:
            first, second = small[TO_5], small[TO_5 + 1]
            x = [sums[q, 0:3, :, here].reshape(24, 128) for q in range(4)]
            results = [times(x[0], first) + times(x[1], second)] + [times(x[q], first + second) for q in (2, 3)]
            for q in range(3):
                for a in range(3):
                    nat[q, pl.ds(a, 8, stride=3), :] = results[q][a * 8 : a * 8 + 8]

    rhs, g, w = nat[0], nat[1], nat[2]
    is_red = red4()
    k, inv = edges4(g, w)
    v = jnp.where(is_red, rhs * inv, 0.0)
    v = jnp.where(is_red, v, (rhs + pull4(k, v)) * inv)
    merged = jnp.where(is_red, rhs, v)
    saved4[0] = merged
    saved4[1] = rhs
    saved4[2] = g
    saved4[3] = w
    nat[3] = jnp.where(is_red, pull4(k, v), 0.0)
    nat[4] = jnp.where(iota((24, 128), 1) < 64, 0.5 * g, w)

    sub, at = iota((8, 128), 0), iota((8, 128), 1)
    mine = sub == (at // 8) % 8
    common = []
    for q in (3, 4):
        x = nat[q, pl.ds(0, 8, stride=2), :] + nat[q, pl.ds(1, 8, stride=2), :]
        common.append(message_row(x, small[COMMON], mine))
    top = message_row(merged[0:8], small[ROWS], sub == (at // 16) % 4)
    bottom = message_row(merged[8:16], small[ROWS], sub == (at // 16) % 4 + 4)
    mine = iota((16, 128), 0) == (iota((16, 128), 1) // 4) % 16
    left = message_row(merged[0:16], small[LEFT], mine)
    right = message_row(merged[0:16], small[RIGHT], mine)

    block = jnp.concatenate((common + [jnp.zeros((2, 128), F32)]) * 8, axis=0)

    def send(i, carry):
        message[pl.ds(pl.multiple_of(i * 32, 32), 32), :] = block
        return carry

    lax.fori_loop(0, 16, send, 0)
    for dr, dc, what in NEIGHBOURS:
        x = {-1: top, 1: bottom}.get(dr, left if dc < 0 else right)
        r, c = row + dr, col + dc

        @pl.when(jnp.logical_and(jnp.logical_and(r >= 0, r < 16), jnp.logical_and(c >= 0, c < 16)))
        def _(r=r, c=c, x=x, dr=dr):
            message[pl.ds(((r >> 1) * 16 + c) * 4 + (3 if dr else 2), 1), :] = x


NEIGHBOURS = [(dr, dc, None) for dr in (-1, 0, 1) for dc in (-1, 0, 1) if dr or dc]


def cg(mine, theirs, mix, kc, e, d, s, w, r):
    lane = iota((8, 128), 1)
    sub = iota((8, 128), 0)
    group = lane // 8
    first_core = place()[0] % 2 == 0
    arrays = [[None] * 16 for _ in range(4)]
    for hi in range(2):
        for pair in range(2):
            v = []
            for c in range(16):
                rows = pl.ds((hi * 64 + c) * 4 + pair, 4, stride=64)
                x, y = mine[rows, :], theirs[rows, :]
                start = ((hi * 2 + pair) * 16 + c) * 8
                mix[pl.ds(start, 4, stride=2), :] = jnp.where(first_core, x, y)
                mix[pl.ds(start + 1, 4, stride=2), :] = jnp.where(first_core, y, x)
            for c in range(16):
                v.append(mix[pl.ds(((hi * 2 + pair) * 16 + c) * 8, 8), :])
            for k in (1, 2, 4, 8):
                low = (group // k) % 2 == 0
                for c in range(16):
                    if not c & k:
                        x, y = v[c], v[c | k]
                        v[c] = jnp.where(low, x, roll(y, 8 * k, 1))
                        v[c | k] = jnp.where(low, roll(x, -8 * k, 1), y)
            for i in range(16):
                arrays[2 * pair + i // 8][hi * 8 + i % 8] = v[i]

    def north(tile, t):
        if t % 8:
            return tile(t - 1)
        turned = roll(tile(t + 7), 1, 0)
        return turned if t == 0 else jnp.where(sub == 0, roll(tile(7), 1, 0), turned)

    def south(tile, t):
        if t % 8 != 7:
            return tile(t + 1)
        turned = roll(tile(t - 7), -1, 0)
        return turned if t == 15 else jnp.where(sub == 7, roll(tile(8), -1, 0), turned)

    g = arrays[2]
    for t in range(16):
        up = jnp.maximum(g[t] + north(lambda i: g[i], t), 0.0)
        down = jnp.maximum(g[t] + south(lambda i: g[i], t), 0.0)
        if t == 0:
            up = jnp.where(sub == 0, 0.0, up)
        if t == 15:
            down = jnp.where(sub == 7, 0.0, down)
        left = jnp.where(lane == 0, 0.0, jnp.maximum(g[t] + roll(g[t], 1, 1), 0.0))
        right = jnp.where(lane == 127, 0.0, jnp.maximum(g[t] + roll(g[t], -1, 1), 0.0))
        kc[0, t] = up
        kc[1, t] = down
        kc[2, t] = left
        kc[3, t] = right
        kc[4, t] = arrays[3][t] + up + down + left + right

    def sums(f):
        x = [r[f, t] for t in range(16)]
        tile = lambda i: x[i]
        total, norm = 0.0, 0.0
        for t in range(16):
            image = kc[4, t] * x[t] - (
                kc[0, t] * north(tile, t)
                + kc[1, t] * south(tile, t)
                + kc[2, t] * roll(x[t], 1, 1)
                + kc[3, t] * roll(x[t], -1, 1)
            )
            w[f, t] = image
            norm += x[t] * x[t]
            total += x[t] * image
        return tuple(jnp.sum(y, axis=(0, 1), keepdims=True) for y in (norm, total))

    state = []
    for f in range(2):
        for t in range(16):
            x = arrays[f][t]
            e[f, t] = jnp.zeros_like(x)
            d[f, t] = jnp.zeros_like(x)
            s[f, t] = jnp.zeros_like(x)
            r[f, t] = x
    for f in range(2):
        norm, total = sums(f)
        state.append((norm, norm / total, jnp.zeros_like(norm)))

    def iterate(_, state):
        for f in range(2):
            norm, alpha, beta = state[f]
            for t in range(16):
                x = r[f, t] + beta * d[f, t]
                y = w[f, t] + beta * s[f, t]
                d[f, t] = x
                s[f, t] = y
                e[f, t] = e[f, t] + alpha * x
                r[f, t] = r[f, t] - alpha * y
        result = []
        fresh = [sums(f) for f in range(2)]
        for f in range(2):
            norm, alpha, _ = state[f]
            beta = fresh[f][0] / norm
            result.append((fresh[f][0], fresh[f][0] / (fresh[f][1] - beta * fresh[f][0] / alpha), beta))
        return tuple(result)

    state = lax.fori_loop(0, CG_ITERS - 1, iterate, tuple(state))
    for f in range(2):
        _, alpha, beta = state[f]
        for t in range(16):
            e[f, t] = e[f, t] + alpha * (r[f, t] + beta * d[f, t])


def merged_frame(mine, theirs, small, merged):
    row, col = place()
    at = iota((24, 128), 0)
    l = iota((24, 128), 1)
    total = {}
    for dr, dc, _ in NEIGHBOURS:
        r, c = row + dr, col + dc
        there = jnp.logical_and(jnp.logical_and(r >= 0, r < 16), jnp.logical_and(c >= 0, c < 16))
        index = jnp.where(there, ((r >> 1) * 16 + c) * 4 + (3 if dr else 2), 0)
        x = (theirs if dr else mine)[pl.ds(index, 1), :] * jnp.where(there, 1.0, 0.0)
        if dr:
            ours = at == (20 if dr < 0 else 16) + (l // 16) % 4
        else:
            ours = at == (l // 4) % 16
        key = dc if dr else 2 * dc
        total[key] = total.get(key, 0.0) + jnp.where(ours, jnp.broadcast_to(x, (24, 128)), 0.0)
    own = jnp.logical_and(at < 16, iota((24, 128), 1) % 64 < 16)
    result = jnp.where(own, merged, 0.0)
    for key, x in total.items():
        result += times(x, small[AROUND + (0, -1, 1, -2, 2).index(key)])
    return result


def up_kernel(mine, theirs, small, up1, up0, saved4, *rest):
    states, out = rest[:4], rest[4]
    full, red, blk, mix, kc, e, d, s, w, r, result, nat, sent = rest[5:]
    cg(mine, theirs, mix, kc, e, d, s, w, r)

    row, col = place()
    n = iota((24, 128), 1)
    at = iota((24, 128), 0)
    grid_row = (n // 64) * 64 + (n % 8) * 8 + (n // 8) % 8
    rows = onehot(grid_row == row * 8 + (jnp.where(at < 20, at, at - 24) >> 1))
    correction = 0.0
    for f in range(2):
        whole = jnp.concatenate([e[f, t] for t in range(16)], axis=0)
        correction += times(pick(rows, whole), small[COLS + f])

    is_red = red4()
    merged = merged_frame(mine, theirs, small, saved4[0])
    k, inv = edges4(saved4[2], saved4[3])
    x = jnp.where(is_red, 0.0, merged + correction)
    x = jnp.where(is_red, (merged + pull4(k, x)) * inv, 0.0)
    nat[...] = jnp.where(is_red, x, (saved4[1] + pull4(k, x)) * inv)
    ordered = jnp.concatenate([nat[pl.ds(a, 8, stride=3), :] for a in range(3)], axis=0)

    for level in range(3, -1, -1):
        count, width = TILES[level] // 2, LANES[level]
        even = even_lanes((8, width))
        state = states[level]
        unroll = (24, 12, 6, 3)[level]
        here = pl.ds(0, width)
        if level == 3:
            corrections = [times(ordered, small[FROM_4 + f]) for f in range(2)]
        else:
            coarse = LANES[level + 1]
            pattern = (up0[...], up1[...], small[FROM_3])[level]
            corrections = [
                times(full[f, 0:count, :, pl.ds(0, coarse)].reshape(count * 8, coarse), pattern) for f in range(2)
            ]
        for f in range(2):
            blk[f, 1 : count + 1, :, here] = state[BLACK + f, 1 : count + 1] + corrections[f].reshape(count, 8, width)
            blk[f, 0, :, here] = roll(blk[f, count, :, here], 1, 0)
            blk[f, count + 1, :, here] = roll(blk[f, 1, :, here], -1, 0)

        def second_red(a, even=even, state=state, here=here):
            view = blk.at[:, :, :, here]
            for f in range(2):
                red[f, a + 1, :, here] = (state[f, a + 1] + pull_red(a, view, f, state, even)) * state[INV, a + 1]

        loop(count, second_red, unroll)
        for f in range(2):
            red[f, 0, :, here] = roll(red[f, count, :, here], 1, 0)
            red[f, count + 1, :, here] = roll(red[f, 1, :, here], -1, 0)

        def second_black(a, fields=(0, 1), level=level, even=even, state=state, here=here):
            view = red.at[:, :, :, here]
            for f in fields:
                x = red[f, a + 1, :, here]
                y = (state[2 + f, a + 1] + pull_black(a, view, f, state, even)) * state[INV + 1, a + 1]
                first, second = jnp.where(even, x, y), jnp.where(even, y, x)
                if level:
                    full[f, 2 * a, :, here] = first
                    full[f, 2 * a + 1, :, here] = second
                else:
                    for half in range(2):
                        lanes = slice(128 * half, 128 + 128 * half)
                        result[f, half, pl.ds(2 * a, 8, stride=48), :] = first[:, lanes]
                        result[f, half, pl.ds(2 * a + 1, 8, stride=48), :] = second[:, lanes]

        if level:
            loop(count, second_black, unroll)

    copies = []
    for f in range(2):
        loop(24, lambda a, f=f: second_black(a, (f,)), 24)
        for half in range(2):
            source = result.at[f, half, pl.ds(0, 256), :]
            copies.append(pltpu.make_async_copy(source, out.at[f, :, pl.ds(half * 128, 128)], sent.at[2 * f + half]))
            copies[-1].start()
    for copy in copies:
        copy.wait()


VMEM = pl.BlockSpec(memory_space=pltpu.VMEM)
ANY = pl.BlockSpec(memory_space=pl.ANY)
SMEM = pl.BlockSpec(memory_space=pltpu.SMEM)
PARAMS = pltpu.CompilerParams(vmem_limit_bytes=24 * 1024 * 1024)


def shaped(*shape):
    return jax.ShapeDtypeStruct(shape, F32)


def scratch(*shape):
    return pltpu.VMEM(shape, F32)


def state_shapes():
    return [(STATE, TILES[level] // 2 + 2, 8, LANES[level]) for level in range(4)]


def side_strips(observed, classes):
    return pl.pallas_call(
        sides_kernel,
        out_shape=[shaped(3, 256, 256), shaped(3, 64, 256), shaped(3, 64, 256), shaped(3, 128, 128), shaped(3, 128, 128)],
        in_specs=[VMEM] * 2,
        out_specs=[VMEM] * 5,
        compiler_params=PARAMS,
        name="sides",
    )(observed, classes)


def corner_strips(row_a, row_b):
    return pl.pallas_call(
        corners_kernel,
        out_shape=[shaped(3, 64, 128)] * 2,
        in_specs=[VMEM] * 2,
        out_specs=[VMEM] * 2,
        compiler_params=PARAMS,
        name="corners",
    )(row_a, row_b)


def middle(own, row_a, row_b, table):
    return pl.pallas_call(
        middle_kernel,
        out_shape=[shaped(4, 24, 8, 256)] * 2 + [jax.ShapeDtypeStruct(x, BF16) for x in ((17, 128, 128), *BIG)],
        in_specs=[VMEM] * 3 + [SMEM],
        out_specs=[VMEM] * 7,
        scratch_shapes=[scratch(3, 2, 384, 128)],
        compiler_params=PARAMS,
        name="middle",
    )(own, row_a, row_b, table)


def down(*args):
    return pl.pallas_call(
        down_kernel,
        out_shape=[shaped(*s) for s in state_shapes()] + [shaped(4, 24, 128), shaped(512, 128)],
        in_specs=[VMEM] * 9 + [SMEM],
        out_specs=[VMEM] * 6,
        scratch_shapes=[
            scratch(4, 26, 8, 384),
            scratch(2, 26, 8, 384),
            scratch(4, 24, 8, 256),
            scratch(4, 24, 8, 384),
            scratch(3, 384, 128),
            scratch(5, 24, 128),
        ],
        compiler_params=PARAMS,
        name="down",
    )(*args)


def up(mine, theirs, small, up1, up0, saved4, saved):
    return pl.pallas_call(
        up_kernel,
        out_shape=shaped(2, 256, 256),
        in_specs=[VMEM] * 10,
        out_specs=ANY,
        scratch_shapes=[
            scratch(2, 24, 8, 256),
            scratch(2, 26, 8, 384),
            scratch(2, 26, 8, 384),
            scratch(512, 128),
            scratch(5, 16, 8, 128),
            scratch(2, 16, 8, 128),
            scratch(2, 16, 8, 128),
            scratch(2, 16, 8, 128),
            scratch(2, 16, 8, 128),
            scratch(2, 16, 8, 128),
            scratch(2, 2, 384, 128),
            scratch(24, 128),
            pltpu.SemaphoreType.DMA((4,)),
        ],
        compiler_params=PARAMS,
        name="up",
    )(mine, theirs, small, up1, up0, saved4, *saved)


def swap(x, axis, first):
    pairs = [(i, i + 1) for i in range(first, 15, 2)]
    return lax.ppermute(x, axis, pairs + [(j, i) for i, j in pairs])


def local(observed, coherence_class, class_weight, class_stiffness):
    own, row_a, row_b, col_a, col_b = side_strips(observed, (coherence_class + 1).astype(F32))
    row_a, row_b = swap(row_a, ROW, 0), swap(row_b, ROW, 1)
    col_a, col_b = swap(col_a, "col", 0), swap(col_b, "col", 1)
    corner_a, corner_b = corner_strips(row_a, row_b)
    held = lax.optimization_barrier((corner_a, corner_b, own, row_a, row_b, class_weight, class_stiffness))
    corner_a, corner_b, own, row_a, row_b, class_weight, class_stiffness = held
    corner_a, corner_b = swap(corner_a, "col", 0), swap(corner_b, "col", 1)
    table = jnp.concatenate([class_weight, class_stiffness])
    rhs, gw, small, down0, down1, up1, up0 = middle(own, row_a, row_b, table)
    results = down(rhs, gw, small, down0, down1, col_a, col_b, corner_a, corner_b, table)
    *saved, saved4, message = results
    mine = lax.all_to_all(message.reshape(128, 4, 128), ("z", "col"), 0, 0)
    theirs = lax.ppermute(mine, "core", [(0, 1), (1, 0)])
    return up(mine.reshape(512, 128), theirs.reshape(512, 128), small, up1, up0, saved4, saved)


def solution(mesh):
    chips = Mesh(mesh.devices.reshape(8, 2, 16), ("z", "core", "col"))
    in_specs = (P(None, ROW, "col"), P(ROW, "col"), P(), P())
    out_specs = P(None, ROW, "col")
    return jax.shard_map(local, mesh=chips, in_specs=in_specs, out_specs=out_specs, check_vma=False)
```

```python
import jax
import jax.numpy as jnp
from jax import lax
from jax.experimental import pallas as pl
from jax.experimental.pallas import tpu as pltpu
from jax.sharding import Mesh
from jax.sharding import PartitionSpec as P

CG_ITERS = 12
FAR = -1.0e4
TILES = (48, 24, 12, 6, 3)
LANES = (384, 256, 128, 128, 128)
F32 = jnp.float32
ROW = ("z", "core")
BF16 = jnp.bfloat16
BLACK, EDGE, INV, STATE = 4, 6, 11, 13


def iota(shape, axis):
    return lax.broadcasted_iota(jnp.int32, shape, axis)


def roll(x, shift, axis):
    return pltpu.roll(x, shift % x.shape[axis], axis)


def dot(a, b):
    return jnp.dot(a, b, preferred_element_type=F32)


def split(x):
    high = x.astype(BF16)
    return high, (x - high.astype(F32)).astype(BF16)


def times(x, pattern):
    high, low = split(x)
    return dot(high, pattern) + dot(low, pattern)


def pick(pattern, x):
    high, low = split(x)
    return dot(pattern, high) + dot(pattern, low)


def onehot(condition):
    return jnp.where(condition, 1.0, 0.0).astype(BF16)


def even_lanes(shape):
    return iota(shape, len(shape) - 1) % 2 == 0


def signed_lane(level, lane):
    width = LANES[level]
    own = 256 >> level
    return jnp.where(lane < (own + width) // 2, lane, lane - width)


def coarse_lane(level, lane):
    c = signed_lane(level, lane) >> 1
    return jnp.where(c < 0, c + LANES[level + 1], c)


def side_lane(field, lane3):
    c = (signed_lane(3, lane3) >> 1) + 64 * field
    return jnp.where(c < 0, c + 128, c)


def ends(ref, index, count):
    ref[index, 0] = roll(ref[index, count], 1, 0)
    ref[index, count + 1] = roll(ref[index, 1], -1, 0)


def loop(count, body, unroll):
    if count <= unroll:
        for i in range(count):
            body(i)
        return

    def step(i, carry):
        for j in range(unroll):
            body(i * unroll + j)
        return carry

    lax.fori_loop(0, count // unroll, step, 0)


def pull_red(a, black, f, state, even):
    b = black[f, a + 1]
    total = state[EDGE, a + 1] * b + state[EDGE + 1, a + 1] * jnp.where(even, black[f, a], black[f, a + 2])
    return total + state[EDGE + 3, a + 1] * roll(b, -1, 1) + roll(state[EDGE + 4, a + 1] * b, 1, 1)


def pull_black(a, red, f, state, even):
    r = red[f, a + 1]
    total = state[EDGE, a + 1] * r + state[EDGE + 2, a + 1] * jnp.where(even, red[f, a + 2], red[f, a])
    return total + state[EDGE + 4, a + 1] * roll(r, -1, 1) + roll(state[EDGE + 3, a + 1] * r, 1, 1)


def lookup(table, index):
    parts = []
    for c in range(index.shape[1] // 128):
        parts.append(jnp.take_along_axis(table, index[:, c * 128 : (c + 1) * 128], axis=1))
    return jnp.concatenate(parts, axis=1)


def edges4(g, w):
    k = [jnp.maximum(g + roll(g, s, x), 0.0) for s, x in ((1, 0), (-1, 0), (1, 1), (-1, 1))]
    return k, 1.0 / jnp.maximum(w + k[0] + k[1] + k[2] + k[3], 1e-20)


def pull4(k, v):
    return k[0] * roll(v, 1, 0) + k[1] * roll(v, -1, 0) + k[2] * roll(v, 1, 1) + k[3] * roll(v, -1, 1)


def red4():
    return (iota((24, 128), 0) + iota((24, 128), 1)) % 2 == 0


def place():
    return 2 * lax.axis_index("z") + lax.axis_index("core"), lax.axis_index("col")


def fold(x, low, swap):
    half = x.shape[0] // 2
    first, second = x[:half], x[half:]
    if swap:
        return jnp.where(low, roll(second, 64, 1), first)
    return jnp.where(low, first, roll(second, 64, 1))


def sides_kernel(observed, classes, own, row_a, row_b, col_a, col_b):
    row, col = place()
    own[0:2] = observed[...]
    own[2] = classes[...]
    low = iota((128, 128), 1) < 64
    for f in range(3):
        x = own.at[f]
        top, bottom = x[0:64, :], x[192:256, :]
        row_a[f] = jnp.where(row % 2 == 0, bottom, top)
        row_b[f] = jnp.where(row % 2 == 0, top, bottom)
        left, right = fold(x[:, 0:128], low, False), fold(x[:, 128:256], low, True)
        col_a[f] = jnp.where(col % 2 == 0, right, left)
        col_b[f] = jnp.where(col % 2 == 0, left, right)


def corners_kernel(row_a, row_b, out_a, out_b):
    row, col = place()
    low = iota((64, 128), 1) < 64
    for f in range(3):
        a, b = row_a[f], row_b[f]
        south, north = jnp.where(row % 2 == 0, a, b), jnp.where(row % 2 == 0, b, a)
        x = jnp.concatenate([south, north], axis=0)
        left, right = fold(x[:, 0:128], low, False), fold(x[:, 128:256], low, True)
        out_a[f] = jnp.where(col % 2 == 0, right, left)
        out_b[f] = jnp.where(col % 2 == 0, left, right)


def message_row(x, pattern, mine):
    return jnp.sum(jnp.where(mine, times(x, pattern), 0.0), axis=0, keepdims=True)


def class_tables(table):
    lane = iota((8, 128), 1)
    g, w = jnp.full((8, 128), FAR, F32), jnp.zeros((8, 128), F32)
    for i in range(8):
        g = jnp.where(lane == i + 1, 0.5 * table[8 + i], g)
        w = jnp.where(lane == i + 1, table[i], w)
    return g, w


def interleave(x, y, even):
    return jnp.where(even, x, y), jnp.where(even, y, x)


def small_patterns(col):
    x, y = iota((128, 128), 0), iota((128, 128), 1)
    same = x // 64 == y // 64
    result = [coarse_lane(2, x) == y, side_lane(0, x) == y, side_lane(1, x) == y]
    result.append(jnp.logical_and(same, (x % 64) // 2 == y % 8))
    result.append(jnp.logical_and(same, x % 64 == y % 16))
    result.append(jnp.logical_and(same, x % 64 == y % 4))
    result.append(jnp.logical_and(same, x % 64 == y % 4 + 12))
    result += [side_lane(0, y) == x, side_lane(1, y) == x, coarse_lane(2, y) == x]
    for f in range(2):
        c = (y + 32) % 128 - 32 - 64 * f
        result.append(jnp.logical_and(jnp.logical_and(c >= -32, c < 32), x == col * 8 + (c >> 1)))
    base = (x // 64) * 64
    j, c = x % 16, x % 4
    result.append(y == base + j)
    result.append(jnp.logical_and(j >= 12, y == (base + j - 16) % 128))
    result.append(jnp.logical_and(j < 4, y == base + 16 + j))
    result.append(y == (base + c - 4) % 128)
    result.append(y == base + 16 + c)
    return result


(TO_4, TO_5, COMMON, ROWS, LEFT, RIGHT, FROM_4, FROM_3, COLS, AROUND) = (0, 1, 3, 4, 5, 6, 7, 9, 10, 12)
BIG = ((384, 256), (256, 128), (128, 256), (256, 384))


def middle_kernel(own, row_a, row_b, table, rhs, gw, small, down0, down1, up1, up0, frame):
    row, col = place()
    for i, pattern in enumerate(small_patterns(col)):
        small[i] = onehot(pattern)
    for level, fine, ref in ((0, 0, down0), (1, 0, down1), (1, 1, up1), (0, 1, up0)):
        ref[...] = onehot(coarse_lane(level, iota(ref.shape, fine)) == iota(ref.shape, 1 - fine))
    for f in range(3):
        for half in range(2):
            lanes = slice(half * 128, half * 128 + 128)
            x, y = row_a[f, :, lanes], row_b[f, :, lanes]
            frame[f, half, 0:256, :] = own[f, :, lanes]
            frame[f, half, 256:320, :] = jnp.where(row % 2 == 0, x, y)
            frame[f, half, 320:384, :] = jnp.where(row % 2 == 0, y, x)
    tables = class_tables(table)
    even = even_lanes((8, 256))

    def tile(f, a):
        return jnp.concatenate([frame[f, c, pl.ds(a, 8, stride=48), :] for c in range(2)], axis=1)

    def pack(a):
        for f in range(2):
            rhs[f, a], rhs[2 + f, a] = interleave(tile(f, 2 * a), tile(f, 2 * a + 1), even)
        i, j = (tile(2, 2 * a + k).astype(jnp.int32) for k in range(2))
        for q in range(2):
            gw[2 * q, a], gw[2 * q + 1, a] = interleave(lookup(tables[q], i), lookup(tables[q], j), even)

    loop(24, pack, 12)


def down_kernel(rhs0, gw0, small, down0, down1, col_a, col_b, corner_a, corner_b, table, *rest):
    states = rest[:4]
    saved4, message = rest[4:6]
    gw, red, full, sums, frame, nat = rest[6:]
    row, col = place()
    even_col = col % 2 == 0

    for a, b, start, size in ((col_a, col_b, 0, 128), (corner_a, corner_b, 256, 64)):
        low = iota((size, 128), 1) < 64
        for f in range(3):
            x, y = a[f], b[f]
            e, w = jnp.where(even_col, x, y), jnp.where(even_col, y, x)
            frame[f, start : start + size, :] = jnp.where(low, e, w)
            frame[f, start + size : start + 2 * size, :] = roll(jnp.where(low, w, e), 64, 1)
    tables = class_tables(table)
    narrow = even_lanes((8, 128))

    def side_tile(f, a):
        return frame[f, pl.ds(a, 8, stride=48), :]

    for level in range(4):
        count, width = TILES[level] // 2, LANES[level]
        even = even_lanes((8, width))
        state = states[level]
        unroll = (24, 12, 6, 3)[level]
        here = pl.ds(0, width)

        def pack(a, level=level, even=even, state=state, here=here):
            if level == 0:
                for f in range(2):
                    x = interleave(side_tile(f, 2 * a), side_tile(f, 2 * a + 1), narrow)
                    for k in range(2):
                        state[2 * k + f, a + 1] = jnp.concatenate([rhs0[2 * k + f, a], x[k]], axis=1)
                i, j = (side_tile(2, 2 * a + k).astype(jnp.int32) for k in range(2))
                for q in range(2):
                    x = interleave(lookup(tables[q], i), lookup(tables[q], j), narrow)
                    for k in range(2):
                        gw[2 * q + k, a + 1] = jnp.concatenate([gw0[2 * q + k, a], x[k]], axis=1)
            else:
                for f in range(2):
                    x = interleave(full[f, 2 * a, :, here], full[f, 2 * a + 1, :, here], even)
                    state[f, a + 1], state[2 + f, a + 1] = x
                for q in range(2):
                    x = interleave(full[2 + q, 2 * a, :, here], full[2 + q, 2 * a + 1, :, here], even)
                    gw[2 * q, a + 1, :, here], gw[2 * q + 1, a + 1, :, here] = x

        loop(count, pack, unroll)
        for q in range(2):
            gw[q, 0, :, here] = roll(gw[q, count, :, here], 1, 0)
            gw[q, count + 1, :, here] = roll(gw[q, 1, :, here], -1, 0)

        def edges(a, even=even, state=state, here=here):
            r, b = gw[0, a + 1, :, here], gw[1, a + 1, :, here]
            same = jnp.maximum(r + b, 0.0)
            r_other = jnp.maximum(r + jnp.where(even, gw[1, a, :, here], gw[1, a + 2, :, here]), 0.0)
            b_other = jnp.maximum(b + jnp.where(even, gw[0, a + 2, :, here], gw[0, a, :, here]), 0.0)
            r_east = jnp.maximum(r + roll(b, -1, 1), 0.0)
            b_east = jnp.maximum(b + roll(r, -1, 1), 0.0)
            r_inv = 1.0 / jnp.maximum(gw[2, a + 1, :, here] + same + r_other + r_east + roll(b_east, 1, 1), 1e-20)
            b_inv = 1.0 / jnp.maximum(gw[3, a + 1, :, here] + same + b_other + b_east + roll(r_east, 1, 1), 1e-20)
            for i, x in enumerate((same, r_other, b_other, r_east, b_east, r_inv, b_inv)):
                state[EDGE + i, a + 1] = x
            for f in range(2):
                red[f, a + 1, :, here] = state[f, a + 1] * r_inv
            sums[2, a, :, here] = 0.5 * (r + b)
            sums[3, a, :, here] = gw[2, a + 1, :, here] + gw[3, a + 1, :, here]

        loop(count, edges, unroll)
        for f in range(2):
            red[f, 0, :, here] = roll(red[f, count, :, here], 1, 0)
            red[f, count + 1, :, here] = roll(red[f, 1, :, here], -1, 0)

        def first_black(a, even=even, state=state, here=here):
            view = red.at[:, :, :, here]
            for f in range(2):
                state[BLACK + f, a + 1] = (state[2 + f, a + 1] + pull_black(a, view, f, state, even)) * state[INV + 1, a + 1]

        loop(count, first_black, unroll)
        for f in range(2):
            ends(state, BLACK + f, count)

        def restrict(a, even=even, state=state, here=here):
            for f in range(2):
                sums[f, a, :, here] = pull_red(a, state.at[BLACK : BLACK + 2], f, state, even)

        loop(count, restrict, unroll)
        if level < 3:
            pattern = (down0[...], down1[...], small[TO_4])[level]
            for q in range(4):
                x = sums[q, 0:count, :, here].reshape(count * 8, width)
                full[q, 0:count, :, pl.ds(0, LANES[level + 1])] = times(x, pattern).reshape(count, 8, LANES[level + 1])
        else:
            first, second = small[TO_5], small[TO_5 + 1]
            x = [sums[q, 0:3, :, here].reshape(24, 128) for q in range(4)]
            results = [times(x[0], first) + times(x[1], second)] + [times(x[q], first + second) for q in (2, 3)]
            for q in range(3):
                for a in range(3):
                    nat[q, pl.ds(a, 8, stride=3), :] = results[q][a * 8 : a * 8 + 8]

    rhs, g, w = nat[0], nat[1], nat[2]
    is_red = red4()
    k, inv = edges4(g, w)
    v = jnp.where(is_red, rhs * inv, 0.0)
    v = jnp.where(is_red, v, (rhs + pull4(k, v)) * inv)
    merged = jnp.where(is_red, rhs, v)
    saved4[0] = merged
    saved4[1] = rhs
    saved4[2] = g
    saved4[3] = w
    nat[3] = jnp.where(is_red, pull4(k, v), 0.0)
    nat[4] = jnp.where(iota((24, 128), 1) < 64, 0.5 * g, w)

    sub, at = iota((8, 128), 0), iota((8, 128), 1)
    mine = sub == (at // 8) % 8
    common = []
    for q in (3, 4):
        x = nat[q, pl.ds(0, 8, stride=2), :] + nat[q, pl.ds(1, 8, stride=2), :]
        common.append(message_row(x, small[COMMON], mine))
    top = message_row(merged[0:8], small[ROWS], sub == (at // 16) % 4)
    bottom = message_row(merged[8:16], small[ROWS], sub == (at // 16) % 4 + 4)
    mine = iota((16, 128), 0) == (iota((16, 128), 1) // 4) % 16
    left = message_row(merged[0:16], small[LEFT], mine)
    right = message_row(merged[0:16], small[RIGHT], mine)

    block = jnp.concatenate((common + [jnp.zeros((2, 128), F32)]) * 8, axis=0)

    def send(i, carry):
        message[pl.ds(pl.multiple_of(i * 32, 32), 32), :] = block
        return carry

    lax.fori_loop(0, 16, send, 0)
    for dr, dc, what in NEIGHBOURS:
        x = {-1: top, 1: bottom}.get(dr, left if dc < 0 else right)
        r, c = row + dr, col + dc

        @pl.when(jnp.logical_and(jnp.logical_and(r >= 0, r < 16), jnp.logical_and(c >= 0, c < 16)))
        def _(r=r, c=c, x=x, dr=dr):
            message[pl.ds(((r >> 1) * 16 + c) * 4 + (3 if dr else 2), 1), :] = x


NEIGHBOURS = [(dr, dc, None) for dr in (-1, 0, 1) for dc in (-1, 0, 1) if dr or dc]


def cg(mine, theirs, mix, kc, e, d, s, w, r):
    lane = iota((8, 128), 1)
    sub = iota((8, 128), 0)
    group = lane // 8
    first_core = place()[0] % 2 == 0
    arrays = [[None] * 16 for _ in range(4)]
    for hi in range(2):
        for pair in range(2):
            v = []
            for c in range(16):
                rows = pl.ds((hi * 64 + c) * 4 + pair, 4, stride=64)
                x, y = mine[rows, :], theirs[rows, :]
                start = ((hi * 2 + pair) * 16 + c) * 8
                mix[pl.ds(start, 4, stride=2), :] = jnp.where(first_core, x, y)
                mix[pl.ds(start + 1, 4, stride=2), :] = jnp.where(first_core, y, x)
            for c in range(16):
                v.append(mix[pl.ds(((hi * 2 + pair) * 16 + c) * 8, 8), :])
            for k in (1, 2, 4, 8):
                low = (group // k) % 2 == 0
                for c in range(16):
                    if not c & k:
                        x, y = v[c], v[c | k]
                        v[c] = jnp.where(low, x, roll(y, 8 * k, 1))
                        v[c | k] = jnp.where(low, roll(x, -8 * k, 1), y)
            for i in range(16):
                arrays[2 * pair + i // 8][hi * 8 + i % 8] = v[i]

    def north(tile, t):
        if t % 8:
            return tile(t - 1)
        turned = roll(tile(t + 7), 1, 0)
        return turned if t == 0 else jnp.where(sub == 0, roll(tile(7), 1, 0), turned)

    def south(tile, t):
        if t % 8 != 7:
            return tile(t + 1)
        turned = roll(tile(t - 7), -1, 0)
        return turned if t == 15 else jnp.where(sub == 7, roll(tile(8), -1, 0), turned)

    g = arrays[2]
    for t in range(16):
        up = jnp.maximum(g[t] + north(lambda i: g[i], t), 0.0)
        down = jnp.maximum(g[t] + south(lambda i: g[i], t), 0.0)
        if t == 0:
            up = jnp.where(sub == 0, 0.0, up)
        if t == 15:
            down = jnp.where(sub == 7, 0.0, down)
        left = jnp.where(lane == 0, 0.0, jnp.maximum(g[t] + roll(g[t], 1, 1), 0.0))
        right = jnp.where(lane == 127, 0.0, jnp.maximum(g[t] + roll(g[t], -1, 1), 0.0))
        kc[0, t] = up
        kc[1, t] = down
        kc[2, t] = left
        kc[3, t] = right
        kc[4, t] = arrays[3][t] + up + down + left + right

    def sums(f):
        x = [r[f, t] for t in range(16)]
        tile = lambda i: x[i]
        total, norm = 0.0, 0.0
        for t in range(16):
            image = kc[4, t] * x[t] - (
                kc[0, t] * north(tile, t)
                + kc[1, t] * south(tile, t)
                + kc[2, t] * roll(x[t], 1, 1)
                + kc[3, t] * roll(x[t], -1, 1)
            )
            w[f, t] = image
            norm += x[t] * x[t]
            total += x[t] * image
        return tuple(jnp.sum(y, axis=(0, 1), keepdims=True) for y in (norm, total))

    state = []
    for f in range(2):
        for t in range(16):
            x = arrays[f][t]
            e[f, t] = jnp.zeros_like(x)
            d[f, t] = jnp.zeros_like(x)
            s[f, t] = jnp.zeros_like(x)
            r[f, t] = x
    for f in range(2):
        norm, total = sums(f)
        state.append((norm, norm / total, jnp.zeros_like(norm)))

    def iterate(_, state):
        for f in range(2):
            norm, alpha, beta = state[f]
            for t in range(16):
                x = r[f, t] + beta * d[f, t]
                y = w[f, t] + beta * s[f, t]
                d[f, t] = x
                s[f, t] = y
                e[f, t] = e[f, t] + alpha * x
                r[f, t] = r[f, t] - alpha * y
        result = []
        fresh = [sums(f) for f in range(2)]
        for f in range(2):
            norm, alpha, _ = state[f]
            beta = fresh[f][0] / norm
            result.append((fresh[f][0], fresh[f][0] / (fresh[f][1] - beta * fresh[f][0] / alpha), beta))
        return tuple(result)

    state = tuple(state)
    for i in range(CG_ITERS - 1):
        state = iterate(i, state)
    for f in range(2):
        _, alpha, beta = state[f]
        for t in range(16):
            e[f, t] = e[f, t] + alpha * (r[f, t] + beta * d[f, t])


def merged_frame(mine, theirs, small, merged):
    row, col = place()
    at = iota((24, 128), 0)
    l = iota((24, 128), 1)
    total = {}
    for dr, dc, _ in NEIGHBOURS:
        r, c = row + dr, col + dc
        there = jnp.logical_and(jnp.logical_and(r >= 0, r < 16), jnp.logical_and(c >= 0, c < 16))
        index = jnp.where(there, ((r >> 1) * 16 + c) * 4 + (3 if dr else 2), 0)
        x = (theirs if dr else mine)[pl.ds(index, 1), :] * jnp.where(there, 1.0, 0.0)
        if dr:
            ours = at == (20 if dr < 0 else 16) + (l // 16) % 4
        else:
            ours = at == (l // 4) % 16
        key = dc if dr else 2 * dc
        total[key] = total.get(key, 0.0) + jnp.where(ours, jnp.broadcast_to(x, (24, 128)), 0.0)
    own = jnp.logical_and(at < 16, iota((24, 128), 1) % 64 < 16)
    result = jnp.where(own, merged, 0.0)
    for key, x in total.items():
        result += times(x, small[AROUND + (0, -1, 1, -2, 2).index(key)])
    return result


def up_kernel(mine, theirs, small, up1, up0, saved4, *rest):
    states, out = rest[:4], rest[4]
    full, red, blk, mix, kc, e, d, s, w, r, result, nat, sent = rest[5:]
    cg(mine, theirs, mix, kc, e, d, s, w, r)

    row, col = place()
    n = iota((24, 128), 1)
    at = iota((24, 128), 0)
    grid_row = (n // 64) * 64 + (n % 8) * 8 + (n // 8) % 8
    rows = onehot(grid_row == row * 8 + (jnp.where(at < 20, at, at - 24) >> 1))
    correction = 0.0
    for f in range(2):
        whole = jnp.concatenate([e[f, t] for t in range(16)], axis=0)
        correction += times(pick(rows, whole), small[COLS + f])

    is_red = red4()
    merged = merged_frame(mine, theirs, small, saved4[0])
    k, inv = edges4(saved4[2], saved4[3])
    x = jnp.where(is_red, 0.0, merged + correction)
    x = jnp.where(is_red, (merged + pull4(k, x)) * inv, 0.0)
    nat[...] = jnp.where(is_red, x, (saved4[1] + pull4(k, x)) * inv)
    ordered = jnp.concatenate([nat[pl.ds(a, 8, stride=3), :] for a in range(3)], axis=0)

    for level in range(3, -1, -1):
        count, width = TILES[level] // 2, LANES[level]
        even = even_lanes((8, width))
        state = states[level]
        unroll = (24, 12, 6, 3)[level]
        here = pl.ds(0, width)
        if level == 3:
            corrections = [times(ordered, small[FROM_4 + f]) for f in range(2)]
        else:
            coarse = LANES[level + 1]
            pattern = (up0[...], up1[...], small[FROM_3])[level]
            corrections = [
                times(full[f, 0:count, :, pl.ds(0, coarse)].reshape(count * 8, coarse), pattern) for f in range(2)
            ]
        for f in range(2):
            blk[f, 1 : count + 1, :, here] = state[BLACK + f, 1 : count + 1] + corrections[f].reshape(count, 8, width)
            blk[f, 0, :, here] = roll(blk[f, count, :, here], 1, 0)
            blk[f, count + 1, :, here] = roll(blk[f, 1, :, here], -1, 0)

        def second_red(a, even=even, state=state, here=here):
            view = blk.at[:, :, :, here]
            for f in range(2):
                red[f, a + 1, :, here] = (state[f, a + 1] + pull_red(a, view, f, state, even)) * state[INV, a + 1]

        loop(count, second_red, unroll)
        for f in range(2):
            red[f, 0, :, here] = roll(red[f, count, :, here], 1, 0)
            red[f, count + 1, :, here] = roll(red[f, 1, :, here], -1, 0)

        def second_black(a, fields=(0, 1), level=level, even=even, state=state, here=here):
            view = red.at[:, :, :, here]
            for f in fields:
                x = red[f, a + 1, :, here]
                y = (state[2 + f, a + 1] + pull_black(a, view, f, state, even)) * state[INV + 1, a + 1]
                first, second = jnp.where(even, x, y), jnp.where(even, y, x)
                if level:
                    full[f, 2 * a, :, here] = first
                    full[f, 2 * a + 1, :, here] = second
                else:
                    for half in range(2):
                        lanes = slice(128 * half, 128 + 128 * half)
                        result[f, half, pl.ds(2 * a, 8, stride=48), :] = first[:, lanes]
                        result[f, half, pl.ds(2 * a + 1, 8, stride=48), :] = second[:, lanes]

        if level:
            loop(count, second_black, unroll)

    copies = []
    for f in range(2):
        loop(24, lambda a, f=f: second_black(a, (f,)), 24)
        for half in range(2):
            source = result.at[f, half, pl.ds(0, 256), :]
            copies.append(pltpu.make_async_copy(source, out.at[f, :, pl.ds(half * 128, 128)], sent.at[2 * f + half]))
            copies[-1].start()
    for copy in copies:
        copy.wait()


VMEM = pl.BlockSpec(memory_space=pltpu.VMEM)
ANY = pl.BlockSpec(memory_space=pl.ANY)
SMEM = pl.BlockSpec(memory_space=pltpu.SMEM)
PARAMS = pltpu.CompilerParams(vmem_limit_bytes=24 * 1024 * 1024)


def shaped(*shape):
    return jax.ShapeDtypeStruct(shape, F32)


def scratch(*shape):
    return pltpu.VMEM(shape, F32)


def state_shapes():
    return [(STATE, TILES[level] // 2 + 2, 8, LANES[level]) for level in range(4)]


def side_strips(observed, classes):
    return pl.pallas_call(
        sides_kernel,
        out_shape=[shaped(3, 256, 256), shaped(3, 64, 256), shaped(3, 64, 256), shaped(3, 128, 128), shaped(3, 128, 128)],
        in_specs=[VMEM] * 2,
        out_specs=[VMEM] * 5,
        compiler_params=PARAMS,
        name="sides",
    )(observed, classes)


def corner_strips(row_a, row_b):
    return pl.pallas_call(
        corners_kernel,
        out_shape=[shaped(3, 64, 128)] * 2,
        in_specs=[VMEM] * 2,
        out_specs=[VMEM] * 2,
        compiler_params=PARAMS,
        name="corners",
    )(row_a, row_b)


def middle(own, row_a, row_b, table):
    return pl.pallas_call(
        middle_kernel,
        out_shape=[shaped(4, 24, 8, 256)] * 2 + [jax.ShapeDtypeStruct(x, BF16) for x in ((17, 128, 128), *BIG)],
        in_specs=[VMEM] * 3 + [SMEM],
        out_specs=[VMEM] * 7,
        scratch_shapes=[scratch(3, 2, 384, 128)],
        compiler_params=PARAMS,
        name="middle",
    )(own, row_a, row_b, table)


def down(*args):
    return pl.pallas_call(
        down_kernel,
        out_shape=[shaped(*s) for s in state_shapes()] + [shaped(4, 24, 128), shaped(512, 128)],
        in_specs=[VMEM] * 9 + [SMEM],
        out_specs=[VMEM] * 6,
        scratch_shapes=[
            scratch(4, 26, 8, 384),
            scratch(2, 26, 8, 384),
            scratch(4, 24, 8, 256),
            scratch(4, 24, 8, 384),
            scratch(3, 384, 128),
            scratch(5, 24, 128),
        ],
        compiler_params=PARAMS,
        name="down",
    )(*args)


def up(mine, theirs, small, up1, up0, saved4, saved):
    return pl.pallas_call(
        up_kernel,
        out_shape=shaped(2, 256, 256),
        in_specs=[VMEM] * 10,
        out_specs=ANY,
        scratch_shapes=[
            scratch(2, 24, 8, 256),
            scratch(2, 26, 8, 384),
            scratch(2, 26, 8, 384),
            scratch(512, 128),
            scratch(5, 16, 8, 128),
            scratch(2, 16, 8, 128),
            scratch(2, 16, 8, 128),
            scratch(2, 16, 8, 128),
            scratch(2, 16, 8, 128),
            scratch(2, 16, 8, 128),
            scratch(2, 2, 384, 128),
            scratch(24, 128),
            pltpu.SemaphoreType.DMA((4,)),
        ],
        compiler_params=PARAMS,
        name="up",
    )(mine, theirs, small, up1, up0, saved4, *saved)


def swap(x, axis, first):
    pairs = [(i, i + 1) for i in range(first, 15, 2)]
    return lax.ppermute(x, axis, pairs + [(j, i) for i, j in pairs])


def local(observed, coherence_class, class_weight, class_stiffness):
    own, row_a, row_b, col_a, col_b = side_strips(observed, (coherence_class + 1).astype(F32))
    row_a, row_b = swap(row_a, ROW, 0), swap(row_b, ROW, 1)
    col_a, col_b = swap(col_a, "col", 0), swap(col_b, "col", 1)
    corner_a, corner_b = corner_strips(row_a, row_b)
    held = lax.optimization_barrier((corner_a, corner_b, own, row_a, row_b, class_weight, class_stiffness))
    corner_a, corner_b, own, row_a, row_b, class_weight, class_stiffness = held
    corner_a, corner_b = swap(corner_a, "col", 0), swap(corner_b, "col", 1)
    table = jnp.concatenate([class_weight, class_stiffness])
    rhs, gw, small, down0, down1, up1, up0 = middle(own, row_a, row_b, table)
    results = down(rhs, gw, small, down0, down1, col_a, col_b, corner_a, corner_b, table)
    *saved, saved4, message = results
    mine = lax.all_to_all(message.reshape(128, 4, 128), ("z", "col"), 0, 0)
    theirs = lax.ppermute(mine, "core", [(0, 1), (1, 0)])
    return up(mine.reshape(512, 128), theirs.reshape(512, 128), small, up1, up0, saved4, saved)


def solution(mesh):
    chips = Mesh(mesh.devices.reshape(8, 2, 16), ("z", "core", "col"))
    in_specs = (P(None, ROW, "col"), P(ROW, "col"), P(), P())
    out_specs = P(None, ROW, "col")
    return jax.shard_map(local, mesh=chips, in_specs=in_specs, out_specs=out_specs, check_vma=False)
```

```python
import jax
import jax.numpy as jnp
from jax import lax
from jax.experimental import pallas as pl
from jax.experimental.pallas import tpu as pltpu
from jax.sharding import Mesh
from jax.sharding import PartitionSpec as P

CG_ITERS = 12
FAR = -1.0e4
TILES = (48, 24, 12, 6, 3)
LANES = (384, 256, 128, 128, 128)
F32 = jnp.float32
ROW = ("z", "core")
BF16 = jnp.bfloat16
BLACK, EDGE, INV, STATE = 4, 6, 11, 13


def iota(shape, axis):
    return lax.broadcasted_iota(jnp.int32, shape, axis)


def roll(x, shift, axis):
    return pltpu.roll(x, shift % x.shape[axis], axis)


def dot(a, b):
    return jnp.dot(a, b, preferred_element_type=F32)


def split(x):
    high = x.astype(BF16)
    return high, (x - high.astype(F32)).astype(BF16)


def times(x, pattern):
    high, low = split(x)
    count = x.shape[0]
    if count % 16:
        return dot(high, pattern) + dot(low, pattern)
    both = dot(jnp.concatenate([high, low], axis=0), pattern)
    return both[:count] + both[count:]


def pick(pattern, x):
    high, low = split(x)
    return dot(pattern, high) + dot(pattern, low)


def onehot(condition):
    return jnp.where(condition, 1.0, 0.0).astype(BF16)


def even_lanes(shape):
    return iota(shape, len(shape) - 1) % 2 == 0


def signed_lane(level, lane):
    width = LANES[level]
    own = 256 >> level
    return jnp.where(lane < (own + width) // 2, lane, lane - width)


def coarse_lane(level, lane):
    c = signed_lane(level, lane) >> 1
    return jnp.where(c < 0, c + LANES[level + 1], c)


def side_lane(field, lane3):
    c = (signed_lane(3, lane3) >> 1) + 64 * field
    return jnp.where(c < 0, c + 128, c)


def ends(ref, index, count):
    ref[index, 0] = roll(ref[index, count], 1, 0)
    ref[index, count + 1] = roll(ref[index, 1], -1, 0)


def loop(count, body, unroll):
    if count <= unroll:
        for i in range(count):
            body(i)
        return

    def step(i, carry):
        for j in range(unroll):
            body(i * unroll + j)
        return carry

    lax.fori_loop(0, count // unroll, step, 0)


def pull_red(a, black, f, state, even):
    b = black[f, a + 1]
    total = state[EDGE, a + 1] * b + state[EDGE + 1, a + 1] * jnp.where(even, black[f, a], black[f, a + 2])
    return total + state[EDGE + 3, a + 1] * roll(b, -1, 1) + roll(state[EDGE + 4, a + 1] * b, 1, 1)


def pull_black(a, red, f, state, even):
    r = red[f, a + 1]
    total = state[EDGE, a + 1] * r + state[EDGE + 2, a + 1] * jnp.where(even, red[f, a + 2], red[f, a])
    return total + state[EDGE + 4, a + 1] * roll(r, -1, 1) + roll(state[EDGE + 3, a + 1] * r, 1, 1)


def lookup(table, index):
    parts = []
    for c in range(index.shape[1] // 128):
        parts.append(jnp.take_along_axis(table, index[:, c * 128 : (c + 1) * 128], axis=1))
    return jnp.concatenate(parts, axis=1)


def edges4(g, w):
    k = [jnp.maximum(g + roll(g, s, x), 0.0) for s, x in ((1, 0), (-1, 0), (1, 1), (-1, 1))]
    return k, 1.0 / jnp.maximum(w + k[0] + k[1] + k[2] + k[3], 1e-20)


def pull4(k, v):
    return k[0] * roll(v, 1, 0) + k[1] * roll(v, -1, 0) + k[2] * roll(v, 1, 1) + k[3] * roll(v, -1, 1)


def red4():
    return (iota((24, 128), 0) + iota((24, 128), 1)) % 2 == 0


def place():
    return 2 * lax.axis_index("z") + lax.axis_index("core"), lax.axis_index("col")


def fold(x, low, swap):
    half = x.shape[0] // 2
    first, second = x[:half], x[half:]
    if swap:
        return jnp.where(low, roll(second, 64, 1), first)
    return jnp.where(low, first, roll(second, 64, 1))


def sides_kernel(observed, classes, own, row_a, row_b, col_a, col_b):
    row, col = place()
    own[0:2] = observed[...]
    own[2] = classes[...]
    low = iota((128, 128), 1) < 64
    for f in range(3):
        x = own.at[f]
        top, bottom = x[0:64, :], x[192:256, :]
        row_a[f] = jnp.where(row % 2 == 0, bottom, top)
        row_b[f] = jnp.where(row % 2 == 0, top, bottom)
        left, right = fold(x[:, 0:128], low, False), fold(x[:, 128:256], low, True)
        col_a[f] = jnp.where(col % 2 == 0, right, left)
        col_b[f] = jnp.where(col % 2 == 0, left, right)


def corners_kernel(row_a, row_b, out_a, out_b):
    row, col = place()
    low = iota((64, 128), 1) < 64
    for f in range(3):
        a, b = row_a[f], row_b[f]
        south, north = jnp.where(row % 2 == 0, a, b), jnp.where(row % 2 == 0, b, a)
        x = jnp.concatenate([south, north], axis=0)
        left, right = fold(x[:, 0:128], low, False), fold(x[:, 128:256], low, True)
        out_a[f] = jnp.where(col % 2 == 0, right, left)
        out_b[f] = jnp.where(col % 2 == 0, left, right)


def message_row(x, pattern, mine):
    return jnp.sum(jnp.where(mine, times(x, pattern), 0.0), axis=0, keepdims=True)


def class_tables(table):
    lane = iota((8, 128), 1)
    g, w = jnp.full((8, 128), FAR, F32), jnp.zeros((8, 128), F32)
    for i in range(8):
        g = jnp.where(lane == i + 1, 0.5 * table[8 + i], g)
        w = jnp.where(lane == i + 1, table[i], w)
    return g, w


def interleave(x, y, even):
    return jnp.where(even, x, y), jnp.where(even, y, x)


def small_patterns(col):
    x, y = iota((128, 128), 0), iota((128, 128), 1)
    same = x // 64 == y // 64
    result = [coarse_lane(2, x) == y, side_lane(0, x) == y, side_lane(1, x) == y]
    result.append(jnp.logical_and(same, (x % 64) // 2 == y % 8))
    result.append(jnp.logical_and(same, x % 64 == y % 16))
    result.append(jnp.logical_and(same, x % 64 == y % 4))
    result.append(jnp.logical_and(same, x % 64 == y % 4 + 12))
    result += [side_lane(0, y) == x, side_lane(1, y) == x, coarse_lane(2, y) == x]
    for f in range(2):
        c = (y + 32) % 128 - 32 - 64 * f
        result.append(jnp.logical_and(jnp.logical_and(c >= -32, c < 32), x == col * 8 + (c >> 1)))
    base = (x // 64) * 64
    j, c = x % 16, x % 4
    result.append(y == base + j)
    result.append(jnp.logical_and(j >= 12, y == (base + j - 16) % 128))
    result.append(jnp.logical_and(j < 4, y == base + 16 + j))
    result.append(y == (base + c - 4) % 128)
    result.append(y == base + 16 + c)
    return result


(TO_4, TO_5, COMMON, ROWS, LEFT, RIGHT, FROM_4, FROM_3, COLS, AROUND) = (0, 1, 3, 4, 5, 6, 7, 9, 10, 12)
BIG = ((384, 256), (256, 128), (128, 256), (256, 384))


def middle_kernel(own, row_a, row_b, table, rhs, gw, small, down0, down1, up1, up0, frame):
    row, col = place()
    for i, pattern in enumerate(small_patterns(col)):
        small[i] = onehot(pattern)
    for level, fine, ref in ((0, 0, down0), (1, 0, down1), (1, 1, up1), (0, 1, up0)):
        ref[...] = onehot(coarse_lane(level, iota(ref.shape, fine)) == iota(ref.shape, 1 - fine))
    for f in range(3):
        for half in range(2):
            lanes = slice(half * 128, half * 128 + 128)
            x, y = row_a[f, :, lanes], row_b[f, :, lanes]
            frame[f, half, 0:256, :] = own[f, :, lanes]
            frame[f, half, 256:320, :] = jnp.where(row % 2 == 0, x, y)
            frame[f, half, 320:384, :] = jnp.where(row % 2 == 0, y, x)
    tables = class_tables(table)
    even = even_lanes((8, 256))

    def tile(f, a):
        return jnp.concatenate([frame[f, c, pl.ds(a, 8, stride=48), :] for c in range(2)], axis=1)

    def pack(a):
        for f in range(2):
            rhs[f, a], rhs[2 + f, a] = interleave(tile(f, 2 * a), tile(f, 2 * a + 1), even)
        i, j = (tile(2, 2 * a + k).astype(jnp.int32) for k in range(2))
        for q in range(2):
            gw[2 * q, a], gw[2 * q + 1, a] = interleave(lookup(tables[q], i), lookup(tables[q], j), even)

    loop(24, pack, 12)


def down_kernel(rhs0, gw0, small, down0, down1, col_a, col_b, corner_a, corner_b, table, *rest):
    states = rest[:4]
    saved4, message = rest[4:6]
    gw, red, full, sums, frame, nat = rest[6:]
    row, col = place()
    even_col = col % 2 == 0

    for a, b, start, size in ((col_a, col_b, 0, 128), (corner_a, corner_b, 256, 64)):
        low = iota((size, 128), 1) < 64
        for f in range(3):
            x, y = a[f], b[f]
            e, w = jnp.where(even_col, x, y), jnp.where(even_col, y, x)
            frame[f, start : start + size, :] = jnp.where(low, e, w)
            frame[f, start + size : start + 2 * size, :] = roll(jnp.where(low, w, e), 64, 1)
    tables = class_tables(table)
    narrow = even_lanes((8, 128))

    def side_tile(f, a):
        return frame[f, pl.ds(a, 8, stride=48), :]

    for level in range(4):
        count, width = TILES[level] // 2, LANES[level]
        even = even_lanes((8, width))
        state = states[level]
        unroll = (24, 12, 6, 3)[level]
        here = pl.ds(0, width)

        def pack(a, level=level, even=even, state=state, here=here):
            if level == 0:
                for f in range(2):
                    x = interleave(side_tile(f, 2 * a), side_tile(f, 2 * a + 1), narrow)
                    for k in range(2):
                        state[2 * k + f, a + 1] = jnp.concatenate([rhs0[2 * k + f, a], x[k]], axis=1)
                i, j = (side_tile(2, 2 * a + k).astype(jnp.int32) for k in range(2))
                for q in range(2):
                    x = interleave(lookup(tables[q], i), lookup(tables[q], j), narrow)
                    for k in range(2):
                        gw[2 * q + k, a + 1] = jnp.concatenate([gw0[2 * q + k, a], x[k]], axis=1)
            else:
                for f in range(2):
                    x = interleave(full[f, 2 * a, :, here], full[f, 2 * a + 1, :, here], even)
                    state[f, a + 1], state[2 + f, a + 1] = x
                for q in range(2):
                    x = interleave(full[2 + q, 2 * a, :, here], full[2 + q, 2 * a + 1, :, here], even)
                    gw[2 * q, a + 1, :, here], gw[2 * q + 1, a + 1, :, here] = x

        loop(count, pack, unroll)
        for q in range(2):
            gw[q, 0, :, here] = roll(gw[q, count, :, here], 1, 0)
            gw[q, count + 1, :, here] = roll(gw[q, 1, :, here], -1, 0)

        def edges(a, even=even, state=state, here=here):
            r, b = gw[0, a + 1, :, here], gw[1, a + 1, :, here]
            same = jnp.maximum(r + b, 0.0)
            r_other = jnp.maximum(r + jnp.where(even, gw[1, a, :, here], gw[1, a + 2, :, here]), 0.0)
            b_other = jnp.maximum(b + jnp.where(even, gw[0, a + 2, :, here], gw[0, a, :, here]), 0.0)
            r_east = jnp.maximum(r + roll(b, -1, 1), 0.0)
            b_east = jnp.maximum(b + roll(r, -1, 1), 0.0)
            r_inv = 1.0 / jnp.maximum(gw[2, a + 1, :, here] + same + r_other + r_east + roll(b_east, 1, 1), 1e-20)
            b_inv = 1.0 / jnp.maximum(gw[3, a + 1, :, here] + same + b_other + b_east + roll(r_east, 1, 1), 1e-20)
            for i, x in enumerate((same, r_other, b_other, r_east, b_east, r_inv, b_inv)):
                state[EDGE + i, a + 1] = x
            for f in range(2):
                red[f, a + 1, :, here] = state[f, a + 1] * r_inv
            sums[2, a, :, here] = 0.5 * (r + b)
            sums[3, a, :, here] = gw[2, a + 1, :, here] + gw[3, a + 1, :, here]

        loop(count, edges, unroll)
        for f in range(2):
            red[f, 0, :, here] = roll(red[f, count, :, here], 1, 0)
            red[f, count + 1, :, here] = roll(red[f, 1, :, here], -1, 0)

        def first_black(a, even=even, state=state, here=here):
            view = red.at[:, :, :, here]
            for f in range(2):
                state[BLACK + f, a + 1] = (state[2 + f, a + 1] + pull_black(a, view, f, state, even)) * state[INV + 1, a + 1]

        loop(count, first_black, unroll)
        for f in range(2):
            ends(state, BLACK + f, count)

        def restrict(a, even=even, state=state, here=here):
            for f in range(2):
                sums[f, a, :, here] = pull_red(a, state.at[BLACK : BLACK + 2], f, state, even)

        loop(count, restrict, unroll)
        if level < 3:
            pattern = (down0[...], down1[...], small[TO_4])[level]
            for q in range(4):
                x = sums[q, 0:count, :, here].reshape(count * 8, width)
                full[q, 0:count, :, pl.ds(0, LANES[level + 1])] = times(x, pattern).reshape(count, 8, LANES[level + 1])
        else:
            first, second = small[TO_5], small[TO_5 + 1]
            x = [sums[q, 0:3, :, here].reshape(24, 128) for q in range(4)]
            results = [times(x[0], first) + times(x[1], second)] + [times(x[q], first + second) for q in (2, 3)]
            for q in range(3):
                for a in range(3):
                    nat[q, pl.ds(a, 8, stride=3), :] = results[q][a * 8 : a * 8 + 8]

    rhs, g, w = nat[0], nat[1], nat[2]
    is_red = red4()
    k, inv = edges4(g, w)
    v = jnp.where(is_red, rhs * inv, 0.0)
    v = jnp.where(is_red, v, (rhs + pull4(k, v)) * inv)
    merged = jnp.where(is_red, rhs, v)
    saved4[0] = merged
    saved4[1] = rhs
    saved4[2] = g
    saved4[3] = w
    nat[3] = jnp.where(is_red, pull4(k, v), 0.0)
    nat[4] = jnp.where(iota((24, 128), 1) < 64, 0.5 * g, w)

    sub, at = iota((8, 128), 0), iota((8, 128), 1)
    mine = sub == (at // 8) % 8
    common = []
    for q in (3, 4):
        x = nat[q, pl.ds(0, 8, stride=2), :] + nat[q, pl.ds(1, 8, stride=2), :]
        common.append(message_row(x, small[COMMON], mine))
    top = message_row(merged[0:8], small[ROWS], sub == (at // 16) % 4)
    bottom = message_row(merged[8:16], small[ROWS], sub == (at // 16) % 4 + 4)
    mine = iota((16, 128), 0) == (iota((16, 128), 1) // 4) % 16
    left = message_row(merged[0:16], small[LEFT], mine)
    right = message_row(merged[0:16], small[RIGHT], mine)

    block = jnp.concatenate((common + [jnp.zeros((2, 128), F32)]) * 8, axis=0)

    def send(i, carry):
        message[pl.ds(pl.multiple_of(i * 32, 32), 32), :] = block
        return carry

    lax.fori_loop(0, 16, send, 0)
    for dr, dc, what in NEIGHBOURS:
        x = {-1: top, 1: bottom}.get(dr, left if dc < 0 else right)
        r, c = row + dr, col + dc

        @pl.when(jnp.logical_and(jnp.logical_and(r >= 0, r < 16), jnp.logical_and(c >= 0, c < 16)))
        def _(r=r, c=c, x=x, dr=dr):
            message[pl.ds(((r >> 1) * 16 + c) * 4 + (3 if dr else 2), 1), :] = x


NEIGHBOURS = [(dr, dc, None) for dr in (-1, 0, 1) for dc in (-1, 0, 1) if dr or dc]


def cg(mine, theirs, mix, kc, e, d, s, w, r):
    lane = iota((8, 128), 1)
    sub = iota((8, 128), 0)
    group = lane // 8
    first_core = place()[0] % 2 == 0
    arrays = [[None] * 16 for _ in range(4)]
    for hi in range(2):
        for pair in range(2):
            v = []
            for c in range(16):
                rows = pl.ds((hi * 64 + c) * 4 + pair, 4, stride=64)
                x, y = mine[rows, :], theirs[rows, :]
                start = ((hi * 2 + pair) * 16 + c) * 8
                mix[pl.ds(start, 4, stride=2), :] = jnp.where(first_core, x, y)
                mix[pl.ds(start + 1, 4, stride=2), :] = jnp.where(first_core, y, x)
            for c in range(16):
                v.append(mix[pl.ds(((hi * 2 + pair) * 16 + c) * 8, 8), :])
            for k in (1, 2, 4, 8):
                low = (group // k) % 2 == 0
                for c in range(16):
                    if not c & k:
                        x, y = v[c], v[c | k]
                        v[c] = jnp.where(low, x, roll(y, 8 * k, 1))
                        v[c | k] = jnp.where(low, roll(x, -8 * k, 1), y)
            for i in range(16):
                arrays[2 * pair + i // 8][hi * 8 + i % 8] = v[i]

    def north(tile, t):
        if t % 8:
            return tile(t - 1)
        turned = roll(tile(t + 7), 1, 0)
        return turned if t == 0 else jnp.where(sub == 0, roll(tile(7), 1, 0), turned)

    def south(tile, t):
        if t % 8 != 7:
            return tile(t + 1)
        turned = roll(tile(t - 7), -1, 0)
        return turned if t == 15 else jnp.where(sub == 7, roll(tile(8), -1, 0), turned)

    g = arrays[2]
    for t in range(16):
        up = jnp.maximum(g[t] + north(lambda i: g[i], t), 0.0)
        down = jnp.maximum(g[t] + south(lambda i: g[i], t), 0.0)
        if t == 0:
            up = jnp.where(sub == 0, 0.0, up)
        if t == 15:
            down = jnp.where(sub == 7, 0.0, down)
        left = jnp.where(lane == 0, 0.0, jnp.maximum(g[t] + roll(g[t], 1, 1), 0.0))
        right = jnp.where(lane == 127, 0.0, jnp.maximum(g[t] + roll(g[t], -1, 1), 0.0))
        kc[0, t] = up
        kc[1, t] = down
        kc[2, t] = left
        kc[3, t] = right
        kc[4, t] = arrays[3][t] + up + down + left + right

    def sums(f):
        x = [r[f, t] for t in range(16)]
        tile = lambda i: x[i]
        total, norm = 0.0, 0.0
        for t in range(16):
            image = kc[4, t] * x[t] - (
                kc[0, t] * north(tile, t)
                + kc[1, t] * south(tile, t)
                + kc[2, t] * roll(x[t], 1, 1)
                + kc[3, t] * roll(x[t], -1, 1)
            )
            w[f, t] = image
            norm += x[t] * x[t]
            total += x[t] * image
        return tuple(jnp.sum(y, axis=(0, 1), keepdims=True) for y in (norm, total))

    state = []
    for f in range(2):
        for t in range(16):
            x = arrays[f][t]
            e[f, t] = jnp.zeros_like(x)
            d[f, t] = jnp.zeros_like(x)
            s[f, t] = jnp.zeros_like(x)
            r[f, t] = x
    for f in range(2):
        norm, total = sums(f)
        state.append((norm, norm / total, jnp.zeros_like(norm)))

    def iterate(_, state):
        for f in range(2):
            norm, alpha, beta = state[f]
            for t in range(16):
                x = r[f, t] + beta * d[f, t]
                y = w[f, t] + beta * s[f, t]
                d[f, t] = x
                s[f, t] = y
                e[f, t] = e[f, t] + alpha * x
                r[f, t] = r[f, t] - alpha * y
        result = []
        fresh = [sums(f) for f in range(2)]
        for f in range(2):
            norm, alpha, _ = state[f]
            beta = fresh[f][0] / norm
            result.append((fresh[f][0], fresh[f][0] / (fresh[f][1] - beta * fresh[f][0] / alpha), beta))
        return tuple(result)

    state = tuple(state)
    for i in range(CG_ITERS - 1):
        state = iterate(i, state)
    for f in range(2):
        _, alpha, beta = state[f]
        for t in range(16):
            e[f, t] = e[f, t] + alpha * (r[f, t] + beta * d[f, t])


def merged_frame(mine, theirs, small, merged):
    row, col = place()
    at = iota((24, 128), 0)
    l = iota((24, 128), 1)
    total = {}
    for dr, dc, _ in NEIGHBOURS:
        r, c = row + dr, col + dc
        there = jnp.logical_and(jnp.logical_and(r >= 0, r < 16), jnp.logical_and(c >= 0, c < 16))
        index = jnp.where(there, ((r >> 1) * 16 + c) * 4 + (3 if dr else 2), 0)
        x = (theirs if dr else mine)[pl.ds(index, 1), :] * jnp.where(there, 1.0, 0.0)
        if dr:
            ours = at == (20 if dr < 0 else 16) + (l // 16) % 4
        else:
            ours = at == (l // 4) % 16
        key = dc if dr else 2 * dc
        total[key] = total.get(key, 0.0) + jnp.where(ours, jnp.broadcast_to(x, (24, 128)), 0.0)
    own = jnp.logical_and(at < 16, iota((24, 128), 1) % 64 < 16)
    result = jnp.where(own, merged, 0.0)
    for key, x in total.items():
        result += times(x, small[AROUND + (0, -1, 1, -2, 2).index(key)])
    return result


def up_kernel(mine, theirs, small, up1, up0, saved4, *rest):
    states, out = rest[:4], rest[4]
    full, red, blk, mix, kc, e, d, s, w, r, result, nat, sent = rest[5:]
    cg(mine, theirs, mix, kc, e, d, s, w, r)

    row, col = place()
    n = iota((24, 128), 1)
    at = iota((24, 128), 0)
    grid_row = (n // 64) * 64 + (n % 8) * 8 + (n // 8) % 8
    rows = onehot(grid_row == row * 8 + (jnp.where(at < 20, at, at - 24) >> 1))
    correction = 0.0
    for f in range(2):
        whole = jnp.concatenate([e[f, t] for t in range(16)], axis=0)
        correction += times(pick(rows, whole), small[COLS + f])

    is_red = red4()
    merged = merged_frame(mine, theirs, small, saved4[0])
    k, inv = edges4(saved4[2], saved4[3])
    x = jnp.where(is_red, 0.0, merged + correction)
    x = jnp.where(is_red, (merged + pull4(k, x)) * inv, 0.0)
    nat[...] = jnp.where(is_red, x, (saved4[1] + pull4(k, x)) * inv)
    ordered = jnp.concatenate([nat[pl.ds(a, 8, stride=3), :] for a in range(3)], axis=0)

    for level in range(3, -1, -1):
        count, width = TILES[level] // 2, LANES[level]
        even = even_lanes((8, width))
        state = states[level]
        unroll = (24, 12, 6, 3)[level]
        here = pl.ds(0, width)
        if level == 3:
            corrections = [times(ordered, small[FROM_4 + f]) for f in range(2)]
        else:
            coarse = LANES[level + 1]
            pattern = (up0[...], up1[...], small[FROM_3])[level]
            corrections = [
                times(full[f, 0:count, :, pl.ds(0, coarse)].reshape(count * 8, coarse), pattern) for f in range(2)
            ]
        for f in range(2):
            blk[f, 1 : count + 1, :, here] = state[BLACK + f, 1 : count + 1] + corrections[f].reshape(count, 8, width)
            blk[f, 0, :, here] = roll(blk[f, count, :, here], 1, 0)
            blk[f, count + 1, :, here] = roll(blk[f, 1, :, here], -1, 0)

        def second_red(a, even=even, state=state, here=here):
            view = blk.at[:, :, :, here]
            for f in range(2):
                red[f, a + 1, :, here] = (state[f, a + 1] + pull_red(a, view, f, state, even)) * state[INV, a + 1]

        loop(count, second_red, unroll)
        for f in range(2):
            red[f, 0, :, here] = roll(red[f, count, :, here], 1, 0)
            red[f, count + 1, :, here] = roll(red[f, 1, :, here], -1, 0)

        def second_black(a, fields=(0, 1), level=level, even=even, state=state, here=here):
            view = red.at[:, :, :, here]
            for f in fields:
                x = red[f, a + 1, :, here]
                y = (state[2 + f, a + 1] + pull_black(a, view, f, state, even)) * state[INV + 1, a + 1]
                first, second = jnp.where(even, x, y), jnp.where(even, y, x)
                if level:
                    full[f, 2 * a, :, here] = first
                    full[f, 2 * a + 1, :, here] = second
                else:
                    for half in range(2):
                        lanes = slice(128 * half, 128 + 128 * half)
                        result[f, half, pl.ds(2 * a, 8, stride=48), :] = first[:, lanes]
                        result[f, half, pl.ds(2 * a + 1, 8, stride=48), :] = second[:, lanes]

        if level:
            loop(count, second_black, unroll)

    copies = []
    for f in range(2):
        loop(24, lambda a, f=f: second_black(a, (f,)), 24)
        for half in range(2):
            source = result.at[f, half, pl.ds(0, 256), :]
            copies.append(pltpu.make_async_copy(source, out.at[f, :, pl.ds(half * 128, 128)], sent.at[2 * f + half]))
            copies[-1].start()
    for copy in copies:
        copy.wait()


VMEM = pl.BlockSpec(memory_space=pltpu.VMEM)
ANY = pl.BlockSpec(memory_space=pl.ANY)
SMEM = pl.BlockSpec(memory_space=pltpu.SMEM)
PARAMS = pltpu.CompilerParams(vmem_limit_bytes=24 * 1024 * 1024)


def shaped(*shape):
    return jax.ShapeDtypeStruct(shape, F32)


def scratch(*shape):
    return pltpu.VMEM(shape, F32)


def state_shapes():
    return [(STATE, TILES[level] // 2 + 2, 8, LANES[level]) for level in range(4)]


def side_strips(observed, classes):
    return pl.pallas_call(
        sides_kernel,
        out_shape=[shaped(3, 256, 256), shaped(3, 64, 256), shaped(3, 64, 256), shaped(3, 128, 128), shaped(3, 128, 128)],
        in_specs=[VMEM] * 2,
        out_specs=[VMEM] * 5,
        compiler_params=PARAMS,
        name="sides",
    )(observed, classes)


def corner_strips(row_a, row_b):
    return pl.pallas_call(
        corners_kernel,
        out_shape=[shaped(3, 64, 128)] * 2,
        in_specs=[VMEM] * 2,
        out_specs=[VMEM] * 2,
        compiler_params=PARAMS,
        name="corners",
    )(row_a, row_b)


def middle(own, row_a, row_b, table):
    return pl.pallas_call(
        middle_kernel,
        out_shape=[shaped(4, 24, 8, 256)] * 2 + [jax.ShapeDtypeStruct(x, BF16) for x in ((17, 128, 128), *BIG)],
        in_specs=[VMEM] * 3 + [SMEM],
        out_specs=[VMEM] * 7,
        scratch_shapes=[scratch(3, 2, 384, 128)],
        compiler_params=PARAMS,
        name="middle",
    )(own, row_a, row_b, table)


def down(*args):
    return pl.pallas_call(
        down_kernel,
        out_shape=[shaped(*s) for s in state_shapes()] + [shaped(4, 24, 128), shaped(512, 128)],
        in_specs=[VMEM] * 9 + [SMEM],
        out_specs=[VMEM] * 6,
        scratch_shapes=[
            scratch(4, 26, 8, 384),
            scratch(2, 26, 8, 384),
            scratch(4, 24, 8, 256),
            scratch(4, 24, 8, 384),
            scratch(3, 384, 128),
            scratch(5, 24, 128),
        ],
        compiler_params=PARAMS,
        name="down",
    )(*args)


def up(mine, theirs, small, up1, up0, saved4, saved):
    return pl.pallas_call(
        up_kernel,
        out_shape=shaped(2, 256, 256),
        in_specs=[VMEM] * 10,
        out_specs=ANY,
        scratch_shapes=[
            scratch(2, 24, 8, 256),
            scratch(2, 26, 8, 384),
            scratch(2, 26, 8, 384),
            scratch(512, 128),
            scratch(5, 16, 8, 128),
            scratch(2, 16, 8, 128),
            scratch(2, 16, 8, 128),
            scratch(2, 16, 8, 128),
            scratch(2, 16, 8, 128),
            scratch(2, 16, 8, 128),
            scratch(2, 2, 384, 128),
            scratch(24, 128),
            pltpu.SemaphoreType.DMA((4,)),
        ],
        compiler_params=PARAMS,
        name="up",
    )(mine, theirs, small, up1, up0, saved4, *saved)


def swap(x, axis, first):
    pairs = [(i, i + 1) for i in range(first, 15, 2)]
    return lax.ppermute(x, axis, pairs + [(j, i) for i, j in pairs])


def local(observed, coherence_class, class_weight, class_stiffness):
    own, row_a, row_b, col_a, col_b = side_strips(observed, (coherence_class + 1).astype(F32))
    row_a, row_b = swap(row_a, ROW, 0), swap(row_b, ROW, 1)
    col_a, col_b = swap(col_a, "col", 0), swap(col_b, "col", 1)
    corner_a, corner_b = corner_strips(row_a, row_b)
    held = lax.optimization_barrier((corner_a, corner_b, own, row_a, row_b, class_weight, class_stiffness))
    corner_a, corner_b, own, row_a, row_b, class_weight, class_stiffness = held
    corner_a, corner_b = swap(corner_a, "col", 0), swap(corner_b, "col", 1)
    table = jnp.concatenate([class_weight, class_stiffness])
    rhs, gw, small, down0, down1, up1, up0 = middle(own, row_a, row_b, table)
    results = down(rhs, gw, small, down0, down1, col_a, col_b, corner_a, corner_b, table)
    *saved, saved4, message = results
    mine = lax.all_to_all(message.reshape(128, 4, 128), ("z", "col"), 0, 0)
    theirs = lax.ppermute(mine, "core", [(0, 1), (1, 0)])
    return up(mine.reshape(512, 128), theirs.reshape(512, 128), small, up1, up0, saved4, saved)


def solution(mesh):
    chips = Mesh(mesh.devices.reshape(8, 2, 16), ("z", "core", "col"))
    in_specs = (P(None, ROW, "col"), P(ROW, "col"), P(), P())
    out_specs = P(None, ROW, "col")
    return jax.shard_map(local, mesh=chips, in_specs=in_specs, out_specs=out_specs, check_vma=False)
```
